32 devices in a mesh: dp: 4 (over z), seq: 8 (over y, x, core).
Axes of the slice: x: 2, y: 2, z: 4, core: 2. Of those that a mesh axis runs over, the one named last changes fastest.
Arguments:
- tokens: bfloat16 [8, 1024, 1024], P('dp', 'seq'), may hold values from -6 to 6
- cotangent: bfloat16 [8, 1024, 1024], P('dp', 'seq'), may hold values from -6 to 6
- doc_lengths: int32 [8, 8], P('dp'), may hold values from 1 to 1017, as said below
- norm1_gain: bfloat16 [1024], P('dp'), may hold values from 0.5 to 1.5
- w_query: bfloat16 [1024, 256], P('dp'), may hold values from -0.1875 to 0.1875
- w_key: bfloat16 [1024, 256], P('dp'), may hold values from -0.1875 to 0.1875
- w_value: bfloat16 [1024, 1024], P('dp'), may hold values from -0.1875 to 0.1875
- w_output: bfloat16 [1024, 1024], P('dp'), may hold values from -1.5 to 1.5
- norm2_gain: bfloat16 [1024], P('dp'), may hold values from 0.5 to 1.5
- w_gate: bfloat16 [1024, 2752], P('dp'), may hold values from -0.1875 to 0.1875
- w_up: bfloat16 [1024, 2752], P('dp'), may hold values from -0.1875 to 0.1875
- w_down: bfloat16 [2752, 1024], P(None, 'dp'), may hold values from -0.109375 to 0.109375
Outputs:
- block_out: bfloat16 [8, 1024, 1024], P('dp', 'seq')
- grad_tokens: float32 [8, 1024, 1024], P('dp', 'seq')
- grad_norm1: float32 [1024], P('dp')
- grad_query: float32 [1024, 256], P('dp')
- grad_key: float32 [1024, 256], P('dp')
- grad_value: float32 [1024, 1024], P('dp')
- grad_output: float32 [1024, 1024], P('dp')
- grad_norm2: float32 [1024], P('dp')
- grad_gate: float32 [1024, 2752], P('dp')
- grad_up: float32 [1024, 2752], P('dp')
- grad_down: float32 [2752, 1024], P(None, 'dp')
The draws below stay inside these ranges and needn't reach their ends.
Inputs may be any that keep to these rules, and one draw needn't show every extreme that they name: `doc_lengths`: each row's lengths sum to 1024. In each aligned block of 2 rows, one row chosen by the seed has 7 documents of length 1 and one of length 1017.
All inputs are finite; a program needn't handle non-finite values.
Results may differ from the reference program's by a relative error of at most 0.02.
Values may be sent and summed in bfloat16 or wider, within the bound.
No kernel may reach another device: no remote copies, remote signals or barrier semaphores. Data moves between devices by JAX's collectives and lax.ppermute only.
A program may use at most 256 MiB of HBM per device.

```python
import math
import jax
import jax.numpy as jnp
from jax import lax

D = 1024
HEADS = 16
FEAT = 16
VDIM = 64
FF = 2752
STRETCH = 128
ROWS_DEV = 2
DOCS = 8
ROWS = 8
LEN = 1024
N_SEQ = 8


def draw_doc_lengths(key, part):
    key = jax.random.fold_in(key, 7)
    subkeys = jax.random.split(key, ROWS + 2)

    def drawn(subkey):
        cut_points = jax.random.permutation(subkey, LEN - 1)[:DOCS - 1] + 1
        edges = jnp.concatenate([jnp.zeros((1,), jnp.int32), jnp.sort(cut_points).astype(jnp.int32), jnp.full((1,), LEN, jnp.int32)])
        return edges[1:] - edges[:-1]
    drawn_rows = jax.vmap(drawn)(subkeys[:ROWS])
    groups = ROWS // ROWS_DEV
    chosen_row = jax.random.randint(subkeys[ROWS], (groups,), 0, ROWS_DEV)
    long_slot = jax.random.randint(subkeys[ROWS + 1], (groups,), 0, DOCS)
    spanning = jnp.where(jnp.arange(DOCS)[None, :] == long_slot[:, None], LEN - DOCS + 1, 1).astype(jnp.int32)
    chosen = jnp.arange(ROWS_DEV)[None, :] == chosen_row[:, None]
    drawn_rows = drawn_rows.reshape(groups, ROWS_DEV, DOCS)
    merged = jnp.where(chosen[:, :, None], spanning[:, None, :], drawn_rows)
    return merged.reshape(ROWS, DOCS).astype(jnp.int32)


def levels(key, dims, cuts, smallest, largest):
    def one(axis_at, blocks):
        draws = jax.random.uniform(jax.random.fold_in(jax.random.fold_in(key, 6), axis_at), (blocks,), jnp.float32, smallest / len(cuts), largest / len(cuts))
        return jnp.repeat(jnp.exp(draws), dims[axis_at] // blocks).reshape((-1,) + (1,) * (len(dims) - axis_at - 1))

    loudness = one(*cuts[0])
    for cut in cuts[1:]:
        loudness = loudness * one(*cut)
    return loudness


def noise(key, dims, width, limit, pieces=(), kind=jnp.bfloat16):
    entries = width * jax.random.normal(key, dims, jnp.float32)
    if pieces:
        entries = entries * levels(key, dims, pieces, -0.22, 0.18)
    return jnp.clip(entries, -limit, limit).astype(kind)


def setup_inputs(seed: int = 0) -> dict:
    seeds = jax.random.split(jax.random.key(seed), 13)
    return {
        "tokens": noise(seeds[0], (ROWS, LEN, D), 1.0, 6.0, ((0, 4), (1, 8))),
        "cotangent": noise(seeds[1], (ROWS, LEN, D), 1.0, 6.0, ((0, 4), (1, 8))),
        "doc_lengths": draw_doc_lengths(jax.random.fold_in(seeds[12], 71), 0),
        "norm1_gain": jnp.clip(1.0 + 0.1 * jax.random.normal(seeds[3], (D,), jnp.float32), 0.5, 1.5).astype(jnp.bfloat16),
        "w_query": noise(seeds[4], (D, HEADS * FEAT), D ** -0.5, 0.1875, ((0, 4),)),
        "w_key": noise(seeds[5], (D, HEADS * FEAT), D ** -0.5, 0.1875, ((0, 4),)),
        "w_value": noise(seeds[6], (D, D), D ** -0.5, 0.1875, ((0, 4),)),
        "w_output": noise(seeds[7], (D, D), 16 ** -0.5, 1.5, ((0, 4),)),
        "norm2_gain": jnp.clip(1.0 + 0.1 * jax.random.normal(seeds[8], (D,), jnp.float32), 0.5, 1.5).astype(jnp.bfloat16),
        "w_gate": noise(seeds[9], (D, FF), D ** -0.5, 0.1875, ((0, 4),)),
        "w_up": noise(seeds[10], (D, FF), D ** -0.5, 0.1875, ((0, 4),)),
        "w_down": noise(seeds[11], (FF, D), FF ** -0.5, 0.109375, ((1, 4),)),
    }


HIGHEST = lax.Precision.HIGHEST
EPSILON = 1e-05
ROOT_HALF = math.sqrt(0.5)

@jax.custom_vjp
def low(v):
    return lax.optimization_barrier(v.astype(jnp.bfloat16)).astype(jnp.float32)

@jax.custom_vjp
def low_back(v):
    return v

def low_keep(v):
    return (low(v), None)

def low_pass(kept, grad):
    return (grad,)

def back_keep(v):
    return (v, None)

def back_low(kept, grad):
    return (low(grad),)
low.defvjp(low_keep, low_pass)
low_back.defvjp(back_keep, back_low)

def features(scaled):
    feat_count = scaled.shape[-1]
    constant = jnp.ones(scaled.shape[:-1] + (1,), jnp.float32)
    squares = scaled[..., :, None] * scaled[..., None, :] * ROOT_HALF
    return jnp.concatenate([constant, scaled, squares.reshape(scaled.shape[:-1] + (feat_count * feat_count,))], axis=-1)

def matmul_hi(left, right):
    return jnp.dot(left, right, precision=HIGHEST)

def rms_norm(values, gain):
    scale = lax.rsqrt(lax.optimization_barrier(jnp.mean(values * values, axis=-1, keepdims=True)) + EPSILON)
    return values * scale * gain

def attend(query_act, key_act, value_act, is_start, doc_index):
    blocks = is_start.shape[0]
    query_half = query_act.reshape(blocks, STRETCH, HEADS, FEAT) * 0.5
    key_half = key_act.reshape(blocks, STRETCH, HEADS, FEAT) * 0.5
    value_heads = value_act.reshape(blocks, STRETCH, HEADS, VDIM)
    causal = jnp.arange(STRETCH)[:, None] >= jnp.arange(STRETCH)[None, :]
    allowed = (causal[None] & (doc_index[:, :, None] == doc_index[:, None, :])).astype(jnp.float32)
    scores = low_back(jnp.einsum('ctho,csho->chts', query_half, key_half, precision=HIGHEST))
    taylor = low(1.0 + scores + 0.5 * scores * scores) * allowed[:, None]
    num_local = jnp.einsum('chts,cshv->cthv', taylor, value_heads, precision=HIGHEST)
    den_local = jnp.einsum('chts->cth', taylor)
    phi_query = low(features(query_half))
    phi_key = low(features(key_half))
    start_flag = lax.optimization_barrier(jnp.max(is_start, axis=1))
    eligible = 1.0 - lax.cummax(is_start, axis=1)
    last_part = (doc_index == doc_index[:, -1:]).astype(jnp.float32)
    own_state = jnp.einsum('cshp,cshv->chpv', phi_key * last_part[:, :, None, None], value_heads, precision=HIGHEST)
    own_norm = jnp.einsum('cshp,cs->chp', phi_key, last_part, precision=HIGHEST)

    def carry_step(carried, carry_item):
        state_sum, norm_sum = carried
        block_state, block_norm, block_flag = carry_item
        keep_on = 1.0 - block_flag
        return ((block_state + keep_on * state_sum, block_norm + keep_on * norm_sum), (state_sum, norm_sum))
    zero_state = jnp.zeros(own_state.shape[1:], jnp.float32)
    zero_norm = jnp.zeros(own_norm.shape[1:], jnp.float32)
    _, (prefix_state, prefix_norm) = lax.scan(carry_step, (zero_state, zero_norm), (own_state, own_norm, start_flag))
    num_carried = jnp.einsum('cthp,chpv->cthv', phi_query, prefix_state, precision=HIGHEST) * eligible[:, :, None, None]
    den_carried = jnp.einsum('cthp,chp->cth', phi_query, prefix_norm, precision=HIGHEST) * eligible[:, :, None]
    numerator = low_back(num_local + num_carried)
    denominator = den_local + den_carried
    return (numerator / denominator[..., None]).reshape(blocks * STRETCH, HEADS * VDIM)

def forward_row(params, row_value, starts):
    gain_one, query_mat, key_mat, value_mat, output_mat, gain_two, gate_mat, up_mat, down_mat = params
    position = jnp.arange(LEN, dtype=jnp.int32)
    is_start = jnp.any(position[:, None] == starts[None, :], axis=1).astype(jnp.float32).reshape(N_SEQ, STRETCH)
    doc_index = (lax.optimization_barrier(jnp.sum((position[:, None] >= starts[None, :]).astype(jnp.int32), axis=1)) - 1).astype(jnp.int32).reshape(N_SEQ, STRETCH)
    entry_one = low(rms_norm(row_value, gain_one))
    query_act = low(low_back(matmul_hi(entry_one, query_mat)))
    key_act = low(low_back(matmul_hi(entry_one, key_mat)))
    value_act = low(low_back(matmul_hi(entry_one, value_mat)))
    mixed_out = low(attend(query_act, key_act, value_act, is_start, doc_index))
    middle = row_value + low_back(matmul_hi(mixed_out, output_mat))
    entry_two = low(rms_norm(middle, gain_two))
    gate_act = low_back(matmul_hi(entry_two, gate_mat))
    upward = low_back(matmul_hi(entry_two, up_mat))
    hidden = low(jax.nn.silu(gate_act) * upward)
    return middle + matmul_hi(hidden, down_mat)

def reference(tokens, cotangent, doc_lengths, norm1_gain, w_query, w_key, w_value, w_output, norm2_gain, w_gate, w_up, w_down):
    weights = (norm1_gain.astype(jnp.float32), w_query.astype(jnp.float32), w_key.astype(jnp.float32), w_value.astype(jnp.float32), w_output.astype(jnp.float32), norm2_gain.astype(jnp.float32), w_gate.astype(jnp.float32), w_up.astype(jnp.float32), w_down.astype(jnp.float32))
    starts_all = (jnp.cumsum(doc_lengths, axis=1) - doc_lengths).astype(jnp.int32)

    def one_row(totals, carry_item):
        row_in, cot_row, starts = carry_item
        result, pullback = jax.vjp(lambda params, row_value: forward_row(params, row_value, starts), weights, row_in.astype(jnp.float32))
        grad_weights, grad_row = pullback(cot_row.astype(jnp.float32))
        return (jax.tree.map(jnp.add, totals, grad_weights), (result.astype(jnp.bfloat16), grad_row))
    zero_totals = jax.tree.map(jnp.zeros_like, weights)
    totals, (block_out, grad_tokens) = lax.scan(one_row, zero_totals, (tokens, cotangent, starts_all))
    return (block_out, grad_tokens, totals[0], totals[1], totals[2], totals[3], totals[4], totals[5], totals[6], totals[7], totals[8])
```

```python
import math
from functools import partial

import jax
import jax.numpy as jnp
from jax import lax
from jax.experimental import pallas as pl
from jax.experimental.pallas import tpu as pltpu
from jax.sharding import Mesh
from jax.sharding import PartitionSpec as P

HEADS = 16
FEAT = 16
VDIM = 64
EPSILON = 1e-05

bf16 = jnp.bfloat16
f32 = jnp.float32
VMEM = pltpu.VMEM
SMEM = pltpu.SMEM
LIMIT = 60 * 1024 * 1024


def mm(left, right):
    return jnp.dot(left, right, preferred_element_type=f32)


def mm_nt(left, right):
    return lax.dot_general(left, right, (((1,), (1,)), ((), ())), preferred_element_type=f32)


def mm_tn(left, right):
    return lax.dot_general(left, right, (((0,), (0,)), ((), ())), preferred_element_type=f32)


def up_to(value, step):
    return -(-value // step) * step


def whole():
    return pl.BlockSpec(memory_space=VMEM, pipeline_mode=pl.Buffered(1))


def anywhere():
    return pl.BlockSpec(memory_space=pl.ANY)


def scalars():
    return pl.BlockSpec(memory_space=SMEM)


def rms(values):
    return lax.rsqrt(jnp.mean(values * values, axis=-1, keepdims=True) + EPSILON)


def shard_row(pieces, row):
    return jnp.concatenate([pieces[z] for z in range(pieces.shape[0])], axis=1)[row : row + 1]


def doc_starts(lengths, row):
    starts, total = [], jnp.int32(0)
    for i in range(lengths.shape[1]):
        starts.append(total)
        total = total + lengths[row, i]
    return starts


def latest_start(position, starts):
    latest = jnp.zeros_like(position)
    for start in starts:
        latest = jnp.where(position >= start, start, latest)
    return latest


class Sizes:
    def __init__(self, planes, chips, block, shard, model, hidden):
        self.planes, self.chips, self.block = planes, chips, block
        self.chunk = 2 * block
        self.tokens = chips * self.chunk
        self.shard, self.half, self.model = shard, shard // 2, model
        self.heads = HEADS // chips
        self.cq = self.heads * FEAT
        self.cv = self.heads * VDIM
        self.co = model // chips
        self.vp = up_to(self.cv, 128)
        self.qw = 256 + self.vp
        self.wa = max(512, 2 * self.cq + self.cv + self.co)
        self.hidden = hidden
        self.ffc = up_to(-(-hidden // chips), 16)
        self.ffp = up_to(self.ffc, 128)
        self.cols = 2 * self.cq + self.cv + self.co
        self.pieces = [(k, 0, 2) for k in range(chips)]
        self.far, self.near = range(chips - 1, chips // 2 - 1, -1), range(chips // 2 - 1, -1, -1)
        if chips == 4:
            self.pieces = [(0, 0, 2), (1, 0, 2), (2, 0, 2), (3, 0, 1), (3, 1, 1)]


def aligned(index, step):
    return pl.multiple_of(index * step, step)


def pack_large_kernel(sz, place, *refs):
    weights, out, sem = refs[:3], refs[-2], refs[-1]
    half, ffc = sz.half, sz.ffc
    j, c = place[0], place[1]
    for chip in range(sz.chips):
        first = chip * ffc
        count = max(0, min(ffc, sz.hidden - first))
        for core in range(2):

            @pl.when((j == chip) & (c == core))
            def _():
                lanes = slice(core * half, (core + 1) * half)
                copies = []
                for i, weight in enumerate(weights):
                    if count == 0:
                        continue
                    if half % 128:
                        out[i * ffc : i * ffc + count, :] = weight[first : first + count, lanes]
                        continue
                    copies.append(
                        pltpu.make_async_copy(
                            weight.at[pl.ds(first, count), pl.ds(core * half, half)],
                            out.at[pl.ds(i * ffc, count)],
                            sem.at[i],
                        )
                    )
                for copy in copies:
                    copy.start()
                for i in range(3):
                    if count < ffc:
                        out[i * ffc + count : (i + 1) * ffc, :] = jnp.zeros(
                            (ffc - count, half), bf16
                        )
                for copy in copies:
                    copy.wait()


def pack_small_kernel(sz, place, w_query, w_key, w_value, w_output, gain_one, gain_two, out):
    half, cq, cv, co = sz.half, sz.cq, sz.cv, sz.co
    j, c = place[0], place[1]
    side = pl.ds(aligned(c, half), half)
    out[...] = jnp.zeros_like(out)
    for chip in range(sz.chips):

        @pl.when(j == chip)
        def _():
            out[0:half, 0:cq] = w_query[side, chip * cq : (chip + 1) * cq]
            out[0:half, cq : 2 * cq] = w_key[side, chip * cq : (chip + 1) * cq]
            out[0:half, 2 * cq : 2 * cq + cv] = w_value[side, chip * cv : (chip + 1) * cv]
            out[0:half, 2 * cq + cv : sz.cols] = w_output[side, chip * co : (chip + 1) * co]

    for i, gain in enumerate((gain_one, gain_two)):
        row = gain[...].reshape(1, sz.shard)
        out[half : half + 16, i * 256 : i * 256 + sz.shard] = jnp.broadcast_to(row, (16, sz.shard))


def project_kernel(sz, place, *refs):
    n, p = len(sz.pieces), sz.planes
    xs, own, oth = refs[:n], refs[n : n + p], refs[n + p : n + 2 * p]
    act, w, entry, gains, gain_c = refs[-5:]
    j, c, plane = place[0], place[1], place[2]
    half, shard, cq, cv, ck = sz.half, sz.shard, sz.cq, sz.cv, sz.chunk
    w[...] = jnp.zeros_like(w)
    for k in range(p):
        z = plane ^ k
        for piece, side in ((own[k], c), (oth[k], 1 - c)):
            rows = pl.ds(pl.multiple_of(z * shard + side * half, half), half)
            w[rows, 0:cq] = piece[0:half, 0:cq]
            w[rows, 128 : 128 + cq] = piece[0:half, cq : 2 * cq]
            w[rows, 256 : 256 + cv] = piece[0:half, 2 * cq : 2 * cq + cv]
        for i in range(2):
            row = own[k][half : half + 16, i * 256 : i * 256 + shard]
            gain_c[z, i : i + 1] = row[0:1].astype(f32)
    for i in range(2):
        gains[i : i + 1] = shard_row(gain_c, i)
    gain = gains[0:1]
    for ref, (k, first, count) in zip(xs, sz.pieces):
        x = ref[...].astype(f32)
        at = k * ck + first * ck // 2
        entry[at : at + count * ck // 2, :] = ((x * rms(x)) * gain).astype(bf16)
    for k in range(sz.chips):
        rows = pl.ds(aligned(j ^ k, ck), ck)
        act[rows, :] = mm(entry[k * ck : (k + 1) * ck, :], w[...]).astype(bf16)


def attend_kernel(sz, place, lengths, act, *refs):
    mixed, den_full, den_rows = refs[-3:]
    c, ck, cv = place[1], sz.chunk, sz.cv
    starts = doc_starts(lengths, c)
    lane_q = lax.broadcasted_iota(jnp.int32, (ck, 128), 1) // FEAT
    lane_v = lax.broadcasted_iota(jnp.int32, (ck, sz.vp), 1) // VDIM
    lane = lax.broadcasted_iota(jnp.int32, (ck, 128), 1)
    for b in range(sz.tokens // ck):
        rows = slice(b * ck, (b + 1) * ck)
        width = (b + 1) * ck
        t_at = b * ck + lax.broadcasted_iota(jnp.int32, (ck, 1), 0)
        first = latest_start(t_at, starts)
        u_at = lax.broadcasted_iota(jnp.int32, (ck, width), 1)
        allowed = (u_at <= t_at) & (u_at >= first)
        query = act[rows, 0:128]
        keys = act[0:width, 128:256]
        values = act[0:width, 256:]
        att = jnp.zeros((ck, sz.vp), f32)
        den_wide = jnp.ones((ck, sz.vp), f32)
        den_some = jnp.ones((ck, 128), f32)
        for h in range(sz.heads):
            mine = jnp.where(lane_q == h, query.astype(f32) * 0.25, 0.0).astype(bf16)
            s = mm_nt(mine, keys)
            taylor = jnp.where(allowed, 1.0 + s + 0.5 * s * s, 0.0).astype(bf16)
            den = jnp.sum(taylor.astype(f32), axis=1, keepdims=True)
            num = mm(taylor, values)
            att = jnp.where(lane_v == h, num / den, att)
            den_wide = jnp.where(lane_v == h, den, den_wide)
            den_some = jnp.where(lane == h, den, den_some)
        mixed[rows, :] = att.astype(bf16)[:, 0:cv]
        den_full[rows, :] = den_wide
        den_rows[b] = den_some.T[0:8]


def take_output_kernel(sz, *refs):
    for k in range(sz.planes):
        refs[-1][k] = refs[k][0 : sz.half, sz.cols - sz.co : sz.cols]


def output_weight_kernel(sz, place, *refs):
    planes = sz.planes
    *pieces, out, out_c = refs
    j, plane = place[0], place[2]
    for ref, (k, first, count) in zip(pieces, sz.pieces):
        out_c[j ^ k, first * planes // 2 : (first + count) * planes // 2] = ref[...]
    for z in range(planes):
        out[plane ^ z] = jnp.concatenate([out_c[q, z] for q in range(sz.chips)], axis=1)


def fetch_weight(sz, large, which, to, stage, sem):
    half, ffc = sz.half, sz.ffc
    rows = pl.ds(which * ffc, ffc)
    if half % 128:
        return [pltpu.make_async_copy(large.at[:, rows], stage, sem)]
    return [
        pltpu.make_async_copy(
            large.at[at, rows], to.at[pl.ds(0, ffc), pl.ds(at * half, half)], sem
        )
        for at in range(2 * sz.planes)
    ]


def settle_weight(sz, to, stage):
    ffc, half = sz.ffc, sz.half
    if half % 128:
        for at in range(2 * sz.planes):
            to[0:ffc, at * half : (at + 1) * half] = stage[at]
    if sz.ffp > ffc:
        to[ffc:, :] = jnp.zeros((sz.ffp - ffc, sz.model), bf16)


def stages(sz, count):
    if sz.half % 128:
        return [((2 * sz.planes, sz.ffc, sz.half), bf16)] * count
    return [((8, 128), bf16)] * count


def picked(sz, ks):
    return [i for i, (k, _, _) in enumerate(sz.pieces) if k in ks]


def mlp_kernel(sz, ks, group, place, *refs):
    n, ck, cv, half, shard, ffc = sz.chips, sz.chunk, sz.cv, sz.half, sz.shard, sz.ffc
    chosen = picked(sz, ks)
    i, total = len(chosen), len(sz.pieces)
    xs, gs, mixed = refs[:i], refs[i : 2 * i], refs[2 * i : 2 * i + total]
    wo_own, wo_oth, large, gains = refs[2 * i + total : 2 * i + total + 4]
    outs = refs[2 * i + total + 4 :]
    dn2_out = outs[: len(ks)]
    n2_out, dgate_out, dup_out, hid_out, norm_out, wo_out, mid_out = outs[len(ks) : len(ks) + 7]
    scratch = outs[len(ks) + 7 :]
    x_s, g_s, o_c, wo, wg, wu, wd, n2_s, dgate_s, dup_s, hid_s, dn2_s, mid_s = scratch[:13]
    stage, sem, out_sem = scratch[13:16], scratch[16], scratch[17]
    j, c = place[0], place[1]
    step = pl.program_id(0)
    size = group * ck
    steps = len(ks) // group

    def inputs(at, which):
        here = list(ks)[at * group : (at + 1) * group]
        found = []
        for x, g, index in zip(xs, gs, chosen):
            k, low, count = sz.pieces[index]
            if k in here:
                rows = pl.ds(here.index(k) * ck + low * ck // 2, count * ck // 2)
                source, to = ((x, x_s), (g, g_s))[which]
                found.append(pltpu.make_async_copy(source, to.at[rows], sem.at[which]))
        if which:
            return found
        for slot, k in enumerate(here):
            rows = pl.ds(slot * ck, ck)
            for ref, (m, low, count) in zip(mixed, sz.pieces):
                lanes = pl.ds(low * cv // 2, count * cv // 2)
                source = ref.at[pl.ds(aligned(j ^ k, ck), ck)]
                found.append(pltpu.make_async_copy(source, o_c.at[j ^ m, rows, lanes], sem.at[0]))
        return found

    wo_copies = []
    for z in range(sz.planes):
        for piece, side in ((wo_own, c), (wo_oth, 1 - c)):
            rows = pl.ds(pl.multiple_of(z * shard + side * half, half), half)
            wo_copies.append(pltpu.make_async_copy(piece.at[z], wo.at[rows], sem.at[2]))
    weight_copies = [
        fetch_weight(sz, large, i, to, stage[i], sem.at[3 + i])
        for i, to in enumerate((wg, wu, wd))
    ]

    def fresh(act):
        if steps == 1:
            act()
        else:
            pl.when(step == 0)(act)

    for at in range(steps):

        @pl.when(step == at)
        def _():
            for copy in inputs(at, 0):
                copy.start()

    @fresh
    def _():
        norm_out[...] = jnp.zeros_like(norm_out)
        for copy in wo_copies + weight_copies[0] + weight_copies[1]:
            copy.start()

    for at in range(steps):

        @pl.when(step == at)
        def _():
            for copy in inputs(at, 1):
                copy.start()

    @fresh
    def _():
        for copy in weight_copies[2]:
            copy.start()

    for at in range(steps):

        @pl.when(step == at)
        def _():
            for copy in inputs(at, 0):
                copy.wait()

    @fresh
    def _():
        for copy in wo_copies:
            copy.wait()

    mix = jnp.concatenate([o_c[q] for q in range(n)], axis=1)
    middle = x_s[...].astype(f32) + mm(mix, wo[...])
    normed = middle * rms(middle)
    entry = (normed * gains[1:2]).astype(bf16)
    n2_s[...] = entry
    mid_s[...] = middle[size - ck :]

    @fresh
    def _():
        for which in range(2):
            for copy in weight_copies[which]:
                copy.wait()
            settle_weight(sz, (wg, wu)[which], stage[which])

    gate = mm_nt(entry, wg[...])
    upward = mm_nt(entry, wu[...])

    for at in range(steps):

        @pl.when(step == at)
        def _():
            for copy in inputs(at, 1):
                copy.wait()

    @fresh
    def _():
        for copy in weight_copies[2]:
            copy.wait()
        settle_weight(sz, wd, stage[2])

    grad_hidden = mm_nt(g_s[...], wd[...])
    sig = jax.nn.sigmoid(gate)
    silu = gate * sig
    dgate = (grad_hidden * upward * (sig * (1.0 + gate * (1.0 - sig)))).astype(bf16)
    dup = (grad_hidden * silu).astype(bf16)
    dgate_s[...] = dgate
    dup_s[...] = dup
    hid_s[...] = (silu * upward).astype(bf16)
    rows = pl.ds(aligned(step, size), size)
    saves = [
        pltpu.make_async_copy(source, to.at[rows], out_sem.at[index])
        for index, (source, to) in enumerate(
            ((n2_s, n2_out), (dgate_s, dgate_out), (dup_s, dup_out), (hid_s, hid_out))
        )
    ]
    saves.append(pltpu.make_async_copy(mid_s, mid_out, out_sem.at[4]))
    saves.append(pltpu.make_async_copy(wo, wo_out, out_sem.at[5]))
    for copy in saves:
        copy.start()
    dn2 = mm(dgate, wg[...]) + mm(dup, wu[...])
    dn2_s[...] = dn2.astype(bf16)
    for at in range(steps):

        @pl.when(step == at)
        def _():
            parts = [
                pltpu.make_async_copy(
                    dn2_s.at[pl.ds(slot * ck, ck)],
                    dn2_out[at * group + slot],
                    out_sem.at[6 + slot],
                )
                for slot in range(group)
            ]
            for copy in parts:
                copy.start()
            norm_out[...] += jnp.sum(dn2 * normed, axis=0, keepdims=True)
            for copy in parts:
                copy.wait()

    for copy in saves:
        copy.wait()


def down_kernel(sz, *refs):
    hids, large = refs[:2], refs[2]
    n, ck = sz.chips, sz.chunk
    outs = refs[-n - 3 : -3]
    wd, stage, sem = refs[-3:]
    copies = fetch_weight(sz, large, 2, wd, stage, sem)
    for copy in copies:
        copy.start()
    for copy in copies:
        copy.wait()
    settle_weight(sz, wd, stage)
    for hid, ks in zip(hids, (sz.far, sz.near)):
        for slot, k in enumerate(ks):
            outs[k][...] = mm(hid[slot * ck : (slot + 1) * ck, :], wd[...]).astype(bf16)


def mlp_grads_kernel(sz, *refs):
    n, ck, ffc, half = len(sz.pieces), sz.chunk, sz.ffc, sz.half
    gs = refs[:n]
    n2, dgate, dup, hid = (refs[n + 2 * i : n + 2 * i + 2] for i in range(4))
    out, g_far, g_near = refs[-3:]
    for to, ks in ((g_far, list(sz.far)), (g_near, list(sz.near))):
        for ref, (k, first, count) in zip(gs, sz.pieces):
            if k in ks:
                at = ks.index(k) * ck + first * ck // 2
                to[at : at + count * ck // 2, :] = ref[...]
    for i, (left, right) in enumerate(((dgate, n2), (dup, n2), (hid, (g_far, g_near)))):
        grads = mm_tn(left[0][...], right[0][...]) + mm_tn(left[1][...], right[1][...])
        grads = grads.astype(bf16)
        for at in range(2 * sz.planes):
            out[at, i * ffc : (i + 1) * ffc, :] = grads[0:ffc, at * half : (at + 1) * half]


def middle_kernel(sz, place, *refs):
    n = sz.chips
    dn2_in = refs[:n]
    middle, g, wo, gains = refs[n : n + 4]
    outs, dh1_out, pay = refs[-n - 2 : -2], refs[-2], refs[-1]
    j = place[0]
    dn2 = dn2_in[0][...].astype(f32)
    for k in range(1, n):
        dn2 = dn2 + dn2_in[k][...].astype(f32)
    mid = middle[...]
    scale = rms(mid)
    normed = mid * scale
    weighted = dn2 * gains[1:2]
    dh1 = g[...].astype(f32) + scale * (
        weighted - normed * jnp.mean(weighted * normed, axis=-1, keepdims=True)
    )
    dh1_out[...] = dh1
    branch = dh1.astype(bf16)
    dmix = mm_nt(branch, wo[...]).astype(bf16)
    for q in range(n):
        pay[q, :, 0 : sz.cv] = dmix[:, q * sz.cv : (q + 1) * sz.cv]
        pay[q, :, sz.cv :] = branch[:, q * sz.co : (q + 1) * sz.co]
    for m in range(n):
        outs[m][...] = pay[j ^ m]


def back_kernel(sz, place, lengths, *refs):
    n, ck, cv = sz.chips, sz.chunk, sz.cv
    heads, total = sz.heads, sz.tokens
    pays = refs[:n]
    act, mixed, den_full, den_rows, w = refs[n : n + 5]
    outs = refs[n + 5 : 2 * n + 5]
    dact, branch_c, dnum_h, q_h, dden, dq_t, dk, dv = refs[2 * n + 5 :]
    j, c = place[0], place[1]
    lane_q = lax.broadcasted_iota(jnp.int32, (ck, 128), 1) // FEAT
    lane_v = lax.broadcasted_iota(jnp.int32, (ck, sz.vp), 1) // VDIM
    picks = (
        lax.broadcasted_iota(jnp.int32, (8, cv), 1) // VDIM
        == lax.broadcasted_iota(jnp.int32, (8, cv), 0)
    ).astype(f32)
    for k in range(n):
        rows = pl.ds(aligned(j ^ k, ck), ck)
        dmix = pays[k][:, 0:cv].astype(f32)
        branch_c[rows, :] = pays[k][:, cv:]
        dnum = dmix / den_full[rows, 0:cv]
        if sz.vp > cv:
            dnum = jnp.concatenate([dnum, jnp.zeros((ck, sz.vp - cv), f32)], axis=1)
        products = dmix * mixed[rows, :].astype(f32)
        sums = lax.dot_general(
            picks,
            products,
            (((1,), (1,)), ((), ())),
            precision=lax.Precision.HIGHEST,
            preferred_element_type=f32,
        )
        dden[j ^ k] = -sums / den_rows[j ^ k]
        query = act[rows, 0:128].astype(f32) * 0.25
        for h in range(heads):
            dnum_h[h, rows, :] = jnp.where(lane_v == h, dnum, 0.0).astype(bf16)
            q_h[h, rows, :] = jnp.where(lane_q == h, query, 0.0).astype(bf16)
    starts = doc_starts(lengths, c)
    dq_t[...] = jnp.zeros_like(dq_t)
    for b in range(total // ck):
        low = b * ck
        width = total - low
        u_rows = slice(low, low + ck)
        u_at = low + lax.broadcasted_iota(jnp.int32, (ck, 1), 0)
        t_row = low + lax.broadcasted_iota(jnp.int32, (1, width), 1)
        first = latest_start(t_row, starts)
        t_at = low + lax.broadcasted_iota(jnp.int32, (ck, width), 1)
        allowed = (u_at <= t_at) & (u_at >= first)
        keys = act[u_rows, 128:256]
        values = act[u_rows, 256:]
        keys_t = keys.astype(f32).T
        dv_here = jnp.zeros((ck, sz.vp), f32)
        dk_here = jnp.zeros((ck, 128), f32)
        for h in range(heads):
            qs = q_h[h, low:, :]
            ds_in = dnum_h[h, low:, :]
            extra = jnp.concatenate(
                [dden[i][h : h + 1] for i in range(b, total // ck)], axis=1
            )
            s = mm_nt(keys, qs)
            dtaylor = mm_nt(values, ds_in) + extra
            slope = 1.0 + s
            taylor = jnp.where(allowed, slope + 0.5 * s * s, 0.0).astype(bf16)
            dscore = jnp.where(allowed, dtaylor * slope, 0.0).astype(bf16)
            dv_here = dv_here + mm(taylor, ds_in)
            dk_here = dk_here + mm(dscore, qs)
            k_t = keys_t[h * FEAT : (h + 1) * FEAT].astype(bf16)
            dq_t[h * FEAT : (h + 1) * FEAT, low:] += mm(k_t, dscore)
        dk[u_rows, :] = dk_here.astype(bf16)
        dv[u_rows, :] = dv_here.astype(bf16)
    dact[:, 0:128] = (dq_t[...] * 0.25).T.astype(bf16)
    dact[:, 128:256] = dk[...]
    dact[:, 256:] = dv[...]
    for k in range(n):
        rows = pl.ds(aligned(j ^ k, ck), ck)
        outs[k][...] = mm_nt(dact[rows, :], w[...]).astype(bf16)


def back_grads_kernel(sz, place, *refs):
    n, ck, cq, cv, co = sz.chips, sz.chunk, sz.cq, sz.cv, sz.co
    half, cols = sz.half, sz.cols
    i = len(sz.pieces)
    mixed, dn1 = refs[:i], refs[i : i + n]
    entry, dact, branch_c, norm2, norm2_more, gains = refs[i + n : i + n + 6]
    out, dact_s = refs[-2:]
    j = place[0]
    norm1 = jnp.zeros((1, sz.model), f32)
    for k in range(n):
        rows = slice(k * ck, (k + 1) * ck)
        dact_s[rows, :] = dact[pl.ds(aligned(j ^ k, ck), ck), :]
        norm1 = norm1 + jnp.sum(
            dn1[k][...].astype(f32) * entry[rows, :].astype(f32), axis=0, keepdims=True
        )
    grads = mm_tn(dact_s[...], entry[...]).astype(bf16)
    norms = jnp.concatenate(
        [norm1 / gains[0:1], norm2[...] + norm2_more[...], jnp.zeros((14, sz.model), f32)], axis=0
    ).astype(bf16)
    for at in range(2 * sz.planes):
        lanes = slice(at * half, (at + 1) * half)
        out[at, 0:cq, :] = grads[0:cq, lanes]
        out[at, cq : 2 * cq, :] = grads[128 : 128 + cq, lanes]
        out[at, 2 * cq : 2 * cq + cv, :] = grads[256 : 256 + cv, lanes]
        out[at, cols:, :] = norms[:, lanes]
    for ref, (m, first, count) in zip(mixed, sz.pieces):
        grads = mm_tn(branch_c[...], ref[...]).astype(bf16)
        at = (j ^ m) * (cv // half) + first * cv // (2 * half)
        for i in range(count * cv // (2 * half)):
            out[at + i, 2 * cq + cv : cols, :] = grads[:, i * half : (i + 1) * half]


def finish_block_kernel(sz, *refs):
    result = refs[0][...]
    for part in refs[1 : sz.chips + 1]:
        result = result + part[...].astype(f32)
    refs[-2][...] = result.astype(bf16)


def finish_tokens_kernel(sz, *refs):
    n = sz.chips
    dn1_in = refs[:n]
    dh1, x, gains, _, grad_out = refs[n:]
    values = x[...].astype(f32)
    scale = rms(values)
    normed = values * scale
    dn1 = dn1_in[0][...].astype(f32)
    for part in dn1_in[1:]:
        dn1 = dn1 + part[...].astype(f32)
    weighted = dn1 * gains[0:1]
    grad_out[...] = dh1[...] + scale * (
        weighted - normed * jnp.mean(weighted * normed, axis=-1, keepdims=True)
    )


def gathered(sz, place, refs, to):
    n = len(sz.pieces)
    j, c = place[0], place[1]
    rows = to.shape[2]
    for refs_of, side in ((refs[:n], c), (refs[n : 2 * n], 1 - c)):
        for ref, (k, first, count) in zip(refs_of, sz.pieces):
            to[j ^ k, side, first * rows // 2 : (first + count) * rows // 2] = ref[...]


def finish_attention_kernel(sz, place, *refs):
    n, shard, cq, cv, co = sz.chips, sz.shard, sz.cq, sz.cv, sz.co
    query, key, value, output, norms, all_c = refs[2 * len(sz.pieces) + 1 :]
    gathered(sz, place, refs, all_c)
    total = jnp.zeros((16, shard), f32)
    for q in range(n):
        part = jnp.concatenate([all_c[q, 0], all_c[q, 1]], axis=1).astype(f32)
        query[:, q * cq : (q + 1) * cq] = part[0:cq].T
        key[:, q * cq : (q + 1) * cq] = part[cq : 2 * cq].T
        value[:, q * cv : (q + 1) * cv] = part[2 * cq : 2 * cq + cv].T
        output[:, q * co : (q + 1) * co] = part[2 * cq + cv : sz.cols].T
        total = total + part[sz.cols :]
    norms[...] = total[0:8]


def finish_mlp_kernel(sz, place, *refs):
    half, ffc = sz.half, sz.ffc
    *outs, all_c = refs[2 * len(sz.pieces) + 1 :]
    gathered(sz, place, refs, all_c)
    for q in range(sz.chips):
        at = q * ffc
        count = max(0, min(ffc, sz.hidden - at))
        for i, out in enumerate(outs):
            for side in range(2):
                if count:
                    out[at : at + count, side * half : (side + 1) * half] = all_c[
                        q, side, i * ffc : i * ffc + count, :
                    ].astype(f32)


def busy(us):
    return pl.CostEstimate(flops=int(us * 1.15e9), bytes_accessed=0, transcendentals=0)


def kernel(body, name, outs, ins, scratch, us, smem, **more):
    shapes = [jax.ShapeDtypeStruct(shape, dtype) for shape, dtype in outs]
    loose = more.pop("loose", 0)
    loose_out = more.pop("loose_out", 0)
    kept = [whole()] * (len(shapes) - loose_out) + [anywhere()] * loose_out
    return pl.pallas_call(
        body,
        name=name,
        out_shape=shapes,
        in_specs=more.pop(
            "in_specs",
            [scalars()] * smem + [whole()] * (ins - smem - loose) + [anywhere()] * loose,
        ),
        out_specs=more.pop("out_specs", kept),
        scratch_shapes=[VMEM(shape, dtype) for shape, dtype in scratch]
        + more.pop("semaphores", []),
        compiler_params=pltpu.CompilerParams(vmem_limit_bytes=LIMIT),
        cost_estimate=busy(us),
        **more,
    )


def shards(
    n_chip,
    n_dp,
    tokens,
    cotangent,
    doc_lengths,
    norm1_gain,
    w_query,
    w_key,
    w_value,
    w_output,
    norm2_gain,
    w_gate,
    w_up,
    w_down,
):
    rows_here, block, model = tokens.shape
    hidden = w_gate.shape[1]
    sz = Sizes(n_dp, n_chip, block, w_query.shape[0], model, hidden)
    n, ck, cq, cv, co, ffc = sz.chips, sz.chunk, sz.cq, sz.cv, sz.co, sz.ffc
    half, shard, total, arrays = sz.half, sz.shard, sz.tokens, len(sz.pieces)
    chip, core = lax.axis_index("chip"), lax.axis_index("core")
    place = jnp.stack([chip, core, lax.axis_index("dp")]).astype(jnp.int32)

    def swap(a):
        return lax.ppermute(a, "core", [(0, 1), (1, 0)])

    def to_chip(a, k):
        return lax.ppermute(a, "chip", [(i, i ^ k) for i in range(n)])

    def to_plane(a, k):
        return lax.ppermute(a, "dp", [(i, i ^ k) for i in range(n_dp)])

    def spread(a, axis=0):
        if n != 4:
            return [a] + [to_chip(a, k) for k in range(1, n)]
        first, second = to_chip(a, 1), to_chip(a, 2)
        middle = a.shape[axis] // 2
        low = to_chip(lax.slice_in_dim(second, 0, middle, axis=axis), 1)
        high = to_chip(lax.slice_in_dim(first, middle, 2 * middle, axis=axis), 2)
        return [a, first, second, low, high]

    def plane_spread(a):
        return [a] + [to_plane(a, k) for k in range(1, n_dp)]

    def exchange(parts):
        return [parts[0]] + [to_chip(parts[k], k) for k in range(1, n)]

    def to_rows(a):
        return lax.all_to_all(a, "core", 0, 0).reshape(ck, model)

    def to_blocks(a):
        return lax.all_to_all(a.reshape(2, block, model), "core", 0, 0)

    with jax.named_scope("pack_small"):
        (small,) = kernel(
            partial(pack_small_kernel, sz),
            "pack_small",
            [((half + 16, sz.wa), bf16)],
            7,
            [],
            2.0,
            1,
        )(place, w_query, w_key, w_value, w_output, norm1_gain, norm2_gain)
        small_own = plane_spread(small)
        small_oth = [swap(a) for a in small_own]

    with jax.named_scope("gather_tokens"):
        xs = spread(to_rows(tokens))

    with jax.named_scope("pack_large"):
        loads = anywhere() if half % 128 == 0 else whole()
        (large,) = kernel(
            partial(pack_large_kernel, sz),
            "pack_large",
            [((3 * ffc, half), bf16)],
            0,
            [],
            1.0,
            1,
            in_specs=[scalars()] + [loads] * 3,
            semaphores=[pltpu.SemaphoreType.DMA((3,))],
        )(place, w_gate.T, w_up.T, w_down)
        waits = [*small_own[1:], *xs[1:3]]
        (large,) = kernel(
            lambda *refs: None,
            "after_small",
            [((3 * ffc, half), bf16)],
            1 + len(waits),
            [],
            1.0,
            0,
            loose=1 + len(waits),
            loose_out=1,
            input_output_aliases={0: 0},
        )(large, *waits)
        large_all = lax.all_gather(large, ("dp", "core"))

    with jax.named_scope("gather_cotangent"):
        gs = spread(to_rows(cotangent))

    with jax.named_scope("project"):
        act, w_act, entry_one, gains = kernel(
            partial(project_kernel, sz),
            "project",
            [
                ((total, sz.qw), bf16),
                ((model, sz.qw), bf16),
                ((total, model), bf16),
                ((2, model), f32),
            ],
            1 + arrays + 2 * n_dp + 2,
            [((n_dp, 2, shard), f32)],
            1.0,
            1,
            loose=2,
        )(place, *xs, *small_own, *small_oth, *gs[1:3])

    with jax.named_scope("output_weight"):
        (wo_half,) = kernel(
            partial(take_output_kernel, sz),
            "take_output",
            [((n_dp, half, co), bf16)],
            n_dp + 2,
            [],
            1.0,
            0,
            loose=2,
        )(*small_own, *gs[1:3])
        wo_parts = spread(wo_half)
        (wo_own,) = kernel(
            partial(output_weight_kernel, sz),
            "output_weight",
            [((n_dp, half, model), bf16)],
            1 + arrays,
            [((n, n_dp, half, co), bf16)],
            2.0,
            1,
        )(place, *wo_parts)
        wo_oth = swap(wo_own)

    with jax.named_scope("attention"):
        mixed_own, den_full, den_rows = kernel(
            partial(attend_kernel, sz),
            "attend",
            [
                ((total, cv), bf16),
                ((total, sz.vp), f32),
                ((total // ck, 8, ck), f32),
            ],
            5,
            [],
            7.0,
            2,
            loose=2,
        )(place, doc_lengths, act, *wo_parts[1:3])
        mixed = spread(mixed_own, 1)

    with jax.named_scope("mlp"):
        group = 2 if n == 4 else 1
        size = group * ck
        part = total // 2

        def mlp(ks, name):
            chosen = picked(sz, ks)
            count = len(ks)
            results = kernel(
                partial(mlp_kernel, sz, ks, group),
                name,
                [((ck, model), bf16)] * count
                + [
                    ((part, model), bf16),
                    ((part, sz.ffp), bf16),
                    ((part, sz.ffp), bf16),
                    ((part, sz.ffp), bf16),
                    ((1, model), f32),
                    ((model, model), bf16),
                    ((ck, model), f32),
                ],
                0,
                [
                    ((size, model), bf16),
                    ((size, model), bf16),
                    ((n, size, cv), bf16),
                    ((model, model), bf16),
                    ((sz.ffp, model), bf16),
                    ((sz.ffp, model), bf16),
                    ((sz.ffp, model), bf16),
                    ((size, model), bf16),
                    ((size, sz.ffp), bf16),
                    ((size, sz.ffp), bf16),
                    ((size, sz.ffp), bf16),
                    ((size, model), bf16),
                    ((ck, model), f32),
                ]
                + stages(sz, 3),
                10.0,
                1,
                semaphores=[
                    pltpu.SemaphoreType.DMA((6,)),
                    pltpu.SemaphoreType.DMA((6 + group,)),
                ],
                in_specs=[scalars()] + [anywhere()] * (2 * len(chosen) + arrays + 3) + [whole()],
                out_specs=[anywhere()] * (count + 4) + [whole()] + [anywhere()] * 2,
                grid=(count // group,),
            )(
                place,
                *[xs[i] for i in chosen],
                *[gs[i] for i in chosen],
                *mixed,
                wo_own,
                wo_oth,
                large_all,
                gains,
            )
            return dict(zip(ks, results[:count])), results[count:]

        far_parts, far = mlp(sz.far, "mlp_far")
        far_in = {k: to_chip(a, k) for k, a in far_parts.items()}
        near_parts, near = mlp(sz.near, "mlp_near")
        near_in = {k: to_chip(a, k) for k, a in near_parts.items() if k}
        dn2_in = [near_parts[0]] + [{**far_in, **near_in}[k] for k in range(1, n)]
        wo, middle = near[5], near[6]

    with jax.named_scope("mlp_grads"):
        (mlp_grads,) = kernel(
            partial(mlp_grads_kernel, sz),
            "mlp_grads",
            [((2 * n_dp, 3 * ffc, half), bf16)],
            arrays + 8,
            [((part, model), bf16)] * 2,
            11.0,
            0,
        )(*gs, *[a for pair in zip(far[:4], near[:4]) for a in pair])
        mlp_shard = lax.psum_scatter(mlp_grads, ("dp", "core"), scatter_dimension=0)

    with jax.named_scope("middle"):
        results = kernel(
            partial(middle_kernel, sz),
            "middle",
            [((ck, cv + co), bf16)] * n + [((ck, model), f32)],
            1 + n + 4 + 1,
            [((n, ck, cv + co), bf16)],
            30.0,
            1,
            loose=1,
        )(place, *dn2_in, middle, gs[0], wo, gains, mlp_grads)
        dh1 = results[n]
        pays = exchange(results[:n])

    with jax.named_scope("down"):
        down_parts = kernel(
            partial(down_kernel, sz),
            "down",
            [((ck, model), bf16)] * n,
            0,
            [((sz.ffp, model), bf16)] + stages(sz, 1),
            3.0,
            0,
            in_specs=[whole()] * 2 + [anywhere()] * 2,
            semaphores=[pltpu.SemaphoreType.DMA],
        )(far[3], near[3], large_all, results[0])
        down_in = exchange(down_parts)

    with jax.named_scope("attention_back"):
        results = kernel(
            partial(back_kernel, sz),
            "attention_back",
            [((ck, model), bf16)] * n + [((total, sz.qw), bf16), ((total, co), bf16)],
            2 + n + 5,
            [
                ((sz.heads, total, sz.vp), bf16),
                ((sz.heads, total, 128), bf16),
                ((total // ck, 8, ck), f32),
                ((128, total), f32),
                ((total, 128), bf16),
                ((total, sz.vp), bf16),
            ],
            60.0,
            2,
        )(place, doc_lengths, *pays, act, mixed_own, den_full, den_rows, w_act)
        dn1_parts, dact, branch_c = results[:n], results[n], results[n + 1]
        dn1_in = exchange(dn1_parts)

    with jax.named_scope("attention_grads"):
        width = sz.cols + 16
        (att_grads,) = kernel(
            partial(back_grads_kernel, sz),
            "attention_grads",
            [((2 * n_dp, width, half), bf16)],
            1 + arrays + n + 6 + n - 1,
            [((total, sz.qw), bf16)],
            20.0,
            1,
            loose=n - 1,
        )(place, *mixed, *dn1_parts, entry_one, dact, branch_c, far[4], near[4], gains, *down_in[1:])
        att_shard = lax.psum_scatter(att_grads, ("dp", "core"), scatter_dimension=0)
        att_own = spread(att_shard)
        att_oth = [swap(a) for a in att_own]

    with jax.named_scope("finish_block"):
        block_here, mlp_shard = kernel(
            partial(finish_block_kernel, sz),
            "finish_block",
            [((ck, model), bf16), ((3 * ffc, half), bf16)],
            1 + n + 2 + n - 1,
            [],
            60.0,
            0,
            loose=2 + n - 1,
            loose_out=1,
            input_output_aliases={1 + n: 1},
        )(middle, *down_in, mlp_shard, att_grads, *dn1_in[1:])
        block_out = to_blocks(block_here)
        mlp_own = spread(mlp_shard)
        mlp_oth = [swap(a) for a in mlp_own]

    with jax.named_scope("finish_tokens"):
        (grad_here,) = kernel(
            partial(finish_tokens_kernel, sz),
            "finish_tokens",
            [((ck, model), f32)],
            n + 4,
            [],
            4.0,
            0,
            loose=1,
        )(*dn1_in, dh1, xs[0], gains, block_out)
        grad_tokens = to_blocks(grad_here)

    with jax.named_scope("finish_attention"):
        total_query, total_key, total_value, total_output, norms = kernel(
            partial(finish_attention_kernel, sz),
            "finish_attention",
            [
                ((shard, n * cq), f32),
                ((shard, n * cq), f32),
                ((shard, n * cv), f32),
                ((shard, n * co), f32),
                ((8, shard), f32),
            ],
            1 + 2 * arrays + 1,
            [((n, 2, width, half), bf16)],
            4.0,
            1,
            loose=1,
        )(place, *att_own, *att_oth, grad_tokens)

    with jax.named_scope("finish_mlp"):
        total_gate, total_up, total_down = kernel(
            partial(finish_mlp_kernel, sz),
            "finish_mlp",
            [((hidden, shard), f32)] * 3,
            1 + 2 * arrays + 1,
            [((n, 2, 3 * ffc, half), bf16)],
            6.0,
            1,
            loose=1,
        )(place, *mlp_own, *mlp_oth, norms)

    return (
        block_out,
        grad_tokens,
        norms[0],
        total_query,
        total_key,
        total_value,
        total_output,
        norms[1],
        total_gate.T,
        total_up.T,
        total_down,
    )


def solution(mesh):
    n_dp, n_seq = mesh.shape["dp"], mesh.shape["seq"]
    n_chip = n_seq // 2
    grid = Mesh(mesh.devices.reshape(n_dp, n_chip, 2), ("dp", "chip", "core"))
    seq = ("chip", "core")
    placed = (
        P("dp", seq, None),
        P("dp", seq, None),
        P("dp", None),
        P("dp"),
        P("dp", None),
        P("dp", None),
        P("dp", None),
        P("dp", None),
        P("dp"),
        P("dp", None),
        P("dp", None),
        P(None, "dp"),
    )
    return jax.shard_map(
        partial(shards, n_chip, n_dp),
        mesh=grid,
        in_specs=placed,
        out_specs=(
            P("dp", seq, None),
            P("dp", seq, None),
            P("dp"),
            P("dp", None),
            P("dp", None),
            P("dp", None),
            P("dp", None),
            P("dp"),
            P("dp", None),
            P("dp", None),
            P(None, "dp"),
        ),
        check_vma=False,
    )
```

```python
import math
from functools import partial

import jax
import jax.numpy as jnp
from jax import lax
from jax.experimental import pallas as pl
from jax.experimental.pallas import tpu as pltpu
from jax.sharding import Mesh
from jax.sharding import PartitionSpec as P

HEADS = 16
FEAT = 16
VDIM = 64
EPSILON = 1e-05

bf16 = jnp.bfloat16
f32 = jnp.float32
VMEM = pltpu.VMEM
SMEM = pltpu.SMEM
MIB = 1024 * 1024

COST = dict(
    pack_small=0.5,
    pack_large=100.0,
    after_small=1.0,
    project=100.0,
    take_output=7.0,
    attend=12.0,
    output_weight=1.0,
    before_mlp=0.1,
    mlp_far=100.0,
    mlp_near=35.0,
    mlp_grads=2.0,
    middle=30.0,
    gather_qkv=1.0,
    down=100.0,
    attention_back=60.0,
    attention_grads=0.1,
    pair_sum=60.0,
    finish_block=1.0,
    finish_tokens=0.5,
    plane_sum=2.0,
    join=2.0,
    finish_attention=0.1,
    finish_mlp=12.0,
)
TWICE = dict(
    x=0,
    g=1,
    wo=1,
    o=1,
    qkv=0,
    att=0,
    mlp=1,
)
TIES = dict(
    small_x=0,
    large_x=1,
    large_x3=0,
    large_g=1,
    g_project=1,
    take_oth=0,
    take_x=0,
    attend_wo=0,
    ow_mixed=1,
    ow_own=0,
    ow_g=1,
    qkv_ow=0,
    qkv_tie=1,
    near_far=1,
    grads_qkv=1,
    grads_far=0,
    middle_grads=1,
    middle_qkv=1,
    gq_middle=1,
    down_middle=1,
    down_gq=0,
    back_down=1,
    back_gq=1,
    ag_down=1,
    pair_tokens=0,
    pair_block=0,
    plane_tokens=0,
    plane_block=0,
    mlp_plane=0,
    fa_tokens=0,
    fm_norms=0,
    fm_join=0,
)


def mm(left, right):
    return jnp.dot(left, right, preferred_element_type=f32)


def mm_nt(left, right):
    return lax.dot_general(left, right, (((1,), (1,)), ((), ())), preferred_element_type=f32)


def mm_tn(left, right):
    return lax.dot_general(left, right, (((0,), (0,)), ((), ())), preferred_element_type=f32)


def up_to(value, step):
    return -(-value // step) * step


def whole():
    return pl.BlockSpec(memory_space=VMEM, pipeline_mode=pl.Buffered(1))


def anywhere():
    return pl.BlockSpec(memory_space=pl.ANY)


def scalars():
    return pl.BlockSpec(memory_space=SMEM)


def rms(values):
    return lax.rsqrt(jnp.mean(values * values, axis=-1, keepdims=True) + EPSILON)


def shard_row(pieces, row):
    return jnp.concatenate([pieces[z] for z in range(pieces.shape[0])], axis=1)[row : row + 1]


def doc_starts(lengths, row):
    starts, total = [], jnp.int32(0)
    for i in range(lengths.shape[1]):
        starts.append(total)
        total = total + lengths[row, i]
    return starts


def latest_start(position, starts):
    latest = jnp.zeros_like(position)
    for start in starts:
        latest = jnp.where(position >= start, start, latest)
    return latest


class Sizes:
    def __init__(self, planes, chips, block, shard, model, hidden):
        self.planes, self.chips, self.block = planes, chips, block
        self.chunk = 2 * block
        self.tokens = chips * self.chunk
        self.shard, self.half, self.model = shard, shard // 2, model
        self.heads = HEADS // chips
        self.cq = self.heads * FEAT
        self.cv = self.heads * VDIM
        self.co = model // chips
        self.vp = up_to(self.cv, 128)
        self.qw = 256 + self.vp
        self.wa = max(512, 2 * self.cq + self.cv + self.co)
        self.hidden = hidden
        self.ffc = up_to(-(-hidden // chips), 16)
        self.ffp = up_to(self.ffc, 128)
        self.cols = 2 * self.cq + self.cv + self.co
        self.qkv = 2 * self.cq + self.cv
        self.pieces = self.direct = [(k, 0, 2) for k in range(chips)]
        self.far, self.near = range(chips - 1, chips // 2 - 1, -1), range(chips // 2 - 1, -1, -1)
        if chips == 4:
            self.pieces = [(0, 0, 2), (1, 0, 2), (2, 0, 2), (3, 0, 1), (3, 1, 1)]


def aligned(index, step):
    return pl.multiple_of(index * step, step)


def pack_large_kernel(sz, place, *refs):
    weights, out, sem = refs[:3], refs[-2], refs[-1]
    half, ffc = sz.half, sz.ffc
    j, c = place[0], place[1]
    for chip in range(sz.chips):
        first = chip * ffc
        count = max(0, min(ffc, sz.hidden - first))
        for core in range(2):

            @pl.when((j == chip) & (c == core))
            def _():
                lanes = slice(core * half, (core + 1) * half)
                copies = []
                for i, weight in enumerate(weights):
                    if count == 0:
                        continue
                    if half % 128:
                        out[i * ffc : i * ffc + count, :] = weight[first : first + count, lanes]
                        continue
                    copies.append(
                        pltpu.make_async_copy(
                            weight.at[pl.ds(first, count), pl.ds(core * half, half)],
                            out.at[pl.ds(i * ffc, count)],
                            sem.at[i],
                        )
                    )
                for copy in copies:
                    copy.start()
                for i in range(3):
                    if count < ffc:
                        out[i * ffc + count : (i + 1) * ffc, :] = jnp.zeros(
                            (ffc - count, half), bf16
                        )
                for copy in copies:
                    copy.wait()


def pack_small_kernel(sz, place, w_query, w_key, w_value, w_output, gain_one, gain_two, out):
    half, cq, cv, co = sz.half, sz.cq, sz.cv, sz.co
    j, c = place[0], place[1]
    side = pl.ds(aligned(c, half), half)
    out[...] = jnp.zeros_like(out)
    for chip in range(sz.chips):

        @pl.when(j == chip)
        def _():
            out[0:half, 0:cq] = w_query[side, chip * cq : (chip + 1) * cq]
            out[0:half, cq : 2 * cq] = w_key[side, chip * cq : (chip + 1) * cq]
            out[0:half, 2 * cq : 2 * cq + cv] = w_value[side, chip * cv : (chip + 1) * cv]
            out[0:half, 2 * cq + cv : sz.cols] = w_output[side, chip * co : (chip + 1) * co]

    for i, gain in enumerate((gain_one, gain_two)):
        row = gain[...].reshape(1, sz.shard)
        out[half : half + 16, i * 256 : i * 256 + sz.shard] = jnp.broadcast_to(row, (16, sz.shard))


def project_kernel(sz, layout, place, *refs):
    n, p = len(layout), sz.planes
    xs, own, oth = refs[:n], refs[n : n + p], refs[n + p : n + 2 * p]
    act, w, entry, gains, gain_c = refs[n + 2 * p :]
    j, c, plane = place[0], place[1], place[2]
    half, shard, cq, cv, ck = sz.half, sz.shard, sz.cq, sz.cv, sz.chunk
    w[...] = jnp.zeros_like(w)
    for k in range(p):
        z = plane ^ k
        for piece, side in ((own[k], c), (oth[k], 1 - c)):
            rows = pl.ds(pl.multiple_of(z * shard + side * half, half), half)
            w[rows, 0:cq] = piece[0:half, 0:cq]
            w[rows, 128 : 128 + cq] = piece[0:half, cq : 2 * cq]
            w[rows, 256 : 256 + cv] = piece[0:half, 2 * cq : 2 * cq + cv]
        for i in range(2):
            row = own[k][half : half + 16, i * 256 : i * 256 + shard]
            gain_c[z, i : i + 1] = row[0:1].astype(f32)
    for i in range(2):
        gains[i : i + 1] = shard_row(gain_c, i)
    gain = gains[0:1]
    for ref, (k, first, count) in zip(xs, layout):
        x = ref[...].astype(f32)
        at = k * ck + first * ck // 2
        entry[at : at + count * ck // 2, :] = ((x * rms(x)) * gain).astype(bf16)
    for k in range(sz.chips):
        rows = pl.ds(aligned(j ^ k, ck), ck)
        act[rows, :] = mm(entry[k * ck : (k + 1) * ck, :], w[...]).astype(bf16)


def attend_kernel(sz, place, lengths, act, mixed, den_full, den_rows):
    c, ck, cv = place[1], sz.chunk, sz.cv
    starts = doc_starts(lengths, c)
    lane_q = lax.broadcasted_iota(jnp.int32, (ck, 128), 1) // FEAT
    lane_v = lax.broadcasted_iota(jnp.int32, (ck, sz.vp), 1) // VDIM
    lane = lax.broadcasted_iota(jnp.int32, (ck, 128), 1)
    for b in range(sz.tokens // ck):
        rows = slice(b * ck, (b + 1) * ck)
        width = (b + 1) * ck
        t_at = b * ck + lax.broadcasted_iota(jnp.int32, (ck, 1), 0)
        first = latest_start(t_at, starts)
        u_at = lax.broadcasted_iota(jnp.int32, (ck, width), 1)
        allowed = (u_at <= t_at) & (u_at >= first)
        query = act[rows, 0:128]
        keys = act[0:width, 128:256]
        values = act[0:width, 256:]
        att = jnp.zeros((ck, sz.vp), f32)
        den_wide = jnp.ones((ck, sz.vp), f32)
        den_some = jnp.ones((ck, 128), f32)
        for h in range(sz.heads):
            mine = jnp.where(lane_q == h, query.astype(f32) * 0.25, 0.0).astype(bf16)
            s = mm_nt(mine, keys)
            taylor = jnp.where(allowed, 1.0 + s + 0.5 * s * s, 0.0).astype(bf16)
            den = jnp.sum(taylor.astype(f32), axis=1, keepdims=True)
            num = mm(taylor, values)
            att = jnp.where(lane_v == h, num / den, att)
            den_wide = jnp.where(lane_v == h, den, den_wide)
            den_some = jnp.where(lane == h, den, den_some)
        mixed[rows, :] = att.astype(bf16)[:, 0:cv]
        den_full[rows, :] = den_wide
        den_rows[b] = den_some.T[0:8]


def take_output_kernel(sz, *refs):
    for k in range(sz.planes):
        refs[-2][k] = refs[k][0 : sz.half, sz.qkv : sz.cols]
        refs[-1][k] = refs[k][0 : sz.half, 0 : sz.qkv]


def gather_qkv_kernel(sz, layout, place, *refs):
    n, half, planes = len(layout), sz.half, sz.planes
    out = refs[-1]
    c, plane = place[1], place[2]
    for pieces, side in ((refs[:n], c), (refs[n : 2 * n], 1 - c)):
        for ref, (k, first, count) in zip(pieces, layout):
            for i in range(count * planes // 2):
                z = plane ^ (first * planes // 2 + i)
                at = pl.multiple_of(z * sz.shard + side * half, half)
                out[k, pl.ds(at, half), :] = ref[i]


def output_weight_kernel(sz, layout, place, *refs):
    planes = sz.planes
    *pieces, out, out_c = refs
    j, plane = place[0], place[2]
    for ref, (k, first, count) in zip(pieces, layout):
        out_c[j ^ k, first * planes // 2 : (first + count) * planes // 2] = ref[...]
    for z in range(planes):
        out[plane ^ z] = jnp.concatenate([out_c[q, z] for q in range(sz.chips)], axis=1)


def fetch_weight(sz, large, which, to, stage, sem):
    half, ffc = sz.half, sz.ffc
    rows = pl.ds(which * ffc, ffc)
    if half % 128:
        return [pltpu.make_async_copy(large.at[:, rows], stage, sem)]
    return [
        pltpu.make_async_copy(
            large.at[at, rows], to.at[pl.ds(0, ffc), pl.ds(at * half, half)], sem
        )
        for at in range(2 * sz.planes)
    ]


def settle_weight(sz, to, stage):
    ffc, half = sz.ffc, sz.half
    if half % 128:
        for at in range(2 * sz.planes):
            to[0:ffc, at * half : (at + 1) * half] = stage[at]
    if sz.ffp > ffc:
        to[ffc:, :] = jnp.zeros((sz.ffp - ffc, sz.model), bf16)


def stages(sz, count):
    if sz.half % 128:
        return [((2 * sz.planes, sz.ffc, sz.half), bf16)] * count
    return [((8, 128), bf16)] * count


def picked(layout, ks):
    return [i for i, (k, _, _) in enumerate(layout) if k in ks]


def mlp_kernel(sz, ks, group, layouts, place, *refs):
    n, ck, cv, half, shard, ffc = sz.chips, sz.chunk, sz.cv, sz.half, sz.shard, sz.ffc
    lay_x, lay_g, lay_o = layouts
    some_x, some_g = picked(lay_x, ks), picked(lay_g, ks)
    i, total = len(some_x), len(some_x) + len(some_g)
    xs, gs, mixed = refs[:i], refs[i:total], refs[total : total + len(lay_o)]
    total = total + len(lay_o)
    wo_own, wo_oth, large, gains = refs[total : total + 4]
    outs = refs[total + 4 :]
    dn2_out = outs[: len(ks)]
    n2_out, dgate_out, dup_out, hid_out, norm_out, wo_out, mid_out = outs[len(ks) : len(ks) + 7]
    scratch = outs[len(ks) + 7 :]
    x_s, g_s, o_c, wo, wg, wu, wd, n2_s, dgate_s, dup_s, hid_s, dn2_s, mid_s = scratch[:13]
    stage, sem, out_sem = scratch[13:16], scratch[16], scratch[17]
    j, c = place[0], place[1]
    step = pl.program_id(0)
    size = group * ck
    steps = len(ks) // group

    def inputs(at, which):
        here = list(ks)[at * group : (at + 1) * group]
        found = []
        to = g_s if which else x_s
        layout, some = (lay_g, some_g) if which else (lay_x, some_x)
        for source, index in zip(gs if which else xs, some):
            k, low, count = layout[index]
            if k in here:
                rows = pl.ds(here.index(k) * ck + low * ck // 2, count * ck // 2)
                found.append(pltpu.make_async_copy(source, to.at[rows], sem.at[which]))
        if which:
            return found
        for slot, k in enumerate(here):
            rows = pl.ds(slot * ck, ck)
            for ref, (m, low, count) in zip(mixed, lay_o):
                lanes = pl.ds(low * cv // 2, count * cv // 2)
                source = ref.at[pl.ds(aligned(j ^ k, ck), ck)]
                found.append(pltpu.make_async_copy(source, o_c.at[j ^ m, rows, lanes], sem.at[0]))
        return found

    wo_copies = []
    for z in range(sz.planes):
        for piece, side in ((wo_own, c), (wo_oth, 1 - c)):
            rows = pl.ds(pl.multiple_of(z * shard + side * half, half), half)
            wo_copies.append(pltpu.make_async_copy(piece.at[z], wo.at[rows], sem.at[2]))
    weight_copies = [
        fetch_weight(sz, large, i, to, stage[i], sem.at[3 + i])
        for i, to in enumerate((wg, wu, wd))
    ]

    def fresh(act):
        if steps == 1:
            act()
        else:
            pl.when(step == 0)(act)

    for at in range(steps):

        @pl.when(step == at)
        def _():
            for copy in inputs(at, 0):
                copy.start()

    @fresh
    def _():
        norm_out[...] = jnp.zeros_like(norm_out)
        for copy in wo_copies + weight_copies[0] + weight_copies[1]:
            copy.start()

    for at in range(steps):

        @pl.when(step == at)
        def _():
            for copy in inputs(at, 1):
                copy.start()

    @fresh
    def _():
        for copy in weight_copies[2]:
            copy.start()

    for at in range(steps):

        @pl.when(step == at)
        def _():
            for copy in inputs(at, 0):
                copy.wait()

    @fresh
    def _():
        for copy in wo_copies:
            copy.wait()

    mix = jnp.concatenate([o_c[q] for q in range(n)], axis=1)
    middle = x_s[...].astype(f32) + mm(mix, wo[...])
    normed = middle * rms(middle)
    entry = (normed * gains[1:2]).astype(bf16)
    n2_s[...] = entry
    mid_s[...] = middle[size - ck :]

    @fresh
    def _():
        for which in range(2):
            for copy in weight_copies[which]:
                copy.wait()
            settle_weight(sz, (wg, wu)[which], stage[which])

    gate = mm_nt(entry, wg[...])
    upward = mm_nt(entry, wu[...])

    for at in range(steps):

        @pl.when(step == at)
        def _():
            for copy in inputs(at, 1):
                copy.wait()

    @fresh
    def _():
        for copy in weight_copies[2]:
            copy.wait()
        settle_weight(sz, wd, stage[2])

    grad_hidden = mm_nt(g_s[...], wd[...])
    sig = jax.nn.sigmoid(gate)
    silu = gate * sig
    dgate = (grad_hidden * upward * (sig * (1.0 + gate * (1.0 - sig)))).astype(bf16)
    dup = (grad_hidden * silu).astype(bf16)
    dgate_s[...] = dgate
    dup_s[...] = dup
    hid_s[...] = (silu * upward).astype(bf16)
    rows = pl.ds(aligned(step, size), size)
    saves = [
        pltpu.make_async_copy(source, to.at[rows], out_sem.at[index])
        for index, (source, to) in enumerate(
            ((n2_s, n2_out), (dgate_s, dgate_out), (dup_s, dup_out), (hid_s, hid_out))
        )
    ]
    saves.append(pltpu.make_async_copy(mid_s, mid_out, out_sem.at[4]))
    saves.append(pltpu.make_async_copy(wo, wo_out, out_sem.at[5]))
    for copy in saves:
        copy.start()
    dn2 = mm(dgate, wg[...]) + mm(dup, wu[...])
    dn2_s[...] = dn2.astype(bf16)
    for at in range(steps):

        @pl.when(step == at)
        def _():
            parts = [
                pltpu.make_async_copy(
                    dn2_s.at[pl.ds(slot * ck, ck)],
                    dn2_out[at * group + slot],
                    out_sem.at[6 + slot],
                )
                for slot in range(group)
            ]
            for copy in parts:
                copy.start()
            norm_out[...] += jnp.sum(dn2 * normed, axis=0, keepdims=True)
            for copy in parts:
                copy.wait()

    for copy in saves:
        copy.wait()


def down_kernel(sz, *refs):
    hids, large = refs[:2], refs[2]
    n, ck = sz.chips, sz.chunk
    outs = refs[-n - 3 : -3]
    wd, stage, sem = refs[-3:]
    copies = fetch_weight(sz, large, 2, wd, stage, sem)
    for copy in copies:
        copy.start()
    for copy in copies:
        copy.wait()
    settle_weight(sz, wd, stage)
    for hid, ks in zip(hids, (sz.far, sz.near)):
        for slot, k in enumerate(ks):
            outs[k][...] = mm(hid[slot * ck : (slot + 1) * ck, :], wd[...]).astype(bf16)


def mlp_grads_kernel(sz, layout, *refs):
    n, ck, ffc, half = len(layout), sz.chunk, sz.ffc, sz.half
    gs = refs[:n]
    n2, dgate, dup, hid = (refs[n + 2 * i : n + 2 * i + 2] for i in range(4))
    out, g_far, g_near = refs[-3:]
    for to, ks in ((g_far, list(sz.far)), (g_near, list(sz.near))):
        for ref, (k, first, count) in zip(gs, layout):
            if k in ks:
                at = ks.index(k) * ck + first * ck // 2
                to[at : at + count * ck // 2, :] = ref[...]
    for i, (left, right) in enumerate(((dgate, n2), (dup, n2), (hid, (g_far, g_near)))):
        grads = mm_tn(left[0][...], right[0][...]) + mm_tn(left[1][...], right[1][...])
        grads = grads.astype(bf16)
        for at in range(2 * sz.planes):
            out[at, i * ffc : (i + 1) * ffc, :] = grads[0:ffc, at * half : (at + 1) * half]


def middle_kernel(sz, place, *refs):
    n = sz.chips
    dn2_in = refs[:n]
    middle, g, wo, gains = refs[n : n + 4]
    outs, dh1_out, pay = refs[-n - 2 : -2], refs[-2], refs[-1]
    j = place[0]
    dn2 = dn2_in[0][...].astype(f32)
    for k in range(1, n):
        dn2 = dn2 + dn2_in[k][...].astype(f32)
    mid = middle[...]
    scale = rms(mid)
    normed = mid * scale
    weighted = dn2 * gains[1:2]
    dh1 = g[...].astype(f32) + scale * (
        weighted - normed * jnp.mean(weighted * normed, axis=-1, keepdims=True)
    )
    dh1_out[...] = dh1
    branch = dh1.astype(bf16)
    dmix = mm_nt(branch, wo[...]).astype(bf16)
    for q in range(n):
        pay[q, :, 0 : sz.cv] = dmix[:, q * sz.cv : (q + 1) * sz.cv]
        pay[q, :, sz.cv :] = branch[:, q * sz.co : (q + 1) * sz.co]
    for m in range(n):
        outs[m][...] = pay[j ^ m]


def back_kernel(sz, place, lengths, *refs):
    n, ck, cv = sz.chips, sz.chunk, sz.cv
    heads, total = sz.heads, sz.tokens
    pays = refs[:n]
    act, mixed, den_full, den_rows = refs[n : n + 4]
    outs = refs[n + 4 : 2 * n + 4]
    dact, branch_c, dnum_h, q_h, dden, dq_t, dk, dv = refs[2 * n + 4 :]
    j, c = place[0], place[1]
    lane_q = lax.broadcasted_iota(jnp.int32, (ck, 128), 1) // FEAT
    lane_v = lax.broadcasted_iota(jnp.int32, (ck, sz.vp), 1) // VDIM
    picks = (
        lax.broadcasted_iota(jnp.int32, (8, cv), 1) // VDIM
        == lax.broadcasted_iota(jnp.int32, (8, cv), 0)
    ).astype(f32)
    for k in range(n):
        rows = pl.ds(aligned(j ^ k, ck), ck)
        dmix = pays[k][:, 0:cv].astype(f32)
        branch_c[rows, :] = pays[k][:, cv:]
        dnum = dmix / den_full[rows, 0:cv]
        if sz.vp > cv:
            dnum = jnp.concatenate([dnum, jnp.zeros((ck, sz.vp - cv), f32)], axis=1)
        products = dmix * mixed[rows, :].astype(f32)
        sums = lax.dot_general(
            picks,
            products,
            (((1,), (1,)), ((), ())),
            precision=lax.Precision.HIGHEST,
            preferred_element_type=f32,
        )
        dden[j ^ k] = -sums / den_rows[j ^ k]
        query = act[rows, 0:128].astype(f32) * 0.25
        for h in range(heads):
            dnum_h[h, rows, :] = jnp.where(lane_v == h, dnum, 0.0).astype(bf16)
            q_h[h, rows, :] = jnp.where(lane_q == h, query, 0.0).astype(bf16)
    starts = doc_starts(lengths, c)
    dq_t[...] = jnp.zeros_like(dq_t)
    for b in range(total // ck):
        low = b * ck
        width = total - low
        u_rows = slice(low, low + ck)
        u_at = low + lax.broadcasted_iota(jnp.int32, (ck, 1), 0)
        t_row = low + lax.broadcasted_iota(jnp.int32, (1, width), 1)
        first = latest_start(t_row, starts)
        t_at = low + lax.broadcasted_iota(jnp.int32, (ck, width), 1)
        allowed = (u_at <= t_at) & (u_at >= first)
        keys = act[u_rows, 128:256]
        values = act[u_rows, 256:]
        keys_t = keys.astype(f32).T
        dv_here = jnp.zeros((ck, sz.vp), f32)
        dk_here = jnp.zeros((ck, 128), f32)
        for h in range(heads):
            qs = q_h[h, low:, :]
            ds_in = dnum_h[h, low:, :]
            extra = jnp.concatenate(
                [dden[i][h : h + 1] for i in range(b, total // ck)], axis=1
            )
            s = mm_nt(keys, qs)
            dtaylor = mm_nt(values, ds_in) + extra
            slope = 1.0 + s
            taylor = jnp.where(allowed, slope + 0.5 * s * s, 0.0).astype(bf16)
            dscore = jnp.where(allowed, dtaylor * slope, 0.0).astype(bf16)
            dv_here = dv_here + mm(taylor, ds_in)
            dk_here = dk_here + mm(dscore, qs)
            k_t = keys_t[h * FEAT : (h + 1) * FEAT].astype(bf16)
            dq_t[h * FEAT : (h + 1) * FEAT, low:] += mm(k_t, dscore)
        dk[u_rows, :] = dk_here.astype(bf16)
        dv[u_rows, :] = dv_here.astype(bf16)
    dact[:, 0:128] = (dq_t[...] * 0.25).T.astype(bf16)
    dact[:, 128:256] = dk[...]
    dact[:, 256:] = dv[...]
    for k in range(n):
        rows = pl.ds(aligned(j ^ k, ck), ck)
        outs[k][:, 0 : sz.cq] = dact[rows, 0 : sz.cq]
        outs[k][:, sz.cq : 2 * sz.cq] = dact[rows, 128 : 128 + sz.cq]
        outs[k][:, 2 * sz.cq :] = dact[rows, 256 : 256 + cv]


def back_grads_kernel(sz, layout, place, *refs):
    n, ck, cq, cv, co = sz.chips, sz.chunk, sz.cq, sz.cv, sz.co
    half, cols = sz.half, sz.cols
    i = len(layout)
    mixed = refs[:i]
    entry, dact, branch_c, norm2, norm2_more, gains, w = refs[i : i + 7]
    keep, sends = refs[-3 - sz.planes], refs[-2 - sz.planes : -2]
    dact_s, out = refs[-2:]
    j, c = place[0], place[1]
    for k in range(n):
        rows = slice(k * ck, (k + 1) * ck)
        dact_s[rows, :] = dact[pl.ds(aligned(j ^ k, ck), ck), :]
    grads = mm_tn(dact_s[...], entry[...])
    norm1 = jnp.sum(grads * w[...].astype(f32).T, axis=0, keepdims=True)
    grads = grads.astype(bf16)
    norms = jnp.concatenate(
        [norm1 / gains[0:1], norm2[...] + norm2_more[...], jnp.zeros((14, sz.model), f32)], axis=0
    ).astype(bf16)
    for at in range(2 * sz.planes):
        lanes = slice(at * half, (at + 1) * half)
        out[at, 0:cq, :] = grads[0:cq, lanes]
        out[at, cq : 2 * cq, :] = grads[128 : 128 + cq, lanes]
        out[at, 2 * cq : 2 * cq + cv, :] = grads[256 : 256 + cv, lanes]
        out[at, cols:, :] = norms[:, lanes]
    for ref, (m, first, count) in zip(mixed, layout):
        grads = mm_tn(branch_c[...], ref[...]).astype(bf16)
        at = (j ^ m) * (cv // half) + first * cv // (2 * half)
        for i in range(count * cv // (2 * half)):
            out[at + i, 2 * cq + cv : cols, :] = grads[:, i * half : (i + 1) * half]
    for z in range(sz.planes):
        keep[z] = out[2 * z + c]
        sends[z][...] = out[2 * z + 1 - c]


def pair_sum_kernel(sz, place, keep, *refs):
    received, outs, sums = refs[: sz.planes], refs[sz.planes : -1], refs[-1]
    plane = place[2]
    for z in range(sz.planes):
        sums[z] = (keep[z].astype(f32) + received[z][...].astype(f32)).astype(bf16)
    for k in range(sz.planes):
        outs[k][...] = sums[plane ^ k]


def plane_sum_kernel(sz, *refs):
    total = refs[0][...].astype(f32)
    for ref in refs[1 : sz.planes]:
        total = total + ref[...].astype(f32)
    refs[-1][...] = total.astype(bf16)


def split_rows(sz, place, values, keep, send):
    for core in range(2):

        @pl.when(place[1] == core)
        def _():
            for to, side in ((keep, core), (send, 1 - core)):
                to[...] = values[side * sz.block : (side + 1) * sz.block]


def join_kernel(sz, place, *refs):
    for i in range(2):
        keep, received = refs[2 * i : 2 * i + 2]
        out = refs[-2 + i]
        out[place[1]] = keep[...]
        out[1 - place[1]] = received[...]


def finish_block_kernel(sz, place, *refs):
    result = refs[0][...]
    for part in refs[1 : sz.chips + 1]:
        result = result + part[...].astype(f32)
    keep, send = refs[-2], refs[-1]
    split_rows(sz, place, result.astype(bf16), keep, send)


def finish_tokens_kernel(sz, place, *refs):
    n = sz.chips
    dact_in = refs[:n]
    w_qkv, dh1, x, gains, keep, send = refs[n:]
    values = x[...].astype(f32)
    scale = rms(values)
    normed = values * scale
    dn1 = mm_nt(dact_in[0][...], w_qkv[0])
    for k in range(1, n):
        dn1 = dn1 + mm_nt(dact_in[k][...], w_qkv[k])
    weighted = dn1 * gains[0:1]
    result = dh1[...] + scale * (
        weighted - normed * jnp.mean(weighted * normed, axis=-1, keepdims=True)
    )
    split_rows(sz, place, result, keep, send)


def gathered(sz, layout, place, refs, to):
    n = len(layout)
    j, c = place[0], place[1]
    rows = to.shape[2]
    for some, side in ((refs[:n], c), (refs[n : 2 * n], 1 - c)):
        for ref, (k, first, count) in zip(some, layout):
            at, size = first * rows // 2, count * rows // 2
            to[j ^ k, side, at : at + size] = ref[...]


def finish_attention_kernel(sz, layout, place, *refs):
    n, shard, cq, cv, co = sz.chips, sz.shard, sz.cq, sz.cv, sz.co
    query, key, value, output, norms, all_c = refs[2 * len(layout) :]
    gathered(sz, layout, place, refs, all_c)
    total = jnp.zeros((16, shard), f32)
    for q in range(n):
        part = jnp.concatenate([all_c[q, 0], all_c[q, 1]], axis=1).astype(f32)
        query[:, q * cq : (q + 1) * cq] = part[0:cq].T
        key[:, q * cq : (q + 1) * cq] = part[cq : 2 * cq].T
        value[:, q * cv : (q + 1) * cv] = part[2 * cq : 2 * cq + cv].T
        output[:, q * co : (q + 1) * co] = part[2 * cq + cv : sz.cols].T
        total = total + part[sz.cols :]
    norms[...] = total[0:8]


def finish_mlp_kernel(sz, layout, place, *refs):
    half, ffc = sz.half, sz.ffc
    *outs, all_c = refs[2 * len(layout) :]
    gathered(sz, layout, place, refs, all_c)
    for q in range(sz.chips):
        at = q * ffc
        count = max(0, min(ffc, sz.hidden - at))
        for i, out in enumerate(outs):
            for side in range(2):
                if count:
                    out[at : at + count, side * half : (side + 1) * half] = all_c[
                        q, side, i * ffc : i * ffc + count, :
                    ].astype(f32)


def kernel(body, name, outs, scratch=(), smem=0, room=60, in_specs=None, out_specs=None, **more):
    shapes = [jax.ShapeDtypeStruct(shape, dtype) for shape, dtype in outs]
    scratch = [VMEM(shape, dtype) for shape, dtype in scratch] + list(more.pop("semaphores", ()))

    def run(*args, after=(), carry=()):
        n_in, n_out = len(args), len(shapes)
        loose = len(after) + len(carry)

        def trimmed(*refs):
            first = n_in + loose
            body(*refs[:n_in], *refs[first : first + n_out], *refs[first + n_out + len(carry) :])

        takes = in_specs or [scalars()] * smem + [whole()] * (n_in - smem)
        gives = out_specs or [whole()] * n_out
        return pl.pallas_call(
            trimmed,
            name=name,
            out_shape=shapes + [jax.ShapeDtypeStruct(a.shape, a.dtype) for a in carry],
            in_specs=takes + [anywhere()] * loose,
            out_specs=gives + [anywhere()] * len(carry),
            scratch_shapes=scratch,
            input_output_aliases={n_in + len(after) + i: n_out + i for i in range(len(carry))},
            compiler_params=pltpu.CompilerParams(vmem_limit_bytes=room * MIB),
            cost_estimate=pl.CostEstimate(
                flops=int(COST[name] * 1.15e9), bytes_accessed=0, transcendentals=0
            ),
            **more,
        )(*args, *after, *carry)

    return run


def shards(
    n_chip,
    n_dp,
    tokens,
    cotangent,
    doc_lengths,
    norm1_gain,
    w_query,
    w_key,
    w_value,
    w_output,
    norm2_gain,
    w_gate,
    w_up,
    w_down,
):
    rows_here, block, model = tokens.shape
    hidden = w_gate.shape[1]
    sz = Sizes(n_dp, n_chip, block, w_query.shape[0], model, hidden)
    n, ck, cq, cv, co, ffc = sz.chips, sz.chunk, sz.cq, sz.cv, sz.co, sz.ffc
    half, shard, total = sz.half, sz.shard, sz.tokens
    tight = lambda mib: mib if n == 4 else 60
    chip, core = lax.axis_index("chip"), lax.axis_index("core")
    place = jnp.stack([chip, core, lax.axis_index("dp")]).astype(jnp.int32)

    def swap(a):
        return lax.ppermute(a, "core", [(0, 1), (1, 0)])

    def to_chip(a, k):
        return lax.ppermute(a, "chip", [(i, i ^ k) for i in range(n)])

    def to_plane(a, k):
        return lax.ppermute(a, "dp", [(i, i ^ k) for i in range(n_dp)])

    def spread(a, name, axis=0):
        if n != 4 or not TWICE[name]:
            return [a] + [to_chip(a, k) for k in range(1, n)], sz.direct
        first, second = to_chip(a, 1), to_chip(a, 2)
        middle = a.shape[axis] // 2
        low = to_chip(lax.slice_in_dim(second, 0, middle, axis=axis), 1)
        high = to_chip(lax.slice_in_dim(first, middle, 2 * middle, axis=axis), 2)
        return [a, first, second, low, high], sz.pieces

    def exchange(parts):
        return [parts[0]] + [to_chip(parts[k], k) for k in range(1, n)]

    def to_rows(a):
        return lax.all_to_all(a, "core", 0, 0).reshape(ck, model)

    def when(name, *arrays):
        return list(arrays) if TIES[name] else []

    with jax.named_scope("gather_tokens"):
        xs, lay_x = spread(to_rows(tokens), "x")

    with jax.named_scope("pack_small"):
        (small,) = kernel(
            partial(pack_small_kernel, sz), "pack_small", [((half + 16, sz.wa), bf16)], smem=1
        )(
            place,
            w_query,
            w_key,
            w_value,
            w_output,
            norm1_gain,
            norm2_gain,
            after=when("small_x", xs[0]),
        )
        small_own = [small] + [to_plane(small, k) for k in range(1, n_dp)]
        small_oth = [swap(a) for a in small_own]

    with jax.named_scope("pack_large"):
        loads = anywhere() if half % 128 == 0 else whole()
        (large,) = kernel(
            partial(pack_large_kernel, sz),
            "pack_large",
            [((3 * ffc, half), bf16)],
            in_specs=[scalars()] + [loads] * 3,
            semaphores=[pltpu.SemaphoreType.DMA((3,))],
        )(place, w_gate.T, w_up.T, w_down)
        g_here = to_rows(cotangent)
        (large,) = kernel(lambda *refs: None, "after_small", [])(
            after=small_own[1:]
            + when("large_x", *xs[1:3])
            + when("large_x3", *xs[3:])
            + when("large_g", g_here),
            carry=[large],
        )
        large_all = lax.all_gather(large, ("dp", "core"))

    with jax.named_scope("project"):
        act, w_act, entry_one, gains, *carried = kernel(
            partial(project_kernel, sz, lay_x),
            "project",
            [
                ((total, sz.qw), bf16),
                ((model, sz.qw), bf16),
                ((total, model), bf16),
                ((2, model), f32),
            ],
            [((n_dp, 2, shard), f32)],
            smem=1,
        )(place, *xs, *small_own, *small_oth, carry=when("g_project", g_here))
        g_here = carried[0] if carried else g_here

    with jax.named_scope("gather_cotangent"):
        gs, lay_g = spread(g_here, "g")

    with jax.named_scope("take"):
        wo_half, qkv_half = kernel(
            partial(take_output_kernel, sz),
            "take_output",
            [((n_dp, half, co), bf16), ((n_dp, half, sz.qkv), bf16)],
        )(*small_own, after=when("take_oth", *small_oth) + when("take_x", *xs[1:]))
        wo_parts, lay_wo = spread(wo_half, "wo")

    with jax.named_scope("attention"):
        mixed_own, den_full, den_rows = kernel(
            partial(attend_kernel, sz),
            "attend",
            [
                ((total, cv), bf16),
                ((total, sz.vp), f32),
                ((total // ck, 8, ck), f32),
            ],
            smem=2,
            room=tight(20),
        )(place, doc_lengths, act, after=when("attend_wo", wo_parts[1]))
        mixed, lay_o = spread(mixed_own, "o", 1)

    with jax.named_scope("output_weight"):
        wo_own, *carried = kernel(
            partial(output_weight_kernel, sz, lay_wo),
            "output_weight",
            [((n_dp, half, model), bf16)],
            [((n, n_dp, half, co), bf16)],
            smem=1,
            room=tight(20),
        )(
            place,
            *wo_parts,
            after=when("ow_mixed", *mixed[1:3])
            + when("ow_own", mixed_own)
            + when("ow_g", *gs[1:3]),
            carry=when("qkv_ow", qkv_half),
        )
        qkv_half = carried[0] if carried else qkv_half
        wo_oth = swap(wo_own)

    with jax.named_scope("before_mlp"):
        if TIES["qkv_tie"]:
            (qkv_half,) = kernel(lambda *refs: None, "before_mlp", [])(
                after=[*mixed[1:], *gs[1:], wo_oth], carry=[qkv_half]
            )

    with jax.named_scope("mlp"):
        group = 2 if n == 4 else 1
        size = group * ck
        part = total // 2

        def mlp(ks, name, after):
            some_x, some_g = picked(lay_x, ks), picked(lay_g, ks)
            count, loads = len(ks), len(some_x) + len(some_g) + len(mixed) + 3
            results = kernel(
                partial(mlp_kernel, sz, ks, group, (lay_x, lay_g, lay_o)),
                name,
                [((ck, model), bf16)] * count
                + [
                    ((part, model), bf16),
                    ((part, sz.ffp), bf16),
                    ((part, sz.ffp), bf16),
                    ((part, sz.ffp), bf16),
                    ((1, model), f32),
                    ((model, model), bf16),
                    ((ck, model), f32),
                ],
                [
                    ((size, model), bf16),
                    ((size, model), bf16),
                    ((n, size, cv), bf16),
                    ((model, model), bf16),
                    ((sz.ffp, model), bf16),
                    ((sz.ffp, model), bf16),
                    ((sz.ffp, model), bf16),
                    ((size, model), bf16),
                    ((size, sz.ffp), bf16),
                    ((size, sz.ffp), bf16),
                    ((size, sz.ffp), bf16),
                    ((size, model), bf16),
                    ((ck, model), f32),
                ]
                + stages(sz, 3),
                semaphores=[
                    pltpu.SemaphoreType.DMA((6,)),
                    pltpu.SemaphoreType.DMA((6 + group,)),
                ],
                in_specs=[scalars()] + [anywhere()] * loads + [whole()],
                out_specs=[anywhere()] * (count + 4) + [whole()] + [anywhere()] * 2,
                grid=(count // group,),
            )(
                place,
                *[xs[i] for i in some_x],
                *[gs[i] for i in some_g],
                *mixed,
                wo_own,
                wo_oth,
                large_all,
                gains,
                after=after,
            )
            return dict(zip(ks, results[:count])), results[count:]

        far_parts, far = mlp(sz.far, "mlp_far", when("qkv_tie", qkv_half))
        far_in = {k: to_chip(a, k) for k, a in far_parts.items()}
        near_parts, near = mlp(sz.near, "mlp_near", when("near_far", far[4]))
        near_in = {k: to_chip(a, k) for k, a in near_parts.items() if k}
        dn2_in = [near_parts[0]] + [{**far_in, **near_in}[k] for k in range(1, n)]
        wo, middle = near[5], near[6]

    with jax.named_scope("gather_qkv"):
        qkv_own, lay_q = spread(qkv_half, "qkv")

    with jax.named_scope("mlp_grads"):
        mlp_grads, *carried = kernel(
            partial(mlp_grads_kernel, sz, lay_g),
            "mlp_grads",
            [((2 * n_dp, 3 * ffc, half), bf16)],
            [((part, model), bf16)] * 2,
        )(
            *gs,
            *[a for pair in zip(far[:4], near[:4]) for a in pair],
            after=when("grads_far", *far_in.values()),
            carry=when("grads_qkv", *qkv_own),
        )
        qkv_own = carried or qkv_own
        qkv_oth = [swap(a) for a in qkv_own]
        mlp_shard = lax.psum_scatter(mlp_grads, ("dp", "core"), scatter_dimension=0)

    with jax.named_scope("middle"):
        results = kernel(
            partial(middle_kernel, sz),
            "middle",
            [((ck, cv + co), bf16)] * n + [((ck, model), f32)],
            [((n, ck, cv + co), bf16)],
            smem=1,
        )(
            place,
            *dn2_in,
            middle,
            gs[0],
            wo,
            gains,
            after=when("middle_grads", mlp_grads) + when("middle_qkv", *qkv_own[1:]),
        )
        dh1 = results[n]
        pays = exchange(results[:n])

    with jax.named_scope("gather_qkv"):
        (w_qkv,) = kernel(
            partial(gather_qkv_kernel, sz, lay_q),
            "gather_qkv",
            [((n, model, sz.qkv), bf16)],
            smem=1,
            room=tight(20),
        )(place, *qkv_own, *qkv_oth, after=when("gq_middle", dh1))

    with jax.named_scope("down"):
        down_parts = kernel(
            partial(down_kernel, sz),
            "down",
            [((ck, model), bf16)] * n,
            [((sz.ffp, model), bf16)] + stages(sz, 1),
            room=tight(20),
            in_specs=[whole()] * 2 + [anywhere()],
            semaphores=[pltpu.SemaphoreType.DMA],
        )(far[3], near[3], large_all, after=when("down_middle", dh1) + when("down_gq", w_qkv))
        down_in = exchange(down_parts)

    with jax.named_scope("attention_back"):
        results = kernel(
            partial(back_kernel, sz),
            "attention_back",
            [((ck, sz.qkv), bf16)] * n + [((total, sz.qw), bf16), ((total, co), bf16)],
            [
                ((sz.heads, total, sz.vp), bf16),
                ((sz.heads, total, 128), bf16),
                ((total // ck, 8, ck), f32),
                ((128, total), f32),
                ((total, 128), bf16),
                ((total, sz.vp), bf16),
            ],
            smem=2,
            room=tight(44),
        )(
            place,
            doc_lengths,
            *pays,
            act,
            mixed_own,
            den_full,
            den_rows,
            after=when("back_down", down_parts[0]) + when("back_gq", w_qkv),
        )
        dact, branch_c = results[n], results[n + 1]
        dact_in = exchange(results[:n])

    with jax.named_scope("attention_grads"):
        width = sz.cols + 16
        keep, *sends = kernel(
            partial(back_grads_kernel, sz, lay_o),
            "attention_grads",
            [((n_dp, width, half), bf16)] + [((width, half), bf16)] * n_dp,
            [((total, sz.qw), bf16), ((2 * n_dp, width, half), bf16)],
            smem=1,
            room=tight(28),
        )(
            place,
            *mixed,
            entry_one,
            dact,
            branch_c,
            far[4],
            near[4],
            gains,
            w_act,
            after=when("ag_down", *down_in[1:]),
        )

    with jax.named_scope("finish_block"):
        block_keep, block_send = kernel(
            partial(finish_block_kernel, sz), "finish_block", [((block, model), bf16)] * 2, smem=1
        )(place, middle, *down_in)
        block_other = swap(block_send)

    with jax.named_scope("finish_tokens"):
        grad_keep, grad_send = kernel(
            partial(finish_tokens_kernel, sz), "finish_tokens", [((block, model), f32)] * 2, smem=1
        )(place, *dact_in, w_qkv, dh1, xs[0], gains)
        grad_other = swap(grad_send)

    with jax.named_scope("sum_gradients"):
        *parts, mlp_shard = kernel(
            partial(pair_sum_kernel, sz),
            "pair_sum",
            [((width, half), bf16)] * n_dp,
            [((n_dp, width, half), bf16)],
            smem=1,
            room=tight(20),
        )(
            place,
            keep,
            *[swap(a) for a in sends],
            after=when("pair_tokens", grad_keep) + when("pair_block", block_keep),
            carry=[mlp_shard],
        )
        sums = [parts[0]] + [to_plane(parts[k], k) for k in range(1, n_dp)]

    with jax.named_scope("spread_gradients"):
        att_shard, *carried = kernel(
            partial(plane_sum_kernel, sz), "plane_sum", [((width, half), bf16)], room=tight(20)
        )(
            *sums,
            after=when("plane_tokens", grad_keep) + when("plane_block", block_keep),
            carry=when("mlp_plane", mlp_shard),
        )
        mlp_shard = carried[0] if carried else mlp_shard
        mlp_own, lay_m = spread(mlp_shard, "mlp")
        mlp_oth = [swap(a) for a in mlp_own]
        att_own, lay_a = spread(att_shard, "att")
        att_oth = [swap(a) for a in att_own]

    with jax.named_scope("join"):
        block_out, grad_tokens = kernel(
            partial(join_kernel, sz),
            "join",
            [((2, block, model), bf16), ((2, block, model), f32)],
            smem=1,
        )(place, block_keep, block_other, grad_keep, grad_other)

    with jax.named_scope("finish_attention"):
        total_query, total_key, total_value, total_output, norms = kernel(
            partial(finish_attention_kernel, sz, lay_a),
            "finish_attention",
            [
                ((shard, n * cq), f32),
                ((shard, n * cq), f32),
                ((shard, n * cv), f32),
                ((shard, n * co), f32),
                ((8, shard), f32),
            ],
            [((n, 2, width, half), bf16)],
            smem=1,
            room=tight(20),
        )(place, *att_own, *att_oth, after=when("fa_tokens", grad_keep))

    with jax.named_scope("finish_mlp"):
        total_gate, total_up, total_down = kernel(
            partial(finish_mlp_kernel, sz, lay_m),
            "finish_mlp",
            [((hidden, shard), f32)] * 3,
            [((n, 2, 3 * ffc, half), bf16)],
            smem=1,
            room=tight(24),
        )(place, *mlp_own, *mlp_oth, after=when("fm_norms", norms) + when("fm_join", block_out))

    return (
        block_out,
        grad_tokens,
        norms[0],
        total_query,
        total_key,
        total_value,
        total_output,
        norms[1],
        total_gate.T,
        total_up.T,
        total_down,
    )


def solution(mesh):
    n_dp, n_seq = mesh.shape["dp"], mesh.shape["seq"]
    n_chip = n_seq // 2
    grid = Mesh(mesh.devices.reshape(n_dp, n_chip, 2), ("dp", "chip", "core"))
    seq = ("chip", "core")
    placed = (
        P("dp", seq, None),
        P("dp", seq, None),
        P("dp", None),
        P("dp"),
        P("dp", None),
        P("dp", None),
        P("dp", None),
        P("dp", None),
        P("dp"),
        P("dp", None),
        P("dp", None),
        P(None, "dp"),
    )
    return jax.shard_map(
        partial(shards, n_chip, n_dp),
        mesh=grid,
        in_specs=placed,
        out_specs=(
            P("dp", seq, None),
            P("dp", seq, None),
            P("dp"),
            P("dp", None),
            P("dp", None),
            P("dp", None),
            P("dp", None),
            P("dp"),
            P("dp", None),
            P("dp", None),
            P(None, "dp"),
        ),
        check_vma=False,
    )
```

```python
import math
from functools import partial

import jax
import jax.numpy as jnp
from jax import lax
from jax.experimental import pallas as pl
from jax.experimental.pallas import tpu as pltpu
from jax.sharding import Mesh
from jax.sharding import PartitionSpec as P

HEADS = 16
FEAT = 16
VDIM = 64
EPSILON = 1e-05

bf16 = jnp.bfloat16
f32 = jnp.float32
VMEM = pltpu.VMEM
SMEM = pltpu.SMEM
MIB = 1024 * 1024

COST = dict(
    g_take=0.1,
    pack_small=0.5,
    pack_large=100.0,
    after_small=0.5,
    project=100.0,
    take_output=7.0,
    attend=4.0,
    output_weight=0.5,
    before_mlp=0.1,
    mlp_far=100.0,
    mlp_near=35.0,
    mlp_grads=2.0,
    middle=30.0,
    gather_qkv=1.0,
    down=0.1,
    attention_back=60.0,
    attention_grads=0.1,
    pair_sum=35.0,
    finish_block=0.5,
    finish_tokens=0.5,
    plane_sum=2.0,
    join=2.0,
    finish_attention=0.1,
    finish_mlp=35.0,
)
TWICE = dict(
    x=0,
    g=1,
    wo=1,
    o=1,
    qkv=0,
    att=0,
    mlp=1,
)
TIES = dict(
    small_x=0,
    large_x=1,
    large_x3=0,
    large_g=0,
    project_g=0,
    attend_g=0,
    attend_g1=0,
    g_take=1,
    take_oth=0,
    take_x=0,
    attend_wo=0,
    ow_mixed=1,
    ow_own=0,
    ow_g=1,
    qkv_ow=0,
    qkv_tie=1,
    near_far=0,
    grads_qkv=1,
    grads_far=0,
    middle_grads=1,
    middle_qkv=0,
    gq_middle=1,
    down_middle=1,
    down_gq=0,
    back_down=1,
    back_gq=1,
    ag_down=1,
    pair_tokens=0,
    pair_block=0,
    plane_tokens=0,
    plane_block=0,
    mlp_plane=0,
    fa_tokens=1,
    fm_norms=0,
    fm_join=0,
)


def mm(left, right):
    return jnp.dot(left, right, preferred_element_type=f32)


def mm_nt(left, right):
    return lax.dot_general(left, right, (((1,), (1,)), ((), ())), preferred_element_type=f32)


def mm_tn(left, right):
    return lax.dot_general(left, right, (((0,), (0,)), ((), ())), preferred_element_type=f32)


def up_to(value, step):
    return -(-value // step) * step


def whole():
    return pl.BlockSpec(memory_space=VMEM, pipeline_mode=pl.Buffered(1))


def anywhere():
    return pl.BlockSpec(memory_space=pl.ANY)


def scalars():
    return pl.BlockSpec(memory_space=SMEM)


def rms(values):
    return lax.rsqrt(jnp.mean(values * values, axis=-1, keepdims=True) + EPSILON)


def shard_row(pieces, row):
    return jnp.concatenate([pieces[z] for z in range(pieces.shape[0])], axis=1)[row : row + 1]


def doc_starts(lengths, row):
    starts, total = [], jnp.int32(0)
    for i in range(lengths.shape[1]):
        starts.append(total)
        total = total + lengths[row, i]
    return starts


def latest_start(position, starts):
    latest = jnp.zeros_like(position)
    for start in starts:
        latest = jnp.where(position >= start, start, latest)
    return latest


class Sizes:
    def __init__(self, planes, chips, block, shard, model, hidden):
        self.planes, self.chips, self.block = planes, chips, block
        self.chunk = 2 * block
        self.tokens = chips * self.chunk
        self.shard, self.half, self.model = shard, shard // 2, model
        self.heads = HEADS // chips
        self.cq = self.heads * FEAT
        self.cv = self.heads * VDIM
        self.co = model // chips
        self.vp = up_to(self.cv, 128)
        self.qw = 256 + self.vp
        self.wa = max(512, 2 * self.cq + self.cv + self.co)
        self.hidden = hidden
        self.ffc = up_to(-(-hidden // chips), 16)
        self.ffp = up_to(self.ffc, 128)
        self.cols = 2 * self.cq + self.cv + self.co
        self.qkv = 2 * self.cq + self.cv
        self.pieces = self.direct = [(k, 0, 2) for k in range(chips)]
        self.far, self.near = range(chips - 1, chips // 2 - 1, -1), range(chips // 2 - 1, -1, -1)
        if chips == 4:
            self.pieces = [(0, 0, 2), (1, 0, 2), (2, 0, 2), (3, 0, 1), (3, 1, 1)]


def aligned(index, step):
    return pl.multiple_of(index * step, step)


def pack_large_kernel(sz, place, *refs):
    weights, out, sem = refs[:3], refs[-2], refs[-1]
    half, ffc = sz.half, sz.ffc
    j, c = place[0], place[1]
    for chip in range(sz.chips):
        first = chip * ffc
        count = max(0, min(ffc, sz.hidden - first))
        for core in range(2):

            @pl.when((j == chip) & (c == core))
            def _():
                lanes = slice(core * half, (core + 1) * half)
                copies = []
                for i, weight in enumerate(weights):
                    if count == 0:
                        continue
                    if half % 128:
                        out[i * ffc : i * ffc + count, :] = weight[first : first + count, lanes]
                        continue
                    copies.append(
                        pltpu.make_async_copy(
                            weight.at[pl.ds(first, count), pl.ds(core * half, half)],
                            out.at[pl.ds(i * ffc, count)],
                            sem.at[i],
                        )
                    )
                for copy in copies:
                    copy.start()
                for i in range(3):
                    if count < ffc:
                        out[i * ffc + count : (i + 1) * ffc, :] = jnp.zeros(
                            (ffc - count, half), bf16
                        )
                for copy in copies:
                    copy.wait()


def pack_small_kernel(sz, place, w_query, w_key, w_value, w_output, gain_one, gain_two, out):
    half, cq, cv, co = sz.half, sz.cq, sz.cv, sz.co
    j, c = place[0], place[1]
    side = pl.ds(aligned(c, half), half)
    out[...] = jnp.zeros_like(out)
    for chip in range(sz.chips):

        @pl.when(j == chip)
        def _():
            out[0:half, 0:cq] = w_query[side, chip * cq : (chip + 1) * cq]
            out[0:half, cq : 2 * cq] = w_key[side, chip * cq : (chip + 1) * cq]
            out[0:half, 2 * cq : 2 * cq + cv] = w_value[side, chip * cv : (chip + 1) * cv]
            out[0:half, 2 * cq + cv : sz.cols] = w_output[side, chip * co : (chip + 1) * co]

    for i, gain in enumerate((gain_one, gain_two)):
        row = gain[...].reshape(1, sz.shard)
        out[half : half + 16, i * 256 : i * 256 + sz.shard] = jnp.broadcast_to(row, (16, sz.shard))


def project_kernel(sz, layout, place, *refs):
    n, p = len(layout), sz.planes
    xs, own, oth = refs[:n], refs[n : n + p], refs[n + p : n + 2 * p]
    act, w, entry, gains, gain_c = refs[n + 2 * p :]
    j, c, plane = place[0], place[1], place[2]
    half, shard, cq, cv, ck = sz.half, sz.shard, sz.cq, sz.cv, sz.chunk
    w[...] = jnp.zeros_like(w)
    for k in range(p):
        z = plane ^ k
        for piece, side in ((own[k], c), (oth[k], 1 - c)):
            rows = pl.ds(pl.multiple_of(z * shard + side * half, half), half)
            w[rows, 0:cq] = piece[0:half, 0:cq]
            w[rows, 128 : 128 + cq] = piece[0:half, cq : 2 * cq]
            w[rows, 256 : 256 + cv] = piece[0:half, 2 * cq : 2 * cq + cv]
        for i in range(2):
            row = own[k][half : half + 16, i * 256 : i * 256 + shard]
            gain_c[z, i : i + 1] = row[0:1].astype(f32)
    for i in range(2):
        gains[i : i + 1] = shard_row(gain_c, i)
    gain = gains[0:1]
    for ref, (k, first, count) in zip(xs, layout):
        x = ref[...].astype(f32)
        at = k * ck + first * ck // 2
        entry[at : at + count * ck // 2, :] = ((x * rms(x)) * gain).astype(bf16)
    for k in range(sz.chips):
        rows = pl.ds(aligned(j ^ k, ck), ck)
        act[rows, :] = mm(entry[k * ck : (k + 1) * ck, :], w[...]).astype(bf16)


def attend_kernel(sz, place, lengths, act, mixed, den_full, den_rows):
    c, ck, cv = place[1], sz.chunk, sz.cv
    starts = doc_starts(lengths, c)
    lane_q = lax.broadcasted_iota(jnp.int32, (ck, 128), 1) // FEAT
    lane_v = lax.broadcasted_iota(jnp.int32, (ck, sz.vp), 1) // VDIM
    lane = lax.broadcasted_iota(jnp.int32, (ck, 128), 1)
    for b in range(sz.tokens // ck):
        rows = slice(b * ck, (b + 1) * ck)
        width = (b + 1) * ck
        t_at = b * ck + lax.broadcasted_iota(jnp.int32, (ck, 1), 0)
        first = latest_start(t_at, starts)
        u_at = lax.broadcasted_iota(jnp.int32, (ck, width), 1)
        allowed = (u_at <= t_at) & (u_at >= first)
        query = act[rows, 0:128]
        keys = act[0:width, 128:256]
        values = act[0:width, 256:]
        att = jnp.zeros((ck, sz.vp), f32)
        den_wide = jnp.ones((ck, sz.vp), f32)
        den_some = jnp.ones((ck, 128), f32)
        for h in range(sz.heads):
            mine = jnp.where(lane_q == h, query.astype(f32) * 0.25, 0.0).astype(bf16)
            s = mm_nt(mine, keys)
            taylor = jnp.where(allowed, 1.0 + s + 0.5 * s * s, 0.0).astype(bf16)
            den = jnp.sum(taylor.astype(f32), axis=1, keepdims=True)
            num = mm(taylor, values)
            att = jnp.where(lane_v == h, num / den, att)
            den_wide = jnp.where(lane_v == h, den, den_wide)
            den_some = jnp.where(lane == h, den, den_some)
        mixed[rows, :] = att.astype(bf16)[:, 0:cv]
        den_full[rows, :] = den_wide
        den_rows[b] = den_some.T[0:8]


def take_output_kernel(sz, *refs):
    for k in range(sz.planes):
        refs[-2][k] = refs[k][0 : sz.half, sz.qkv : sz.cols]
        refs[-1][k] = refs[k][0 : sz.half, 0 : sz.qkv]


def gather_qkv_kernel(sz, layout, place, *refs):
    n, half, planes = len(layout), sz.half, sz.planes
    out = refs[-1]
    c, plane = place[1], place[2]
    for pieces, side in ((refs[:n], c), (refs[n : 2 * n], 1 - c)):
        for ref, (k, first, count) in zip(pieces, layout):
            for i in range(count * planes // 2):
                z = plane ^ (first * planes // 2 + i)
                at = pl.multiple_of(z * sz.shard + side * half, half)
                out[k, pl.ds(at, half), :] = ref[i]


def output_weight_kernel(sz, layout, place, *refs):
    planes = sz.planes
    *pieces, out, out_c = refs
    j, plane = place[0], place[2]
    for ref, (k, first, count) in zip(pieces, layout):
        out_c[j ^ k, first * planes // 2 : (first + count) * planes // 2] = ref[...]
    for z in range(planes):
        out[plane ^ z] = jnp.concatenate([out_c[q, z] for q in range(sz.chips)], axis=1)


def fetch_weight(sz, large, which, to, stage, sem):
    half, ffc = sz.half, sz.ffc
    rows = pl.ds(which * ffc, ffc)
    if half % 128:
        return [pltpu.make_async_copy(large.at[:, rows], stage, sem)]
    return [
        pltpu.make_async_copy(
            large.at[at, rows], to.at[pl.ds(0, ffc), pl.ds(at * half, half)], sem
        )
        for at in range(2 * sz.planes)
    ]


def settle_weight(sz, to, stage):
    ffc, half = sz.ffc, sz.half
    if half % 128:
        for at in range(2 * sz.planes):
            to[0:ffc, at * half : (at + 1) * half] = stage[at]
    if sz.ffp > ffc:
        to[ffc:, :] = jnp.zeros((sz.ffp - ffc, sz.model), bf16)


def stages(sz, count):
    if sz.half % 128:
        return [((2 * sz.planes, sz.ffc, sz.half), bf16)] * count
    return [((8, 128), bf16)] * count


def picked(layout, ks):
    return [i for i, (k, _, _) in enumerate(layout) if k in ks]


def mlp_kernel(sz, ks, group, layouts, place, *refs):
    n, ck, cv, half, shard, ffc = sz.chips, sz.chunk, sz.cv, sz.half, sz.shard, sz.ffc
    lay_x, lay_g, lay_o = layouts
    some_x, some_g = picked(lay_x, ks), picked(lay_g, ks)
    i, total = len(some_x), len(some_x) + len(some_g)
    xs, gs, mixed = refs[:i], refs[i:total], refs[total : total + len(lay_o)]
    total = total + len(lay_o)
    wo_own, wo_oth, large, gains = refs[total : total + 4]
    outs = refs[total + 4 :]
    dn2_out = outs[: len(ks)]
    n2_out, dgate_out, dup_out, hid_out, norm_out, wo_out, mid_out = outs[len(ks) : len(ks) + 7]
    scratch = outs[len(ks) + 7 :]
    x_s, g_s, o_c, wo, wg, wu, wd, n2_s, dgate_s, dup_s, hid_s, dn2_s, mid_s = scratch[:13]
    stage, sem, out_sem = scratch[13:16], scratch[16], scratch[17]
    j, c = place[0], place[1]
    step = pl.program_id(0)
    size = group * ck
    steps = len(ks) // group

    def inputs(at, which):
        here = list(ks)[at * group : (at + 1) * group]
        found = []
        to = g_s if which else x_s
        layout, some = (lay_g, some_g) if which else (lay_x, some_x)
        for source, index in zip(gs if which else xs, some):
            k, low, count = layout[index]
            if k in here:
                rows = pl.ds(here.index(k) * ck + low * ck // 2, count * ck // 2)
                found.append(pltpu.make_async_copy(source, to.at[rows], sem.at[which]))
        if which:
            return found
        for slot, k in enumerate(here):
            rows = pl.ds(slot * ck, ck)
            for ref, (m, low, count) in zip(mixed, lay_o):
                lanes = pl.ds(low * cv // 2, count * cv // 2)
                source = ref.at[pl.ds(aligned(j ^ k, ck), ck)]
                found.append(pltpu.make_async_copy(source, o_c.at[j ^ m, rows, lanes], sem.at[0]))
        return found

    wo_copies = []
    for z in range(sz.planes):
        for piece, side in ((wo_own, c), (wo_oth, 1 - c)):
            rows = pl.ds(pl.multiple_of(z * shard + side * half, half), half)
            wo_copies.append(pltpu.make_async_copy(piece.at[z], wo.at[rows], sem.at[2]))
    weight_copies = [
        fetch_weight(sz, large, i, to, stage[i], sem.at[3 + i])
        for i, to in enumerate((wg, wu, wd))
    ]

    def fresh(act):
        if steps == 1:
            act()
        else:
            pl.when(step == 0)(act)

    for at in range(steps):

        @pl.when(step == at)
        def _():
            for copy in inputs(at, 0):
                copy.start()

    @fresh
    def _():
        norm_out[...] = jnp.zeros_like(norm_out)
        for copy in wo_copies + weight_copies[0] + weight_copies[1]:
            copy.start()

    for at in range(steps):

        @pl.when(step == at)
        def _():
            for copy in inputs(at, 1):
                copy.start()

    @fresh
    def _():
        for copy in weight_copies[2]:
            copy.start()

    for at in range(steps):

        @pl.when(step == at)
        def _():
            for copy in inputs(at, 0):
                copy.wait()

    @fresh
    def _():
        for copy in wo_copies:
            copy.wait()

    mix = jnp.concatenate([o_c[q] for q in range(n)], axis=1)
    middle = x_s[...].astype(f32) + mm(mix, wo[...])
    normed = middle * rms(middle)
    entry = (normed * gains[1:2]).astype(bf16)
    n2_s[...] = entry
    mid_s[...] = middle[size - ck :]

    @fresh
    def _():
        for which in range(2):
            for copy in weight_copies[which]:
                copy.wait()
            settle_weight(sz, (wg, wu)[which], stage[which])

    gate = mm_nt(entry, wg[...])
    upward = mm_nt(entry, wu[...])

    for at in range(steps):

        @pl.when(step == at)
        def _():
            for copy in inputs(at, 1):
                copy.wait()

    @fresh
    def _():
        for copy in weight_copies[2]:
            copy.wait()
        settle_weight(sz, wd, stage[2])

    grad_hidden = mm_nt(g_s[...], wd[...])
    sig = jax.nn.sigmoid(gate)
    silu = gate * sig
    dgate = (grad_hidden * upward * (sig * (1.0 + gate * (1.0 - sig)))).astype(bf16)
    dup = (grad_hidden * silu).astype(bf16)
    dgate_s[...] = dgate
    dup_s[...] = dup
    hid_s[...] = (silu * upward).astype(bf16)
    rows = pl.ds(aligned(step, size), size)
    saves = [
        pltpu.make_async_copy(source, to.at[rows], out_sem.at[index])
        for index, (source, to) in enumerate(
            ((n2_s, n2_out), (dgate_s, dgate_out), (dup_s, dup_out), (hid_s, hid_out))
        )
    ]
    saves.append(pltpu.make_async_copy(mid_s, mid_out, out_sem.at[4]))
    saves.append(pltpu.make_async_copy(wo, wo_out, out_sem.at[5]))
    for copy in saves:
        copy.start()
    dn2 = mm(dgate, wg[...]) + mm(dup, wu[...])
    dn2_s[...] = dn2.astype(bf16)
    for at in range(steps):

        @pl.when(step == at)
        def _():
            parts = [
                pltpu.make_async_copy(
                    dn2_s.at[pl.ds(slot * ck, ck)],
                    dn2_out[at * group + slot],
                    out_sem.at[6 + slot],
                )
                for slot in range(group)
            ]
            for copy in parts:
                copy.start()
            norm_out[...] += jnp.sum(dn2 * normed, axis=0, keepdims=True)
            for copy in parts:
                copy.wait()

    for copy in saves:
        copy.wait()


def down_kernel(sz, *refs):
    hids, large = refs[:2], refs[2]
    n, ck = sz.chips, sz.chunk
    outs = refs[-n - 3 : -3]
    wd, stage, sem = refs[-3:]
    copies = fetch_weight(sz, large, 2, wd, stage, sem)
    for copy in copies:
        copy.start()
    for copy in copies:
        copy.wait()
    settle_weight(sz, wd, stage)
    for hid, ks in zip(hids, (sz.far, sz.near)):
        for slot, k in enumerate(ks):
            outs[k][...] = mm(hid[slot * ck : (slot + 1) * ck, :], wd[...]).astype(bf16)


def mlp_grads_kernel(sz, layout, *refs):
    n, ck, ffc, half = len(layout), sz.chunk, sz.ffc, sz.half
    gs = refs[:n]
    n2, dgate, dup, hid = (refs[n + 2 * i : n + 2 * i + 2] for i in range(4))
    out, g_far, g_near = refs[-3:]
    for to, ks in ((g_far, list(sz.far)), (g_near, list(sz.near))):
        for ref, (k, first, count) in zip(gs, layout):
            if k in ks:
                at = ks.index(k) * ck + first * ck // 2
                to[at : at + count * ck // 2, :] = ref[...]
    for i, (left, right) in enumerate(((dgate, n2), (dup, n2), (hid, (g_far, g_near)))):
        grads = mm_tn(left[0][...], right[0][...]) + mm_tn(left[1][...], right[1][...])
        grads = grads.astype(bf16)
        for at in range(2 * sz.planes):
            out[at, i * ffc : (i + 1) * ffc, :] = grads[0:ffc, at * half : (at + 1) * half]


def middle_kernel(sz, place, *refs):
    n = sz.chips
    dn2_in = refs[:n]
    middle, g, wo, gains = refs[n : n + 4]
    outs, dh1_out, pay = refs[-n - 2 : -2], refs[-2], refs[-1]
    j = place[0]
    dn2 = dn2_in[0][...].astype(f32)
    for k in range(1, n):
        dn2 = dn2 + dn2_in[k][...].astype(f32)
    mid = middle[...]
    scale = rms(mid)
    normed = mid * scale
    weighted = dn2 * gains[1:2]
    dh1 = g[...].astype(f32) + scale * (
        weighted - normed * jnp.mean(weighted * normed, axis=-1, keepdims=True)
    )
    dh1_out[...] = dh1
    branch = dh1.astype(bf16)
    dmix = mm_nt(branch, wo[...]).astype(bf16)
    for q in range(n):
        pay[q, :, 0 : sz.cv] = dmix[:, q * sz.cv : (q + 1) * sz.cv]
        pay[q, :, sz.cv :] = branch[:, q * sz.co : (q + 1) * sz.co]
    for m in range(n):
        outs[m][...] = pay[j ^ m]


def back_kernel(sz, place, lengths, *refs):
    n, ck, cv = sz.chips, sz.chunk, sz.cv
    heads, total = sz.heads, sz.tokens
    pays = refs[:n]
    act, mixed, den_full, den_rows = refs[n : n + 4]
    outs = refs[n + 4 : 2 * n + 4]
    dact, branch_c, dnum_h, q_h, dden, dq_t, dk, dv = refs[2 * n + 4 :]
    j, c = place[0], place[1]
    lane_q = lax.broadcasted_iota(jnp.int32, (ck, 128), 1) // FEAT
    lane_v = lax.broadcasted_iota(jnp.int32, (ck, sz.vp), 1) // VDIM
    picks = (
        lax.broadcasted_iota(jnp.int32, (8, cv), 1) // VDIM
        == lax.broadcasted_iota(jnp.int32, (8, cv), 0)
    ).astype(f32)
    for k in range(n):
        rows = pl.ds(aligned(j ^ k, ck), ck)
        dmix = pays[k][:, 0:cv].astype(f32)
        branch_c[rows, :] = pays[k][:, cv:]
        dnum = dmix / den_full[rows, 0:cv]
        if sz.vp > cv:
            dnum = jnp.concatenate([dnum, jnp.zeros((ck, sz.vp - cv), f32)], axis=1)
        products = dmix * mixed[rows, :].astype(f32)
        sums = lax.dot_general(
            picks,
            products,
            (((1,), (1,)), ((), ())),
            precision=lax.Precision.HIGHEST,
            preferred_element_type=f32,
        )
        dden[j ^ k] = -sums / den_rows[j ^ k]
        query = act[rows, 0:128].astype(f32) * 0.25
        for h in range(heads):
            dnum_h[h, rows, :] = jnp.where(lane_v == h, dnum, 0.0).astype(bf16)
            q_h[h, rows, :] = jnp.where(lane_q == h, query, 0.0).astype(bf16)
    starts = doc_starts(lengths, c)
    dq_t[...] = jnp.zeros_like(dq_t)
    for b in range(total // ck):
        low = b * ck
        width = total - low
        u_rows = slice(low, low + ck)
        u_at = low + lax.broadcasted_iota(jnp.int32, (ck, 1), 0)
        t_row = low + lax.broadcasted_iota(jnp.int32, (1, width), 1)
        first = latest_start(t_row, starts)
        t_at = low + lax.broadcasted_iota(jnp.int32, (ck, width), 1)
        allowed = (u_at <= t_at) & (u_at >= first)
        keys = act[u_rows, 128:256]
        values = act[u_rows, 256:]
        keys_t = keys.astype(f32).T
        dv_here = jnp.zeros((ck, sz.vp), f32)
        dk_here = jnp.zeros((ck, 128), f32)
        for h in range(heads):
            qs = q_h[h, low:, :]
            ds_in = dnum_h[h, low:, :]
            extra = jnp.concatenate(
                [dden[i][h : h + 1] for i in range(b, total // ck)], axis=1
            )
            s = mm_nt(keys, qs)
            dtaylor = mm_nt(values, ds_in) + extra
            slope = 1.0 + s
            taylor = jnp.where(allowed, slope + 0.5 * s * s, 0.0).astype(bf16)
            dscore = jnp.where(allowed, dtaylor * slope, 0.0).astype(bf16)
            dv_here = dv_here + mm(taylor, ds_in)
            dk_here = dk_here + mm(dscore, qs)
            k_t = keys_t[h * FEAT : (h + 1) * FEAT].astype(bf16)
            dq_t[h * FEAT : (h + 1) * FEAT, low:] += mm(k_t, dscore)
        dk[u_rows, :] = dk_here.astype(bf16)
        dv[u_rows, :] = dv_here.astype(bf16)
    dact[:, 0:128] = (dq_t[...] * 0.25).T.astype(bf16)
    dact[:, 128:256] = dk[...]
    dact[:, 256:] = dv[...]
    for k in range(n):
        rows = pl.ds(aligned(j ^ k, ck), ck)
        outs[k][:, 0 : sz.cq] = dact[rows, 0 : sz.cq]
        outs[k][:, sz.cq : 2 * sz.cq] = dact[rows, 128 : 128 + sz.cq]
        outs[k][:, 2 * sz.cq :] = dact[rows, 256 : 256 + cv]


def back_grads_kernel(sz, layout, place, *refs):
    n, ck, cq, cv, co = sz.chips, sz.chunk, sz.cq, sz.cv, sz.co
    half, cols = sz.half, sz.cols
    i = len(layout)
    mixed = refs[:i]
    entry, dact, branch_c, norm2, norm2_more, gains, w = refs[i : i + 7]
    keep, sends = refs[-3 - sz.planes], refs[-2 - sz.planes : -2]
    dact_s, out = refs[-2:]
    j, c = place[0], place[1]
    for k in range(n):
        rows = slice(k * ck, (k + 1) * ck)
        dact_s[rows, :] = dact[pl.ds(aligned(j ^ k, ck), ck), :]
    grads = mm_tn(dact_s[...], entry[...])
    norm1 = jnp.sum(grads * w[...].astype(f32).T, axis=0, keepdims=True)
    grads = grads.astype(bf16)
    norms = jnp.concatenate(
        [norm1 / gains[0:1], norm2[...] + norm2_more[...], jnp.zeros((14, sz.model), f32)], axis=0
    ).astype(bf16)
    for at in range(2 * sz.planes):
        lanes = slice(at * half, (at + 1) * half)
        out[at, 0:cq, :] = grads[0:cq, lanes]
        out[at, cq : 2 * cq, :] = grads[128 : 128 + cq, lanes]
        out[at, 2 * cq : 2 * cq + cv, :] = grads[256 : 256 + cv, lanes]
        out[at, cols:, :] = norms[:, lanes]
    for ref, (m, first, count) in zip(mixed, layout):
        grads = mm_tn(branch_c[...], ref[...]).astype(bf16)
        at = (j ^ m) * (cv // half) + first * cv // (2 * half)
        for i in range(count * cv // (2 * half)):
            out[at + i, 2 * cq + cv : cols, :] = grads[:, i * half : (i + 1) * half]
    for z in range(sz.planes):
        keep[z] = out[2 * z + c]
        sends[z][...] = out[2 * z + 1 - c]


def pair_sum_kernel(sz, place, keep, *refs):
    received, outs, sums = refs[: sz.planes], refs[sz.planes : -1], refs[-1]
    plane = place[2]
    for z in range(sz.planes):
        sums[z] = (keep[z].astype(f32) + received[z][...].astype(f32)).astype(bf16)
    for k in range(sz.planes):
        outs[k][...] = sums[plane ^ k]


def plane_sum_kernel(sz, *refs):
    total = refs[0][...].astype(f32)
    for ref in refs[1 : sz.planes]:
        total = total + ref[...].astype(f32)
    refs[-1][...] = total.astype(bf16)


def split_rows(sz, place, values, keep, send):
    for core in range(2):

        @pl.when(place[1] == core)
        def _():
            for to, side in ((keep, core), (send, 1 - core)):
                to[...] = values[side * sz.block : (side + 1) * sz.block]


def join_kernel(sz, place, *refs):
    for i in range(2):
        keep, received = refs[2 * i : 2 * i + 2]
        out = refs[-2 + i]
        out[place[1]] = keep[...]
        out[1 - place[1]] = received[...]


def finish_block_kernel(sz, place, *refs):
    result = refs[0][...]
    for part in refs[1 : sz.chips + 1]:
        result = result + part[...].astype(f32)
    keep, send = refs[-2], refs[-1]
    split_rows(sz, place, result.astype(bf16), keep, send)


def finish_tokens_kernel(sz, place, *refs):
    n = sz.chips
    dact_in = refs[:n]
    w_qkv, dh1, x, gains, keep, send = refs[n:]
    values = x[...].astype(f32)
    scale = rms(values)
    normed = values * scale
    dn1 = mm_nt(dact_in[0][...], w_qkv[0])
    for k in range(1, n):
        dn1 = dn1 + mm_nt(dact_in[k][...], w_qkv[k])
    weighted = dn1 * gains[0:1]
    result = dh1[...] + scale * (
        weighted - normed * jnp.mean(weighted * normed, axis=-1, keepdims=True)
    )
    split_rows(sz, place, result, keep, send)


def gathered(sz, layout, place, refs, to):
    n = len(layout)
    j, c = place[0], place[1]
    rows = to.shape[2]
    for some, side in ((refs[:n], c), (refs[n : 2 * n], 1 - c)):
        for ref, (k, first, count) in zip(some, layout):
            at, size = first * rows // 2, count * rows // 2
            to[j ^ k, side, at : at + size] = ref[...]


def finish_attention_kernel(sz, layout, place, *refs):
    n, shard, cq, cv, co = sz.chips, sz.shard, sz.cq, sz.cv, sz.co
    query, key, value, output, norms, all_c = refs[2 * len(layout) :]
    gathered(sz, layout, place, refs, all_c)
    total = jnp.zeros((16, shard), f32)
    for q in range(n):
        part = jnp.concatenate([all_c[q, 0], all_c[q, 1]], axis=1).astype(f32)
        query[:, q * cq : (q + 1) * cq] = part[0:cq].T
        key[:, q * cq : (q + 1) * cq] = part[cq : 2 * cq].T
        value[:, q * cv : (q + 1) * cv] = part[2 * cq : 2 * cq + cv].T
        output[:, q * co : (q + 1) * co] = part[2 * cq + cv : sz.cols].T
        total = total + part[sz.cols :]
    norms[...] = total[0:8]


def finish_mlp_kernel(sz, layout, place, *refs):
    half, ffc = sz.half, sz.ffc
    *outs, all_c = refs[2 * len(layout) :]
    gathered(sz, layout, place, refs, all_c)
    for q in range(sz.chips):
        at = q * ffc
        count = max(0, min(ffc, sz.hidden - at))
        for i, out in enumerate(outs):
            for side in range(2):
                if count:
                    out[at : at + count, side * half : (side + 1) * half] = all_c[
                        q, side, i * ffc : i * ffc + count, :
                    ].astype(f32)


def kernel(body, name, outs, scratch=(), smem=0, room=60, in_specs=None, out_specs=None, **more):
    shapes = [jax.ShapeDtypeStruct(shape, dtype) for shape, dtype in outs]
    scratch = [VMEM(shape, dtype) for shape, dtype in scratch] + list(more.pop("semaphores", ()))

    def run(*args, after=(), carry=()):
        n_in, n_out = len(args), len(shapes)
        loose = len(after) + len(carry)

        def trimmed(*refs):
            first = n_in + loose
            body(*refs[:n_in], *refs[first : first + n_out], *refs[first + n_out + len(carry) :])

        takes = in_specs or [scalars()] * smem + [whole()] * (n_in - smem)
        gives = out_specs or [whole()] * n_out
        return pl.pallas_call(
            trimmed,
            name=name,
            out_shape=shapes + [jax.ShapeDtypeStruct(a.shape, a.dtype) for a in carry],
            in_specs=takes + [anywhere()] * loose,
            out_specs=gives + [anywhere()] * len(carry),
            scratch_shapes=scratch,
            input_output_aliases={n_in + len(after) + i: n_out + i for i in range(len(carry))},
            compiler_params=pltpu.CompilerParams(vmem_limit_bytes=room * MIB),
            cost_estimate=pl.CostEstimate(
                flops=int(COST[name] * 1.15e9), bytes_accessed=0, transcendentals=0
            ),
            **more,
        )(*args, *after, *carry)

    return run


def shards(
    n_chip,
    n_dp,
    tokens,
    cotangent,
    doc_lengths,
    norm1_gain,
    w_query,
    w_key,
    w_value,
    w_output,
    norm2_gain,
    w_gate,
    w_up,
    w_down,
):
    rows_here, block, model = tokens.shape
    hidden = w_gate.shape[1]
    sz = Sizes(n_dp, n_chip, block, w_query.shape[0], model, hidden)
    n, ck, cq, cv, co, ffc = sz.chips, sz.chunk, sz.cq, sz.cv, sz.co, sz.ffc
    half, shard, total = sz.half, sz.shard, sz.tokens
    tight = lambda mib: mib if n == 4 else 60
    chip, core = lax.axis_index("chip"), lax.axis_index("core")
    place = jnp.stack([chip, core, lax.axis_index("dp")]).astype(jnp.int32)

    def swap(a):
        return lax.ppermute(a, "core", [(0, 1), (1, 0)])

    def to_chip(a, k):
        return lax.ppermute(a, "chip", [(i, i ^ k) for i in range(n)])

    def to_plane(a, k):
        return lax.ppermute(a, "dp", [(i, i ^ k) for i in range(n_dp)])

    def spread(a, name, axis=0):
        if n != 4 or not TWICE[name]:
            return [a] + [to_chip(a, k) for k in range(1, n)], sz.direct
        first, second = to_chip(a, 1), to_chip(a, 2)
        middle = a.shape[axis] // 2
        low = to_chip(lax.slice_in_dim(second, 0, middle, axis=axis), 1)
        high = to_chip(lax.slice_in_dim(first, middle, 2 * middle, axis=axis), 2)
        return [a, first, second, low, high], sz.pieces

    def exchange(parts):
        return [parts[0]] + [to_chip(parts[k], k) for k in range(1, n)]

    def to_rows(a):
        return lax.all_to_all(a, "core", 0, 0).reshape(ck, model)

    def when(name, *arrays):
        return list(arrays) if TIES[name] else []

    with jax.named_scope("gather_tokens"):
        xs, lay_x = spread(to_rows(tokens), "x")

    with jax.named_scope("pack_small"):
        (small,) = kernel(
            partial(pack_small_kernel, sz), "pack_small", [((half + 16, sz.wa), bf16)], smem=1
        )(
            place,
            w_query,
            w_key,
            w_value,
            w_output,
            norm1_gain,
            norm2_gain,
            after=when("small_x", xs[0]),
        )
        small_own = [small] + [to_plane(small, k) for k in range(1, n_dp)]
        small_oth = [swap(a) for a in small_own]

    with jax.named_scope("pack_large"):
        loads = anywhere() if half % 128 == 0 else whole()
        (large,) = kernel(
            partial(pack_large_kernel, sz),
            "pack_large",
            [((3 * ffc, half), bf16)],
            in_specs=[scalars()] + [loads] * 3,
            semaphores=[pltpu.SemaphoreType.DMA((3,))],
        )(place, w_gate.T, w_up.T, w_down)
        g_here = to_rows(cotangent)
        (large,) = kernel(lambda *refs: None, "after_small", [])(
            after=small_own[1:]
            + when("large_x", *xs[1:3])
            + when("large_x3", *xs[3:])
            + when("large_g", g_here),
            carry=[large],
        )
        large_all = lax.all_gather(large, ("dp", "core"))

    with jax.named_scope("gather_cotangent"):
        if TIES["g_take"]:
            (g_here,) = kernel(lambda *refs: None, "g_take", [])(after=small_own[1:] + xs[1:3], carry=[g_here])
        gs, lay_g = spread(g_here, "g")

    with jax.named_scope("project"):
        act, w_act, entry_one, gains = kernel(
            partial(project_kernel, sz, lay_x),
            "project",
            [
                ((total, sz.qw), bf16),
                ((model, sz.qw), bf16),
                ((total, model), bf16),
                ((2, model), f32),
            ],
            [((n_dp, 2, shard), f32)],
            smem=1,
        )(place, *xs, *small_own, *small_oth, after=when("project_g", *gs[1:3]))

    with jax.named_scope("take"):
        wo_half, qkv_half = kernel(
            partial(take_output_kernel, sz),
            "take_output",
            [((n_dp, half, co), bf16), ((n_dp, half, sz.qkv), bf16)],
        )(*small_own, after=when("take_oth", *small_oth) + when("take_x", *xs[1:]))
        wo_parts, lay_wo = spread(wo_half, "wo")

    with jax.named_scope("attention"):
        mixed_own, den_full, den_rows = kernel(
            partial(attend_kernel, sz),
            "attend",
            [
                ((total, cv), bf16),
                ((total, sz.vp), f32),
                ((total // ck, 8, ck), f32),
            ],
            smem=2,
            room=tight(20),
        )(place, doc_lengths, act, after=when("attend_wo", wo_parts[1])
            + when("attend_g", *gs[1:3])
            + when("attend_g1", gs[1]),
        )
        mixed, lay_o = spread(mixed_own, "o", 1)

    with jax.named_scope("output_weight"):
        wo_own, *carried = kernel(
            partial(output_weight_kernel, sz, lay_wo),
            "output_weight",
            [((n_dp, half, model), bf16)],
            [((n, n_dp, half, co), bf16)],
            smem=1,
            room=tight(20),
        )(
            place,
            *wo_parts,
            after=when("ow_mixed", *mixed[1:3])
            + when("ow_own", mixed_own)
            + when("ow_g", *gs[1:3]),
            carry=when("qkv_ow", qkv_half),
        )
        qkv_half = carried[0] if carried else qkv_half
        wo_oth = swap(wo_own)

    with jax.named_scope("before_mlp"):
        if TIES["qkv_tie"]:
            (qkv_half,) = kernel(lambda *refs: None, "before_mlp", [])(
                after=[*mixed[1:], *gs[1:], wo_oth], carry=[qkv_half]
            )

    with jax.named_scope("mlp"):
        group = 2 if n == 4 else 1
        size = group * ck
        part = total // 2

        def mlp(ks, name, after):
            some_x, some_g = picked(lay_x, ks), picked(lay_g, ks)
            count, loads = len(ks), len(some_x) + len(some_g) + len(mixed) + 3
            results = kernel(
                partial(mlp_kernel, sz, ks, group, (lay_x, lay_g, lay_o)),
                name,
                [((ck, model), bf16)] * count
                + [
                    ((part, model), bf16),
                    ((part, sz.ffp), bf16),
                    ((part, sz.ffp), bf16),
                    ((part, sz.ffp), bf16),
                    ((1, model), f32),
                    ((model, model), bf16),
                    ((ck, model), f32),
                ],
                [
                    ((size, model), bf16),
                    ((size, model), bf16),
                    ((n, size, cv), bf16),
                    ((model, model), bf16),
                    ((sz.ffp, model), bf16),
                    ((sz.ffp, model), bf16),
                    ((sz.ffp, model), bf16),
                    ((size, model), bf16),
                    ((size, sz.ffp), bf16),
                    ((size, sz.ffp), bf16),
                    ((size, sz.ffp), bf16),
                    ((size, model), bf16),
                    ((ck, model), f32),
                ]
                + stages(sz, 3),
                semaphores=[
                    pltpu.SemaphoreType.DMA((6,)),
                    pltpu.SemaphoreType.DMA((6 + group,)),
                ],
                in_specs=[scalars()] + [anywhere()] * loads + [whole()],
                out_specs=[anywhere()] * (count + 4) + [whole()] + [anywhere()] * 2,
                grid=(count // group,),
            )(
                place,
                *[xs[i] for i in some_x],
                *[gs[i] for i in some_g],
                *mixed,
                wo_own,
                wo_oth,
                large_all,
                gains,
                after=after,
            )
            return dict(zip(ks, results[:count])), results[count:]

        far_parts, far = mlp(sz.far, "mlp_far", when("qkv_tie", qkv_half))
        far_in = {k: to_chip(a, k) for k, a in far_parts.items()}
        near_parts, near = mlp(sz.near, "mlp_near", when("near_far", far[4]))
        near_in = {k: to_chip(a, k) for k, a in near_parts.items() if k}
        dn2_in = [near_parts[0]] + [{**far_in, **near_in}[k] for k in range(1, n)]
        wo, middle = near[5], near[6]

    with jax.named_scope("gather_qkv"):
        qkv_own, lay_q = spread(qkv_half, "qkv")

    with jax.named_scope("mlp_grads"):
        mlp_grads, *carried = kernel(
            partial(mlp_grads_kernel, sz, lay_g),
            "mlp_grads",
            [((2 * n_dp, 3 * ffc, half), bf16)],
            [((part, model), bf16)] * 2,
        )(
            *gs,
            *[a for pair in zip(far[:4], near[:4]) for a in pair],
            after=when("grads_far", *far_in.values()),
            carry=when("grads_qkv", *qkv_own),
        )
        qkv_own = carried or qkv_own
        qkv_oth = [swap(a) for a in qkv_own]
        mlp_shard = lax.psum_scatter(mlp_grads, ("dp", "core"), scatter_dimension=0)

    with jax.named_scope("middle"):
        results = kernel(
            partial(middle_kernel, sz),
            "middle",
            [((ck, cv + co), bf16)] * n + [((ck, model), f32)],
            [((n, ck, cv + co), bf16)],
            smem=1,
        )(
            place,
            *dn2_in,
            middle,
            gs[0],
            wo,
            gains,
            after=when("middle_grads", mlp_grads) + when("middle_qkv", *qkv_own[1:]),
        )
        dh1 = results[n]
        pays = exchange(results[:n])

    with jax.named_scope("gather_qkv"):
        (w_qkv,) = kernel(
            partial(gather_qkv_kernel, sz, lay_q),
            "gather_qkv",
            [((n, model, sz.qkv), bf16)],
            smem=1,
            room=tight(20),
        )(place, *qkv_own, *qkv_oth, after=when("gq_middle", dh1))

    with jax.named_scope("down"):
        down_parts = kernel(
            partial(down_kernel, sz),
            "down",
            [((ck, model), bf16)] * n,
            [((sz.ffp, model), bf16)] + stages(sz, 1),
            room=tight(20),
            in_specs=[whole()] * 2 + [anywhere()],
            semaphores=[pltpu.SemaphoreType.DMA],
        )(far[3], near[3], large_all, after=when("down_middle", dh1) + when("down_gq", w_qkv))
        down_in = exchange(down_parts)

    with jax.named_scope("attention_back"):
        results = kernel(
            partial(back_kernel, sz),
            "attention_back",
            [((ck, sz.qkv), bf16)] * n + [((total, sz.qw), bf16), ((total, co), bf16)],
            [
                ((sz.heads, total, sz.vp), bf16),
                ((sz.heads, total, 128), bf16),
                ((total // ck, 8, ck), f32),
                ((128, total), f32),
                ((total, 128), bf16),
                ((total, sz.vp), bf16),
            ],
            smem=2,
            room=tight(44),
        )(
            place,
            doc_lengths,
            *pays,
            act,
            mixed_own,
            den_full,
            den_rows,
            after=when("back_down", down_parts[0]) + when("back_gq", w_qkv),
        )
        dact, branch_c = results[n], results[n + 1]
        dact_in = exchange(results[:n])

    with jax.named_scope("attention_grads"):
        width = sz.cols + 16
        keep, *sends = kernel(
            partial(back_grads_kernel, sz, lay_o),
            "attention_grads",
            [((n_dp, width, half), bf16)] + [((width, half), bf16)] * n_dp,
            [((total, sz.qw), bf16), ((2 * n_dp, width, half), bf16)],
            smem=1,
            room=tight(28),
        )(
            place,
            *mixed,
            entry_one,
            dact,
            branch_c,
            far[4],
            near[4],
            gains,
            w_act,
            after=when("ag_down", *down_in[1:]),
        )

    with jax.named_scope("finish_block"):
        block_keep, block_send = kernel(
            partial(finish_block_kernel, sz), "finish_block", [((block, model), bf16)] * 2, smem=1
        )(place, middle, *down_in)
        block_other = swap(block_send)

    with jax.named_scope("finish_tokens"):
        grad_keep, grad_send = kernel(
            partial(finish_tokens_kernel, sz), "finish_tokens", [((block, model), f32)] * 2, smem=1
        )(place, *dact_in, w_qkv, dh1, xs[0], gains)
        grad_other = swap(grad_send)

    with jax.named_scope("sum_gradients"):
        *parts, mlp_shard = kernel(
            partial(pair_sum_kernel, sz),
            "pair_sum",
            [((width, half), bf16)] * n_dp,
            [((n_dp, width, half), bf16)],
            smem=1,
            room=tight(20),
        )(
            place,
            keep,
            *[swap(a) for a in sends],
            after=when("pair_tokens", grad_keep) + when("pair_block", block_keep),
            carry=[mlp_shard],
        )
        sums = [parts[0]] + [to_plane(parts[k], k) for k in range(1, n_dp)]

    with jax.named_scope("spread_gradients"):
        att_shard, *carried = kernel(
            partial(plane_sum_kernel, sz), "plane_sum", [((width, half), bf16)], room=tight(20)
        )(
            *sums,
            after=when("plane_tokens", grad_keep) + when("plane_block", block_keep),
            carry=when("mlp_plane", mlp_shard),
        )
        mlp_shard = carried[0] if carried else mlp_shard
        mlp_own, lay_m = spread(mlp_shard, "mlp")
        mlp_oth = [swap(a) for a in mlp_own]
        att_own, lay_a = spread(att_shard, "att")
        att_oth = [swap(a) for a in att_own]

    with jax.named_scope("join"):
        block_out, grad_tokens = kernel(
            partial(join_kernel, sz),
            "join",
            [((2, block, model), bf16), ((2, block, model), f32)],
            smem=1,
        )(place, block_keep, block_other, grad_keep, grad_other)

    with jax.named_scope("finish_attention"):
        total_query, total_key, total_value, total_output, norms = kernel(
            partial(finish_attention_kernel, sz, lay_a),
            "finish_attention",
            [
                ((shard, n * cq), f32),
                ((shard, n * cq), f32),
                ((shard, n * cv), f32),
                ((shard, n * co), f32),
                ((8, shard), f32),
            ],
            [((n, 2, width, half), bf16)],
            smem=1,
            room=tight(20),
        )(place, *att_own, *att_oth, after=when("fa_tokens", grad_keep))

    with jax.named_scope("finish_mlp"):
        total_gate, total_up, total_down = kernel(
            partial(finish_mlp_kernel, sz, lay_m),
            "finish_mlp",
            [((hidden, shard), f32)] * 3,
            [((n, 2, 3 * ffc, half), bf16)],
            smem=1,
            room=tight(24),
        )(place, *mlp_own, *mlp_oth, after=when("fm_norms", norms) + when("fm_join", block_out))

    return (
        block_out,
        grad_tokens,
        norms[0],
        total_query,
        total_key,
        total_value,
        total_output,
        norms[1],
        total_gate.T,
        total_up.T,
        total_down,
    )


def solution(mesh):
    n_dp, n_seq = mesh.shape["dp"], mesh.shape["seq"]
    n_chip = n_seq // 2
    grid = Mesh(mesh.devices.reshape(n_dp, n_chip, 2), ("dp", "chip", "core"))
    seq = ("chip", "core")
    placed = (
        P("dp", seq, None),
        P("dp", seq, None),
        P("dp", None),
        P("dp"),
        P("dp", None),
        P("dp", None),
        P("dp", None),
        P("dp", None),
        P("dp"),
        P("dp", None),
        P("dp", None),
        P(None, "dp"),
    )
    return jax.shard_map(
        partial(shards, n_chip, n_dp),
        mesh=grid,
        in_specs=placed,
        out_specs=(
            P("dp", seq, None),
            P("dp", seq, None),
            P("dp"),
            P("dp", None),
            P("dp", None),
            P("dp", None),
            P("dp", None),
            P("dp"),
            P("dp", None),
            P("dp", None),
            P(None, "dp"),
        ),
        check_vma=False,
    )
```

```python
import math
from functools import partial

import jax
import jax.numpy as jnp
from jax import lax
from jax.experimental import pallas as pl
from jax.experimental.pallas import tpu as pltpu
from jax.sharding import Mesh
from jax.sharding import PartitionSpec as P

HEADS = 16
FEAT = 16
VDIM = 64
EPSILON = 1e-05

bf16 = jnp.bfloat16
f32 = jnp.float32
VMEM = pltpu.VMEM
SMEM = pltpu.SMEM
MIB = 1024 * 1024

COST = dict(
    g_take=0.1,
    pack_small=0.5,
    pack_large=100.0,
    after_small=0.5,
    project=100.0,
    take_output=7.0,
    attend=4.0,
    output_weight=0.5,
    before_mlp=0.1,
    mlp_far=100.0,
    mlp_near=35.0,
    mlp_grads=2.0,
    middle=30.0,
    gather_qkv=1.0,
    down=0.1,
    attention_back=60.0,
    attention_grads=0.1,
    pair_sum=35.0,
    finish_block=0.5,
    finish_tokens=0.5,
    plane_sum=2.0,
    join=2.0,
    finish_attention=0.1,
    finish_mlp=35.0,
)
TWICE = dict(
    x=0,
    g=1,
    wo=1,
    o=1,
    qkv=0,
    att=0,
    mlp=1,
)
TIES = dict(
    small_x=0,
    large_x=1,
    large_x3=0,
    large_g=0,
    project_g=0,
    attend_g=0,
    attend_g1=0,
    g_take=1,
    take_oth=0,
    take_x=0,
    attend_wo=0,
    ow_mixed=1,
    ow_own=0,
    ow_g=1,
    qkv_ow=0,
    qkv_tie=1,
    near_far=0,
    grads_qkv=1,
    grads_far=0,
    middle_grads=1,
    middle_qkv=0,
    gq_middle=1,
    down_middle=1,
    down_gq=0,
    back_down=1,
    back_gq=1,
    ag_down=1,
    pair_tokens=1,
    pair_block=0,
    plane_tokens=0,
    plane_block=0,
    mlp_plane=0,
    fa_tokens=1,
    fm_norms=0,
    fm_join=0,
)


def mm(left, right):
    return jnp.dot(left, right, preferred_element_type=f32)


def mm_nt(left, right):
    return lax.dot_general(left, right, (((1,), (1,)), ((), ())), preferred_element_type=f32)


def mm_tn(left, right):
    return lax.dot_general(left, right, (((0,), (0,)), ((), ())), preferred_element_type=f32)


def up_to(value, step):
    return -(-value // step) * step


def whole():
    return pl.BlockSpec(memory_space=VMEM, pipeline_mode=pl.Buffered(1))


def anywhere():
    return pl.BlockSpec(memory_space=pl.ANY)


def scalars():
    return pl.BlockSpec(memory_space=SMEM)


def rms(values):
    return lax.rsqrt(jnp.mean(values * values, axis=-1, keepdims=True) + EPSILON)


def shard_row(pieces, row):
    return jnp.concatenate([pieces[z] for z in range(pieces.shape[0])], axis=1)[row : row + 1]


def doc_starts(lengths, row):
    starts, total = [], jnp.int32(0)
    for i in range(lengths.shape[1]):
        starts.append(total)
        total = total + lengths[row, i]
    return starts


def latest_start(position, starts):
    latest = jnp.zeros_like(position)
    for start in starts:
        latest = jnp.where(position >= start, start, latest)
    return latest


class Sizes:
    def __init__(self, planes, chips, block, shard, model, hidden):
        self.planes, self.chips, self.block = planes, chips, block
        self.chunk = 2 * block
        self.tokens = chips * self.chunk
        self.shard, self.half, self.model = shard, shard // 2, model
        self.heads = HEADS // chips
        self.cq = self.heads * FEAT
        self.cv = self.heads * VDIM
        self.co = model // chips
        self.vp = up_to(self.cv, 128)
        self.qw = 256 + self.vp
        self.wa = max(512, 2 * self.cq + self.cv + self.co)
        self.hidden = hidden
        self.ffc = up_to(-(-hidden // chips), 16)
        self.ffp = up_to(self.ffc, 128)
        self.cols = 2 * self.cq + self.cv + self.co
        self.qkv = 2 * self.cq + self.cv
        self.pieces = self.direct = [(k, 0, 2) for k in range(chips)]
        self.far, self.near = range(chips - 1, chips // 2 - 1, -1), range(chips // 2 - 1, -1, -1)
        if chips == 4:
            self.pieces = [(0, 0, 2), (1, 0, 2), (2, 0, 2), (3, 0, 1), (3, 1, 1)]


def aligned(index, step):
    return pl.multiple_of(index * step, step)


def pack_large_kernel(sz, place, *refs):
    weights, out, sem = refs[:3], refs[-2], refs[-1]
    half, ffc = sz.half, sz.ffc
    j, c = place[0], place[1]
    for chip in range(sz.chips):
        first = chip * ffc
        count = max(0, min(ffc, sz.hidden - first))
        for core in range(2):

            @pl.when((j == chip) & (c == core))
            def _():
                lanes = slice(core * half, (core + 1) * half)
                copies = []
                for i, weight in enumerate(weights):
                    if count == 0:
                        continue
                    if half % 128:
                        out[i * ffc : i * ffc + count, :] = weight[first : first + count, lanes]
                        continue
                    copies.append(
                        pltpu.make_async_copy(
                            weight.at[pl.ds(first, count), pl.ds(core * half, half)],
                            out.at[pl.ds(i * ffc, count)],
                            sem.at[i],
                        )
                    )
                for copy in copies:
                    copy.start()
                for i in range(3):
                    if count < ffc:
                        out[i * ffc + count : (i + 1) * ffc, :] = jnp.zeros(
                            (ffc - count, half), bf16
                        )
                for copy in copies:
                    copy.wait()


def pack_small_kernel(sz, place, w_query, w_key, w_value, w_output, gain_one, gain_two, out):
    half, cq, cv, co = sz.half, sz.cq, sz.cv, sz.co
    j, c = place[0], place[1]
    side = pl.ds(aligned(c, half), half)
    out[...] = jnp.zeros_like(out)
    for chip in range(sz.chips):

        @pl.when(j == chip)
        def _():
            out[0:half, 0:cq] = w_query[side, chip * cq : (chip + 1) * cq]
            out[0:half, cq : 2 * cq] = w_key[side, chip * cq : (chip + 1) * cq]
            out[0:half, 2 * cq : 2 * cq + cv] = w_value[side, chip * cv : (chip + 1) * cv]
            out[0:half, 2 * cq + cv : sz.cols] = w_output[side, chip * co : (chip + 1) * co]

    for i, gain in enumerate((gain_one, gain_two)):
        row = gain[...].reshape(1, sz.shard)
        out[half : half + 16, i * 256 : i * 256 + sz.shard] = jnp.broadcast_to(row, (16, sz.shard))


def project_kernel(sz, layout, place, *refs):
    n, p = len(layout), sz.planes
    xs, own, oth = refs[:n], refs[n : n + p], refs[n + p : n + 2 * p]
    act, w, entry, gains, gain_c = refs[n + 2 * p :]
    j, c, plane = place[0], place[1], place[2]
    half, shard, cq, cv, ck = sz.half, sz.shard, sz.cq, sz.cv, sz.chunk
    w[...] = jnp.zeros_like(w)
    for k in range(p):
        z = plane ^ k
        for piece, side in ((own[k], c), (oth[k], 1 - c)):
            rows = pl.ds(pl.multiple_of(z * shard + side * half, half), half)
            w[rows, 0:cq] = piece[0:half, 0:cq]
            w[rows, 128 : 128 + cq] = piece[0:half, cq : 2 * cq]
            w[rows, 256 : 256 + cv] = piece[0:half, 2 * cq : 2 * cq + cv]
        for i in range(2):
            row = own[k][half : half + 16, i * 256 : i * 256 + shard]
            gain_c[z, i : i + 1] = row[0:1].astype(f32)
    for i in range(2):
        gains[i : i + 1] = shard_row(gain_c, i)
    gain = gains[0:1]
    for ref, (k, first, count) in zip(xs, layout):
        x = ref[...].astype(f32)
        at = k * ck + first * ck // 2
        entry[at : at + count * ck // 2, :] = ((x * rms(x)) * gain).astype(bf16)
    for k in range(sz.chips):
        rows = pl.ds(aligned(j ^ k, ck), ck)
        act[rows, :] = mm(entry[k * ck : (k + 1) * ck, :], w[...]).astype(bf16)


def attend_kernel(sz, place, lengths, act, mixed, den_full, den_rows):
    c, ck, cv = place[1], sz.chunk, sz.cv
    starts = doc_starts(lengths, c)
    lane_q = lax.broadcasted_iota(jnp.int32, (ck, 128), 1) // FEAT
    lane_v = lax.broadcasted_iota(jnp.int32, (ck, sz.vp), 1) // VDIM
    lane = lax.broadcasted_iota(jnp.int32, (ck, 128), 1)
    for b in range(sz.tokens // ck):
        rows = slice(b * ck, (b + 1) * ck)
        width = (b + 1) * ck
        t_at = b * ck + lax.broadcasted_iota(jnp.int32, (ck, 1), 0)
        first = latest_start(t_at, starts)
        u_at = lax.broadcasted_iota(jnp.int32, (ck, width), 1)
        allowed = (u_at <= t_at) & (u_at >= first)
        query = act[rows, 0:128]
        keys = act[0:width, 128:256]
        values = act[0:width, 256:]
        att = jnp.zeros((ck, sz.vp), f32)
        den_wide = jnp.ones((ck, sz.vp), f32)
        den_some = jnp.ones((ck, 128), f32)
        for h in range(sz.heads):
            mine = jnp.where(lane_q == h, query.astype(f32) * 0.25, 0.0).astype(bf16)
            s = mm_nt(mine, keys)
            taylor = jnp.where(allowed, 1.0 + s + 0.5 * s * s, 0.0).astype(bf16)
            den = jnp.sum(taylor.astype(f32), axis=1, keepdims=True)
            num = mm(taylor, values)
            att = jnp.where(lane_v == h, num / den, att)
            den_wide = jnp.where(lane_v == h, den, den_wide)
            den_some = jnp.where(lane == h, den, den_some)
        mixed[rows, :] = att.astype(bf16)[:, 0:cv]
        den_full[rows, :] = den_wide
        den_rows[b] = den_some.T[0:8]


def take_output_kernel(sz, *refs):
    for k in range(sz.planes):
        refs[-2][k] = refs[k][0 : sz.half, sz.qkv : sz.cols]
        refs[-1][k] = refs[k][0 : sz.half, 0 : sz.qkv]


def gather_qkv_kernel(sz, layout, place, *refs):
    n, half, planes = len(layout), sz.half, sz.planes
    out = refs[-1]
    c, plane = place[1], place[2]
    for pieces, side in ((refs[:n], c), (refs[n : 2 * n], 1 - c)):
        for ref, (k, first, count) in zip(pieces, layout):
            for i in range(count * planes // 2):
                z = plane ^ (first * planes // 2 + i)
                at = pl.multiple_of(z * sz.shard + side * half, half)
                out[k, pl.ds(at, half), :] = ref[i]


def output_weight_kernel(sz, layout, place, *refs):
    planes = sz.planes
    *pieces, out, out_c = refs
    j, plane = place[0], place[2]
    for ref, (k, first, count) in zip(pieces, layout):
        out_c[j ^ k, first * planes // 2 : (first + count) * planes // 2] = ref[...]
    for z in range(planes):
        out[plane ^ z] = jnp.concatenate([out_c[q, z] for q in range(sz.chips)], axis=1)


def fetch_weight(sz, large, which, to, stage, sem):
    half, ffc = sz.half, sz.ffc
    rows = pl.ds(which * ffc, ffc)
    if half % 128:
        return [pltpu.make_async_copy(large.at[:, rows], stage, sem)]
    return [
        pltpu.make_async_copy(
            large.at[at, rows], to.at[pl.ds(0, ffc), pl.ds(at * half, half)], sem
        )
        for at in range(2 * sz.planes)
    ]


def settle_weight(sz, to, stage):
    ffc, half = sz.ffc, sz.half
    if half % 128:
        for at in range(2 * sz.planes):
            to[0:ffc, at * half : (at + 1) * half] = stage[at]
    if sz.ffp > ffc:
        to[ffc:, :] = jnp.zeros((sz.ffp - ffc, sz.model), bf16)


def stages(sz, count):
    if sz.half % 128:
        return [((2 * sz.planes, sz.ffc, sz.half), bf16)] * count
    return [((8, 128), bf16)] * count


def picked(layout, ks):
    return [i for i, (k, _, _) in enumerate(layout) if k in ks]


def mlp_kernel(sz, ks, group, layouts, place, *refs):
    n, ck, cv, half, shard, ffc = sz.chips, sz.chunk, sz.cv, sz.half, sz.shard, sz.ffc
    lay_x, lay_g, lay_o = layouts
    some_x, some_g = picked(lay_x, ks), picked(lay_g, ks)
    i, total = len(some_x), len(some_x) + len(some_g)
    xs, gs, mixed = refs[:i], refs[i:total], refs[total : total + len(lay_o)]
    total = total + len(lay_o)
    wo_own, wo_oth, large, gains = refs[total : total + 4]
    outs = refs[total + 4 :]
    dn2_out = outs[: len(ks)]
    n2_out, dgate_out, dup_out, hid_out, norm_out, wo_out, mid_out = outs[len(ks) : len(ks) + 7]
    scratch = outs[len(ks) + 7 :]
    x_s, g_s, o_c, wo, wg, wu, wd, n2_s, dgate_s, dup_s, hid_s, dn2_s, mid_s = scratch[:13]
    stage, sem, out_sem = scratch[13:16], scratch[16], scratch[17]
    j, c = place[0], place[1]
    step = pl.program_id(0)
    size = group * ck
    steps = len(ks) // group

    def inputs(at, which):
        here = list(ks)[at * group : (at + 1) * group]
        found = []
        to = g_s if which else x_s
        layout, some = (lay_g, some_g) if which else (lay_x, some_x)
        for source, index in zip(gs if which else xs, some):
            k, low, count = layout[index]
            if k in here:
                rows = pl.ds(here.index(k) * ck + low * ck // 2, count * ck // 2)
                found.append(pltpu.make_async_copy(source, to.at[rows], sem.at[which]))
        if which:
            return found
        for slot, k in enumerate(here):
            rows = pl.ds(slot * ck, ck)
            for ref, (m, low, count) in zip(mixed, lay_o):
                lanes = pl.ds(low * cv // 2, count * cv // 2)
                source = ref.at[pl.ds(aligned(j ^ k, ck), ck)]
                found.append(pltpu.make_async_copy(source, o_c.at[j ^ m, rows, lanes], sem.at[0]))
        return found

    wo_copies = []
    for z in range(sz.planes):
        for piece, side in ((wo_own, c), (wo_oth, 1 - c)):
            rows = pl.ds(pl.multiple_of(z * shard + side * half, half), half)
            wo_copies.append(pltpu.make_async_copy(piece.at[z], wo.at[rows], sem.at[2]))
    weight_copies = [
        fetch_weight(sz, large, i, to, stage[i], sem.at[3 + i])
        for i, to in enumerate((wg, wu, wd))
    ]

    def fresh(act):
        if steps == 1:
            act()
        else:
            pl.when(step == 0)(act)

    for at in range(steps):

        @pl.when(step == at)
        def _():
            for copy in inputs(at, 0):
                copy.start()

    @fresh
    def _():
        norm_out[...] = jnp.zeros_like(norm_out)
        for copy in wo_copies + weight_copies[0] + weight_copies[1]:
            copy.start()

    for at in range(steps):

        @pl.when(step == at)
        def _():
            for copy in inputs(at, 1):
                copy.start()

    @fresh
    def _():
        for copy in weight_copies[2]:
            copy.start()

    for at in range(steps):

        @pl.when(step == at)
        def _():
            for copy in inputs(at, 0):
                copy.wait()

    @fresh
    def _():
        for copy in wo_copies:
            copy.wait()

    mix = jnp.concatenate([o_c[q] for q in range(n)], axis=1)
    middle = x_s[...].astype(f32) + mm(mix, wo[...])
    normed = middle * rms(middle)
    entry = (normed * gains[1:2]).astype(bf16)
    n2_s[...] = entry
    mid_s[...] = middle[size - ck :]

    @fresh
    def _():
        for which in range(2):
            for copy in weight_copies[which]:
                copy.wait()
            settle_weight(sz, (wg, wu)[which], stage[which])

    gate = mm_nt(entry, wg[...])
    upward = mm_nt(entry, wu[...])

    for at in range(steps):

        @pl.when(step == at)
        def _():
            for copy in inputs(at, 1):
                copy.wait()

    @fresh
    def _():
        for copy in weight_copies[2]:
            copy.wait()
        settle_weight(sz, wd, stage[2])

    grad_hidden = mm_nt(g_s[...], wd[...])
    sig = jax.nn.sigmoid(gate)
    silu = gate * sig
    dgate = (grad_hidden * upward * (sig * (1.0 + gate * (1.0 - sig)))).astype(bf16)
    dup = (grad_hidden * silu).astype(bf16)
    dgate_s[...] = dgate
    dup_s[...] = dup
    hid_s[...] = (silu * upward).astype(bf16)
    rows = pl.ds(aligned(step, size), size)
    saves = [
        pltpu.make_async_copy(source, to.at[rows], out_sem.at[index])
        for index, (source, to) in enumerate(
            ((n2_s, n2_out), (dgate_s, dgate_out), (dup_s, dup_out), (hid_s, hid_out))
        )
    ]
    saves.append(pltpu.make_async_copy(mid_s, mid_out, out_sem.at[4]))
    saves.append(pltpu.make_async_copy(wo, wo_out, out_sem.at[5]))
    for copy in saves:
        copy.start()
    dn2 = mm(dgate, wg[...]) + mm(dup, wu[...])
    dn2_s[...] = dn2.astype(bf16)
    for at in range(steps):

        @pl.when(step == at)
        def _():
            parts = [
                pltpu.make_async_copy(
                    dn2_s.at[pl.ds(slot * ck, ck)],
                    dn2_out[at * group + slot],
                    out_sem.at[6 + slot],
                )
                for slot in range(group)
            ]
            for copy in parts:
                copy.start()
            norm_out[...] += jnp.sum(dn2 * normed, axis=0, keepdims=True)
            for copy in parts:
                copy.wait()

    for copy in saves:
        copy.wait()


def down_kernel(sz, *refs):
    hids, large = refs[:2], refs[2]
    n, ck = sz.chips, sz.chunk
    outs = refs[-n - 3 : -3]
    wd, stage, sem = refs[-3:]
    copies = fetch_weight(sz, large, 2, wd, stage, sem)
    for copy in copies:
        copy.start()
    for copy in copies:
        copy.wait()
    settle_weight(sz, wd, stage)
    for hid, ks in zip(hids, (sz.far, sz.near)):
        for slot, k in enumerate(ks):
            outs[k][...] = mm(hid[slot * ck : (slot + 1) * ck, :], wd[...]).astype(bf16)


def mlp_grads_kernel(sz, layout, *refs):
    n, ck, ffc, half = len(layout), sz.chunk, sz.ffc, sz.half
    gs = refs[:n]
    n2, dgate, dup, hid = (refs[n + 2 * i : n + 2 * i + 2] for i in range(4))
    out, g_far, g_near = refs[-3:]
    for to, ks in ((g_far, list(sz.far)), (g_near, list(sz.near))):
        for ref, (k, first, count) in zip(gs, layout):
            if k in ks:
                at = ks.index(k) * ck + first * ck // 2
                to[at : at + count * ck // 2, :] = ref[...]
    for i, (left, right) in enumerate(((dgate, n2), (dup, n2), (hid, (g_far, g_near)))):
        grads = mm_tn(left[0][...], right[0][...]) + mm_tn(left[1][...], right[1][...])
        grads = grads.astype(bf16)
        for at in range(2 * sz.planes):
            out[at, i * ffc : (i + 1) * ffc, :] = grads[0:ffc, at * half : (at + 1) * half]


def middle_kernel(sz, place, *refs):
    n = sz.chips
    dn2_in = refs[:n]
    middle, g, wo, gains = refs[n : n + 4]
    outs, dh1_out, pay = refs[-n - 2 : -2], refs[-2], refs[-1]
    j = place[0]
    dn2 = dn2_in[0][...].astype(f32)
    for k in range(1, n):
        dn2 = dn2 + dn2_in[k][...].astype(f32)
    mid = middle[...]
    scale = rms(mid)
    normed = mid * scale
    weighted = dn2 * gains[1:2]
    dh1 = g[...].astype(f32) + scale * (
        weighted - normed * jnp.mean(weighted * normed, axis=-1, keepdims=True)
    )
    dh1_out[...] = dh1
    branch = dh1.astype(bf16)
    dmix = mm_nt(branch, wo[...]).astype(bf16)
    for q in range(n):
        pay[q, :, 0 : sz.cv] = dmix[:, q * sz.cv : (q + 1) * sz.cv]
        pay[q, :, sz.cv :] = branch[:, q * sz.co : (q + 1) * sz.co]
    for m in range(n):
        outs[m][...] = pay[j ^ m]


def back_kernel(sz, place, lengths, *refs):
    n, ck, cv = sz.chips, sz.chunk, sz.cv
    heads, total = sz.heads, sz.tokens
    pays = refs[:n]
    act, mixed, den_full, den_rows = refs[n : n + 4]
    outs = refs[n + 4 : 2 * n + 4]
    dact, branch_c, dnum_h, q_h, dden, dq_t, dk, dv = refs[2 * n + 4 :]
    j, c = place[0], place[1]
    lane_q = lax.broadcasted_iota(jnp.int32, (ck, 128), 1) // FEAT
    lane_v = lax.broadcasted_iota(jnp.int32, (ck, sz.vp), 1) // VDIM
    picks = (
        lax.broadcasted_iota(jnp.int32, (8, cv), 1) // VDIM
        == lax.broadcasted_iota(jnp.int32, (8, cv), 0)
    ).astype(f32)
    for k in range(n):
        rows = pl.ds(aligned(j ^ k, ck), ck)
        dmix = pays[k][:, 0:cv].astype(f32)
        branch_c[rows, :] = pays[k][:, cv:]
        dnum = dmix / den_full[rows, 0:cv]
        if sz.vp > cv:
            dnum = jnp.concatenate([dnum, jnp.zeros((ck, sz.vp - cv), f32)], axis=1)
        products = dmix * mixed[rows, :].astype(f32)
        sums = lax.dot_general(
            picks,
            products,
            (((1,), (1,)), ((), ())),
            precision=lax.Precision.HIGHEST,
            preferred_element_type=f32,
        )
        dden[j ^ k] = -sums / den_rows[j ^ k]
        query = act[rows, 0:128].astype(f32) * 0.25
        for h in range(heads):
            dnum_h[h, rows, :] = jnp.where(lane_v == h, dnum, 0.0).astype(bf16)
            q_h[h, rows, :] = jnp.where(lane_q == h, query, 0.0).astype(bf16)
    starts = doc_starts(lengths, c)
    dq_t[...] = jnp.zeros_like(dq_t)
    for b in range(total // ck):
        low = b * ck
        width = total - low
        u_rows = slice(low, low + ck)
        u_at = low + lax.broadcasted_iota(jnp.int32, (ck, 1), 0)
        t_row = low + lax.broadcasted_iota(jnp.int32, (1, width), 1)
        first = latest_start(t_row, starts)
        t_at = low + lax.broadcasted_iota(jnp.int32, (ck, width), 1)
        allowed = (u_at <= t_at) & (u_at >= first)
        keys = act[u_rows, 128:256]
        values = act[u_rows, 256:]
        keys_t = keys.astype(f32).T
        dv_here = jnp.zeros((ck, sz.vp), f32)
        dk_here = jnp.zeros((ck, 128), f32)
        for h in range(heads):
            qs = q_h[h, low:, :]
            ds_in = dnum_h[h, low:, :]
            extra = jnp.concatenate(
                [dden[i][h : h + 1] for i in range(b, total // ck)], axis=1
            )
            s = mm_nt(keys, qs)
            dtaylor = mm_nt(values, ds_in) + extra
            slope = 1.0 + s
            taylor = jnp.where(allowed, slope + 0.5 * s * s, 0.0).astype(bf16)
            dscore = jnp.where(allowed, dtaylor * slope, 0.0).astype(bf16)
            dv_here = dv_here + mm(taylor, ds_in)
            dk_here = dk_here + mm(dscore, qs)
            k_t = keys_t[h * FEAT : (h + 1) * FEAT].astype(bf16)
            dq_t[h * FEAT : (h + 1) * FEAT, low:] += mm(k_t, dscore)
        dk[u_rows, :] = dk_here.astype(bf16)
        dv[u_rows, :] = dv_here.astype(bf16)
    dact[:, 0:128] = (dq_t[...] * 0.25).T.astype(bf16)
    dact[:, 128:256] = dk[...]
    dact[:, 256:] = dv[...]
    for k in range(n):
        rows = pl.ds(aligned(j ^ k, ck), ck)
        outs[k][:, 0 : sz.cq] = dact[rows, 0 : sz.cq]
        outs[k][:, sz.cq : 2 * sz.cq] = dact[rows, 128 : 128 + sz.cq]
        outs[k][:, 2 * sz.cq :] = dact[rows, 256 : 256 + cv]


def back_grads_kernel(sz, layout, place, *refs):
    n, ck, cq, cv, co = sz.chips, sz.chunk, sz.cq, sz.cv, sz.co
    half, cols = sz.half, sz.cols
    i = len(layout)
    mixed = refs[:i]
    entry, dact, branch_c, norm2, norm2_more, gains, w = refs[i : i + 7]
    keep, sends = refs[-3 - sz.planes], refs[-2 - sz.planes : -2]
    dact_s, out = refs[-2:]
    j, c = place[0], place[1]
    for k in range(n):
        rows = slice(k * ck, (k + 1) * ck)
        dact_s[rows, :] = dact[pl.ds(aligned(j ^ k, ck), ck), :]
    grads = mm_tn(dact_s[...], entry[...])
    norm1 = jnp.sum(grads * w[...].astype(f32).T, axis=0, keepdims=True)
    grads = grads.astype(bf16)
    norms = jnp.concatenate(
        [norm1 / gains[0:1], norm2[...] + norm2_more[...], jnp.zeros((14, sz.model), f32)], axis=0
    ).astype(bf16)
    for at in range(2 * sz.planes):
        lanes = slice(at * half, (at + 1) * half)
        out[at, 0:cq, :] = grads[0:cq, lanes]
        out[at, cq : 2 * cq, :] = grads[128 : 128 + cq, lanes]
        out[at, 2 * cq : 2 * cq + cv, :] = grads[256 : 256 + cv, lanes]
        out[at, cols:, :] = norms[:, lanes]
    for ref, (m, first, count) in zip(mixed, layout):
        grads = mm_tn(branch_c[...], ref[...]).astype(bf16)
        at = (j ^ m) * (cv // half) + first * cv // (2 * half)
        for i in range(count * cv // (2 * half)):
            out[at + i, 2 * cq + cv : cols, :] = grads[:, i * half : (i + 1) * half]
    for z in range(sz.planes):
        keep[z] = out[2 * z + c]
        sends[z][...] = out[2 * z + 1 - c]


def pair_sum_kernel(sz, place, keep, *refs):
    received, outs, sums = refs[: sz.planes], refs[sz.planes : -1], refs[-1]
    plane = place[2]
    for z in range(sz.planes):
        sums[z] = (keep[z].astype(f32) + received[z][...].astype(f32)).astype(bf16)
    for k in range(sz.planes):
        outs[k][...] = sums[plane ^ k]


def plane_sum_kernel(sz, *refs):
    total = refs[0][...].astype(f32)
    for ref in refs[1 : sz.planes]:
        total = total + ref[...].astype(f32)
    refs[-1][...] = total.astype(bf16)


def split_rows(sz, place, values, keep, send):
    for core in range(2):

        @pl.when(place[1] == core)
        def _():
            for to, side in ((keep, core), (send, 1 - core)):
                to[...] = values[side * sz.block : (side + 1) * sz.block]


def join_kernel(sz, place, *refs):
    for i in range(2):
        keep, received = refs[2 * i : 2 * i + 2]
        out = refs[-2 + i]
        out[place[1]] = keep[...]
        out[1 - place[1]] = received[...]


def finish_block_kernel(sz, place, *refs):
    result = refs[0][...]
    for part in refs[1 : sz.chips + 1]:
        result = result + part[...].astype(f32)
    keep, send = refs[-2], refs[-1]
    split_rows(sz, place, result.astype(bf16), keep, send)


def finish_tokens_kernel(sz, place, *refs):
    n = sz.chips
    dact_in = refs[:n]
    w_qkv, dh1, x, gains, keep, send = refs[n:]
    values = x[...].astype(f32)
    scale = rms(values)
    normed = values * scale
    dn1 = mm_nt(dact_in[0][...], w_qkv[0])
    for k in range(1, n):
        dn1 = dn1 + mm_nt(dact_in[k][...], w_qkv[k])
    weighted = dn1 * gains[0:1]
    result = dh1[...] + scale * (
        weighted - normed * jnp.mean(weighted * normed, axis=-1, keepdims=True)
    )
    split_rows(sz, place, result, keep, send)


def gathered(sz, layout, place, refs, to):
    n = len(layout)
    j, c = place[0], place[1]
    rows = to.shape[2]
    for some, side in ((refs[:n], c), (refs[n : 2 * n], 1 - c)):
        for ref, (k, first, count) in zip(some, layout):
            at, size = first * rows // 2, count * rows // 2
            to[j ^ k, side, at : at + size] = ref[...]


def finish_attention_kernel(sz, layout, place, *refs):
    n, shard, cq, cv, co = sz.chips, sz.shard, sz.cq, sz.cv, sz.co
    query, key, value, output, norms, all_c = refs[2 * len(layout) :]
    gathered(sz, layout, place, refs, all_c)
    total = jnp.zeros((16, shard), f32)
    for q in range(n):
        part = jnp.concatenate([all_c[q, 0], all_c[q, 1]], axis=1).astype(f32)
        query[:, q * cq : (q + 1) * cq] = part[0:cq].T
        key[:, q * cq : (q + 1) * cq] = part[cq : 2 * cq].T
        value[:, q * cv : (q + 1) * cv] = part[2 * cq : 2 * cq + cv].T
        output[:, q * co : (q + 1) * co] = part[2 * cq + cv : sz.cols].T
        total = total + part[sz.cols :]
    norms[...] = total[0:8]


def finish_mlp_kernel(sz, layout, place, *refs):
    half, ffc = sz.half, sz.ffc
    *outs, all_c = refs[2 * len(layout) :]
    gathered(sz, layout, place, refs, all_c)
    for q in range(sz.chips):
        at = q * ffc
        count = max(0, min(ffc, sz.hidden - at))
        for i, out in enumerate(outs):
            for side in range(2):
                if count:
                    out[at : at + count, side * half : (side + 1) * half] = all_c[
                        q, side, i * ffc : i * ffc + count, :
                    ].astype(f32)


def kernel(body, name, outs, scratch=(), smem=0, room=60, in_specs=None, out_specs=None, **more):
    shapes = [jax.ShapeDtypeStruct(shape, dtype) for shape, dtype in outs]
    scratch = [VMEM(shape, dtype) for shape, dtype in scratch] + list(more.pop("semaphores", ()))

    def run(*args, after=(), carry=()):
        n_in, n_out = len(args), len(shapes)
        loose = len(after) + len(carry)

        def trimmed(*refs):
            first = n_in + loose
            body(*refs[:n_in], *refs[first : first + n_out], *refs[first + n_out + len(carry) :])

        takes = in_specs or [scalars()] * smem + [whole()] * (n_in - smem)
        gives = out_specs or [whole()] * n_out
        return pl.pallas_call(
            trimmed,
            name=name,
            out_shape=shapes + [jax.ShapeDtypeStruct(a.shape, a.dtype) for a in carry],
            in_specs=takes + [anywhere()] * loose,
            out_specs=gives + [anywhere()] * len(carry),
            scratch_shapes=scratch,
            input_output_aliases={n_in + len(after) + i: n_out + i for i in range(len(carry))},
            compiler_params=pltpu.CompilerParams(vmem_limit_bytes=room * MIB),
            cost_estimate=pl.CostEstimate(
                flops=int(COST[name] * 1.15e9), bytes_accessed=0, transcendentals=0
            ),
            **more,
        )(*args, *after, *carry)

    return run


def shards(
    n_chip,
    n_dp,
    tokens,
    cotangent,
    doc_lengths,
    norm1_gain,
    w_query,
    w_key,
    w_value,
    w_output,
    norm2_gain,
    w_gate,
    w_up,
    w_down,
):
    rows_here, block, model = tokens.shape
    hidden = w_gate.shape[1]
    sz = Sizes(n_dp, n_chip, block, w_query.shape[0], model, hidden)
    n, ck, cq, cv, co, ffc = sz.chips, sz.chunk, sz.cq, sz.cv, sz.co, sz.ffc
    half, shard, total = sz.half, sz.shard, sz.tokens
    tight = lambda mib: mib if n == 4 else 60
    chip, core = lax.axis_index("chip"), lax.axis_index("core")
    place = jnp.stack([chip, core, lax.axis_index("dp")]).astype(jnp.int32)

    def swap(a):
        return lax.ppermute(a, "core", [(0, 1), (1, 0)])

    def to_chip(a, k):
        return lax.ppermute(a, "chip", [(i, i ^ k) for i in range(n)])

    def to_plane(a, k):
        return lax.ppermute(a, "dp", [(i, i ^ k) for i in range(n_dp)])

    def spread(a, name, axis=0):
        if n != 4 or not TWICE[name]:
            return [a] + [to_chip(a, k) for k in range(1, n)], sz.direct
        first, second = to_chip(a, 1), to_chip(a, 2)
        middle = a.shape[axis] // 2
        low = to_chip(lax.slice_in_dim(second, 0, middle, axis=axis), 1)
        high = to_chip(lax.slice_in_dim(first, middle, 2 * middle, axis=axis), 2)
        return [a, first, second, low, high], sz.pieces

    def exchange(parts):
        return [parts[0]] + [to_chip(parts[k], k) for k in range(1, n)]

    def to_rows(a):
        return lax.all_to_all(a, "core", 0, 0).reshape(ck, model)

    def when(name, *arrays):
        return list(arrays) if TIES[name] else []

    with jax.named_scope("gather_tokens"):
        xs, lay_x = spread(to_rows(tokens), "x")

    with jax.named_scope("pack_small"):
        (small,) = kernel(
            partial(pack_small_kernel, sz), "pack_small", [((half + 16, sz.wa), bf16)], smem=1
        )(
            place,
            w_query,
            w_key,
            w_value,
            w_output,
            norm1_gain,
            norm2_gain,
            after=when("small_x", xs[0]),
        )
        small_own = [small] + [to_plane(small, k) for k in range(1, n_dp)]
        small_oth = [swap(a) for a in small_own]

    with jax.named_scope("pack_large"):
        loads = anywhere() if half % 128 == 0 else whole()
        (large,) = kernel(
            partial(pack_large_kernel, sz),
            "pack_large",
            [((3 * ffc, half), bf16)],
            in_specs=[scalars()] + [loads] * 3,
            semaphores=[pltpu.SemaphoreType.DMA((3,))],
        )(place, w_gate.T, w_up.T, w_down)
        g_here = to_rows(cotangent)
        (large,) = kernel(lambda *refs: None, "after_small", [])(
            after=small_own[1:]
            + when("large_x", *xs[1:3])
            + when("large_x3", *xs[3:])
            + when("large_g", g_here),
            carry=[large],
        )
        large_all = lax.all_gather(large, ("dp", "core"))

    with jax.named_scope("gather_cotangent"):
        if TIES["g_take"]:
            (g_here,) = kernel(lambda *refs: None, "g_take", [])(after=small_own[1:] + xs[1:3], carry=[g_here])
        gs, lay_g = spread(g_here, "g")

    with jax.named_scope("project"):
        act, w_act, entry_one, gains = kernel(
            partial(project_kernel, sz, lay_x),
            "project",
            [
                ((total, sz.qw), bf16),
                ((model, sz.qw), bf16),
                ((total, model), bf16),
                ((2, model), f32),
            ],
            [((n_dp, 2, shard), f32)],
            smem=1,
        )(place, *xs, *small_own, *small_oth, after=when("project_g", *gs[1:3]))

    with jax.named_scope("take"):
        wo_half, qkv_half = kernel(
            partial(take_output_kernel, sz),
            "take_output",
            [((n_dp, half, co), bf16), ((n_dp, half, sz.qkv), bf16)],
        )(*small_own, after=when("take_oth", *small_oth) + when("take_x", *xs[1:]))
        wo_parts, lay_wo = spread(wo_half, "wo")

    with jax.named_scope("attention"):
        mixed_own, den_full, den_rows = kernel(
            partial(attend_kernel, sz),
            "attend",
            [
                ((total, cv), bf16),
                ((total, sz.vp), f32),
                ((total // ck, 8, ck), f32),
            ],
            smem=2,
            room=tight(20),
        )(place, doc_lengths, act, after=when("attend_wo", wo_parts[1])
            + when("attend_g", *gs[1:3])
            + when("attend_g1", gs[1]),
        )
        mixed, lay_o = spread(mixed_own, "o", 1)

    with jax.named_scope("output_weight"):
        wo_own, *carried = kernel(
            partial(output_weight_kernel, sz, lay_wo),
            "output_weight",
            [((n_dp, half, model), bf16)],
            [((n, n_dp, half, co), bf16)],
            smem=1,
            room=tight(20),
        )(
            place,
            *wo_parts,
            after=when("ow_mixed", *mixed[1:3])
            + when("ow_own", mixed_own)
            + when("ow_g", *gs[1:3]),
            carry=when("qkv_ow", qkv_half),
        )
        qkv_half = carried[0] if carried else qkv_half
        wo_oth = swap(wo_own)

    with jax.named_scope("before_mlp"):
        if TIES["qkv_tie"]:
            (qkv_half,) = kernel(lambda *refs: None, "before_mlp", [])(
                after=[*mixed[1:], *gs[1:], wo_oth], carry=[qkv_half]
            )

    with jax.named_scope("mlp"):
        group = 2 if n == 4 else 1
        size = group * ck
        part = total // 2

        def mlp(ks, name, after):
            some_x, some_g = picked(lay_x, ks), picked(lay_g, ks)
            count, loads = len(ks), len(some_x) + len(some_g) + len(mixed) + 3
            results = kernel(
                partial(mlp_kernel, sz, ks, group, (lay_x, lay_g, lay_o)),
                name,
                [((ck, model), bf16)] * count
                + [
                    ((part, model), bf16),
                    ((part, sz.ffp), bf16),
                    ((part, sz.ffp), bf16),
                    ((part, sz.ffp), bf16),
                    ((1, model), f32),
                    ((model, model), bf16),
                    ((ck, model), f32),
                ],
                [
                    ((size, model), bf16),
                    ((size, model), bf16),
                    ((n, size, cv), bf16),
                    ((model, model), bf16),
                    ((sz.ffp, model), bf16),
                    ((sz.ffp, model), bf16),
                    ((sz.ffp, model), bf16),
                    ((size, model), bf16),
                    ((size, sz.ffp), bf16),
                    ((size, sz.ffp), bf16),
                    ((size, sz.ffp), bf16),
                    ((size, model), bf16),
                    ((ck, model), f32),
                ]
                + stages(sz, 3),
                semaphores=[
                    pltpu.SemaphoreType.DMA((6,)),
                    pltpu.SemaphoreType.DMA((6 + group,)),
                ],
                in_specs=[scalars()] + [anywhere()] * loads + [whole()],
                out_specs=[anywhere()] * (count + 4) + [whole()] + [anywhere()] * 2,
                grid=(count // group,),
            )(
                place,
                *[xs[i] for i in some_x],
                *[gs[i] for i in some_g],
                *mixed,
                wo_own,
                wo_oth,
                large_all,
                gains,
                after=after,
            )
            return dict(zip(ks, results[:count])), results[count:]

        far_parts, far = mlp(sz.far, "mlp_far", when("qkv_tie", qkv_half))
        far_in = {k: to_chip(a, k) for k, a in far_parts.items()}
        near_parts, near = mlp(sz.near, "mlp_near", when("near_far", far[4]))
        near_in = {k: to_chip(a, k) for k, a in near_parts.items() if k}
        dn2_in = [near_parts[0]] + [{**far_in, **near_in}[k] for k in range(1, n)]
        wo, middle = near[5], near[6]

    with jax.named_scope("gather_qkv"):
        qkv_own, lay_q = spread(qkv_half, "qkv")

    with jax.named_scope("mlp_grads"):
        mlp_grads, *carried = kernel(
            partial(mlp_grads_kernel, sz, lay_g),
            "mlp_grads",
            [((2 * n_dp, 3 * ffc, half), bf16)],
            [((part, model), bf16)] * 2,
        )(
            *gs,
            *[a for pair in zip(far[:4], near[:4]) for a in pair],
            after=when("grads_far", *far_in.values()),
            carry=when("grads_qkv", *qkv_own),
        )
        qkv_own = carried or qkv_own
        qkv_oth = [swap(a) for a in qkv_own]
        mlp_shard = lax.psum_scatter(mlp_grads, ("dp", "core"), scatter_dimension=0)

    with jax.named_scope("middle"):
        results = kernel(
            partial(middle_kernel, sz),
            "middle",
            [((ck, cv + co), bf16)] * n + [((ck, model), f32)],
            [((n, ck, cv + co), bf16)],
            smem=1,
        )(
            place,
            *dn2_in,
            middle,
            gs[0],
            wo,
            gains,
            after=when("middle_grads", mlp_grads) + when("middle_qkv", *qkv_own[1:]),
        )
        dh1 = results[n]
        pays = exchange(results[:n])

    with jax.named_scope("gather_qkv"):
        (w_qkv,) = kernel(
            partial(gather_qkv_kernel, sz, lay_q),
            "gather_qkv",
            [((n, model, sz.qkv), bf16)],
            smem=1,
            room=tight(20),
        )(place, *qkv_own, *qkv_oth, after=when("gq_middle", dh1))

    with jax.named_scope("down"):
        down_parts = kernel(
            partial(down_kernel, sz),
            "down",
            [((ck, model), bf16)] * n,
            [((sz.ffp, model), bf16)] + stages(sz, 1),
            room=tight(20),
            in_specs=[whole()] * 2 + [anywhere()],
            semaphores=[pltpu.SemaphoreType.DMA],
        )(far[3], near[3], large_all, after=when("down_middle", dh1) + when("down_gq", w_qkv))
        down_in = exchange(down_parts)

    with jax.named_scope("attention_back"):
        results = kernel(
            partial(back_kernel, sz),
            "attention_back",
            [((ck, sz.qkv), bf16)] * n + [((total, sz.qw), bf16), ((total, co), bf16)],
            [
                ((sz.heads, total, sz.vp), bf16),
                ((sz.heads, total, 128), bf16),
                ((total // ck, 8, ck), f32),
                ((128, total), f32),
                ((total, 128), bf16),
                ((total, sz.vp), bf16),
            ],
            smem=2,
            room=tight(44),
        )(
            place,
            doc_lengths,
            *pays,
            act,
            mixed_own,
            den_full,
            den_rows,
            after=when("back_down", down_parts[0]) + when("back_gq", w_qkv),
        )
        dact, branch_c = results[n], results[n + 1]
        dact_in = exchange(results[:n])

    with jax.named_scope("attention_grads"):
        width = sz.cols + 16
        keep, *sends = kernel(
            partial(back_grads_kernel, sz, lay_o),
            "attention_grads",
            [((n_dp, width, half), bf16)] + [((width, half), bf16)] * n_dp,
            [((total, sz.qw), bf16), ((2 * n_dp, width, half), bf16)],
            smem=1,
            room=tight(28),
        )(
            place,
            *mixed,
            entry_one,
            dact,
            branch_c,
            far[4],
            near[4],
            gains,
            w_act,
            after=when("ag_down", *down_in[1:3]),
        )

    with jax.named_scope("finish_block"):
        block_keep, block_send = kernel(
            partial(finish_block_kernel, sz), "finish_block", [((block, model), bf16)] * 2, smem=1
        )(place, middle, *down_in)
        block_other = swap(block_send)

    with jax.named_scope("finish_tokens"):
        grad_keep, grad_send = kernel(
            partial(finish_tokens_kernel, sz), "finish_tokens", [((block, model), f32)] * 2, smem=1
        )(place, *dact_in, w_qkv, dh1, xs[0], gains)
        grad_other = swap(grad_send)

    with jax.named_scope("sum_gradients"):
        *parts, mlp_shard = kernel(
            partial(pair_sum_kernel, sz),
            "pair_sum",
            [((width, half), bf16)] * n_dp,
            [((n_dp, width, half), bf16)],
            smem=1,
            room=tight(20),
        )(
            place,
            keep,
            *[swap(a) for a in sends],
            after=when("pair_tokens", grad_keep) + when("pair_block", block_keep),
            carry=[mlp_shard],
        )
        sums = [parts[0]] + [to_plane(parts[k], k) for k in range(1, n_dp)]

    with jax.named_scope("spread_gradients"):
        att_shard, *carried = kernel(
            partial(plane_sum_kernel, sz), "plane_sum", [((width, half), bf16)], room=tight(20)
        )(
            *sums,
            after=when("plane_tokens", grad_keep) + when("plane_block", block_keep),
            carry=when("mlp_plane", mlp_shard),
        )
        mlp_shard = carried[0] if carried else mlp_shard
        mlp_own, lay_m = spread(mlp_shard, "mlp")
        mlp_oth = [swap(a) for a in mlp_own]
        att_own, lay_a = spread(att_shard, "att")
        att_oth = [swap(a) for a in att_own]

    with jax.named_scope("join"):
        block_out, grad_tokens = kernel(
            partial(join_kernel, sz),
            "join",
            [((2, block, model), bf16), ((2, block, model), f32)],
            smem=1,
        )(place, block_keep, block_other, grad_keep, grad_other)

    with jax.named_scope("finish_attention"):
        total_query, total_key, total_value, total_output, norms = kernel(
            partial(finish_attention_kernel, sz, lay_a),
            "finish_attention",
            [
                ((shard, n * cq), f32),
                ((shard, n * cq), f32),
                ((shard, n * cv), f32),
                ((shard, n * co), f32),
                ((8, shard), f32),
            ],
            [((n, 2, width, half), bf16)],
            smem=1,
            room=tight(20),
        )(place, *att_own, *att_oth, after=when("fa_tokens", grad_keep))

    with jax.named_scope("finish_mlp"):
        total_gate, total_up, total_down = kernel(
            partial(finish_mlp_kernel, sz, lay_m),
            "finish_mlp",
            [((hidden, shard), f32)] * 3,
            [((n, 2, 3 * ffc, half), bf16)],
            smem=1,
            room=tight(24),
        )(place, *mlp_own, *mlp_oth, after=when("fm_norms", norms) + when("fm_join", block_out))

    return (
        block_out,
        grad_tokens,
        norms[0],
        total_query,
        total_key,
        total_value,
        total_output,
        norms[1],
        total_gate.T,
        total_up.T,
        total_down,
    )


def solution(mesh):
    n_dp, n_seq = mesh.shape["dp"], mesh.shape["seq"]
    n_chip = n_seq // 2
    grid = Mesh(mesh.devices.reshape(n_dp, n_chip, 2), ("dp", "chip", "core"))
    seq = ("chip", "core")
    placed = (
        P("dp", seq, None),
        P("dp", seq, None),
        P("dp", None),
        P("dp"),
        P("dp", None),
        P("dp", None),
        P("dp", None),
        P("dp", None),
        P("dp"),
        P("dp", None),
        P("dp", None),
        P(None, "dp"),
    )
    return jax.shard_map(
        partial(shards, n_chip, n_dp),
        mesh=grid,
        in_specs=placed,
        out_specs=(
            P("dp", seq, None),
            P("dp", seq, None),
            P("dp"),
            P("dp", None),
            P("dp", None),
            P("dp", None),
            P("dp", None),
            P("dp"),
            P("dp", None),
            P("dp", None),
            P(None, "dp"),
        ),
        check_vma=False,
    )
```

```python
import math
from functools import partial

import jax
import jax.numpy as jnp
from jax import lax
from jax.experimental import pallas as pl
from jax.experimental.pallas import tpu as pltpu
from jax.sharding import Mesh
from jax.sharding import PartitionSpec as P

HEADS = 16
FEAT = 16
VDIM = 64
EPSILON = 1e-05

bf16 = jnp.bfloat16
f32 = jnp.float32
VMEM = pltpu.VMEM
SMEM = pltpu.SMEM
MIB = 1024 * 1024

COST = dict(
    g_take=0.1,
    pack_small=0.5,
    pack_large=100.0,
    after_small=0.5,
    project=100.0,
    take_output=7.0,
    attend=4.0,
    output_weight=0.5,
    before_mlp=0.1,
    mlp_far=100.0,
    mlp_near=35.0,
    mlp_grads=2.0,
    middle=30.0,
    gather_qkv=1.0,
    down=0.1,
    attention_back=60.0,
    attention_grads=0.1,
    pair_sum=35.0,
    finish_block=0.5,
    finish_tokens=0.5,
    plane_sum=2.0,
    join=2.0,
    finish_attention=0.1,
    finish_mlp=35.0,
)
TWICE = dict(
    x=0,
    g=1,
    wo=1,
    o=1,
    qkv=0,
    att=0,
    mlp=1,
)
TIES = dict(
    small_x=0,
    large_x=1,
    large_x3=0,
    large_g=0,
    project_g=0,
    attend_g=0,
    attend_g1=0,
    g_take=1,
    take_oth=0,
    take_x=0,
    attend_wo=0,
    ow_mixed=1,
    ow_own=0,
    ow_g=1,
    qkv_ow=0,
    qkv_tie=1,
    near_far=0,
    grads_qkv=1,
    grads_far=0,
    middle_grads=1,
    middle_qkv=0,
    gq_middle=1,
    down_middle=1,
    down_gq=0,
    back_down=1,
    back_gq=1,
    ag_down=1,
    pair_tokens=1,
    pair_block=0,
    plane_tokens=0,
    plane_block=0,
    mlp_plane=0,
    fa_tokens=1,
    fm_norms=0,
    fm_join=0,
)


def mm(left, right):
    return jnp.dot(left, right, preferred_element_type=f32)


def mm_nt(left, right):
    return lax.dot_general(left, right, (((1,), (1,)), ((), ())), preferred_element_type=f32)


def mm_tn(left, right):
    return lax.dot_general(left, right, (((0,), (0,)), ((), ())), preferred_element_type=f32)


def up_to(value, step):
    return -(-value // step) * step


def whole():
    return pl.BlockSpec(memory_space=VMEM, pipeline_mode=pl.Buffered(1))


def anywhere():
    return pl.BlockSpec(memory_space=pl.ANY)


def scalars():
    return pl.BlockSpec(memory_space=SMEM)


def rms(values):
    return lax.rsqrt(jnp.mean(values * values, axis=-1, keepdims=True) + EPSILON)


def shard_row(pieces, row):
    return jnp.concatenate([pieces[z] for z in range(pieces.shape[0])], axis=1)[row : row + 1]


def doc_starts(lengths, row):
    starts, total = [], jnp.int32(0)
    for i in range(lengths.shape[1]):
        starts.append(total)
        total = total + lengths[row, i]
    return starts


def latest_start(position, starts):
    latest = jnp.zeros_like(position)
    for start in starts:
        latest = jnp.where(position >= start, start, latest)
    return latest


class Sizes:
    def __init__(self, planes, chips, block, shard, model, hidden):
        self.planes, self.chips, self.block = planes, chips, block
        self.chunk = 2 * block
        self.tokens = chips * self.chunk
        self.shard, self.half, self.model = shard, shard // 2, model
        self.heads = HEADS // chips
        self.cq = self.heads * FEAT
        self.cv = self.heads * VDIM
        self.co = model // chips
        self.vp = up_to(self.cv, 128)
        self.qw = 256 + self.vp
        self.wa = max(512, 2 * self.cq + self.cv + self.co)
        self.hidden = hidden
        self.ffc = up_to(-(-hidden // chips), 16)
        self.ffp = up_to(self.ffc, 128)
        self.cols = 2 * self.cq + self.cv + self.co
        self.qkv = 2 * self.cq + self.cv
        self.pieces = self.direct = [(k, 0, 2) for k in range(chips)]
        self.far, self.near = range(chips - 1, chips // 2 - 1, -1), range(chips // 2 - 1, -1, -1)
        if chips == 4:
            self.pieces = [(0, 0, 2), (1, 0, 2), (2, 0, 2), (3, 0, 1), (3, 1, 1)]


def aligned(index, step):
    return pl.multiple_of(index * step, step)


def pack_large_kernel(sz, place, *refs):
    weights, out, sem = refs[:3], refs[-2], refs[-1]
    half, ffc = sz.half, sz.ffc
    j, c = place[0], place[1]
    for chip in range(sz.chips):
        first = chip * ffc
        count = max(0, min(ffc, sz.hidden - first))
        for core in range(2):

            @pl.when((j == chip) & (c == core))
            def _():
                lanes = slice(core * half, (core + 1) * half)
                copies = []
                for i, weight in enumerate(weights):
                    if count == 0:
                        continue
                    if half % 128:
                        out[i * ffc : i * ffc + count, :] = weight[first : first + count, lanes]
                        continue
                    copies.append(
                        pltpu.make_async_copy(
                            weight.at[pl.ds(first, count), pl.ds(core * half, half)],
                            out.at[pl.ds(i * ffc, count)],
                            sem.at[i],
                        )
                    )
                for copy in copies:
                    copy.start()
                for i in range(3):
                    if count < ffc:
                        out[i * ffc + count : (i + 1) * ffc, :] = jnp.zeros(
                            (ffc - count, half), bf16
                        )
                for copy in copies:
                    copy.wait()


def pack_small_kernel(sz, place, w_query, w_key, w_value, w_output, gain_one, gain_two, out):
    half, cq, cv, co = sz.half, sz.cq, sz.cv, sz.co
    j, c = place[0], place[1]
    side = pl.ds(aligned(c, half), half)
    out[...] = jnp.zeros_like(out)
    for chip in range(sz.chips):

        @pl.when(j == chip)
        def _():
            out[0:half, 0:cq] = w_query[side, chip * cq : (chip + 1) * cq]
            out[0:half, cq : 2 * cq] = w_key[side, chip * cq : (chip + 1) * cq]
            out[0:half, 2 * cq : 2 * cq + cv] = w_value[side, chip * cv : (chip + 1) * cv]
            out[0:half, 2 * cq + cv : sz.cols] = w_output[side, chip * co : (chip + 1) * co]

    for i, gain in enumerate((gain_one, gain_two)):
        row = gain[...].reshape(1, sz.shard)
        out[half : half + 16, i * 256 : i * 256 + sz.shard] = jnp.broadcast_to(row, (16, sz.shard))


def project_kernel(sz, layout, place, *refs):
    n, p = len(layout), sz.planes
    xs, own, oth = refs[:n], refs[n : n + p], refs[n + p : n + 2 * p]
    act, w, entry, gains, gain_c = refs[n + 2 * p :]
    j, c, plane = place[0], place[1], place[2]
    half, shard, cq, cv, ck = sz.half, sz.shard, sz.cq, sz.cv, sz.chunk
    w[...] = jnp.zeros_like(w)
    for k in range(p):
        z = plane ^ k
        for piece, side in ((own[k], c), (oth[k], 1 - c)):
            rows = pl.ds(pl.multiple_of(z * shard + side * half, half), half)
            w[rows, 0:cq] = piece[0:half, 0:cq]
            w[rows, 128 : 128 + cq] = piece[0:half, cq : 2 * cq]
            w[rows, 256 : 256 + cv] = piece[0:half, 2 * cq : 2 * cq + cv]
        for i in range(2):
            row = own[k][half : half + 16, i * 256 : i * 256 + shard]
            gain_c[z, i : i + 1] = row[0:1].astype(f32)
    for i in range(2):
        gains[i : i + 1] = shard_row(gain_c, i)
    gain = gains[0:1]
    for ref, (k, first, count) in zip(xs, layout):
        x = ref[...].astype(f32)
        at = k * ck + first * ck // 2
        entry[at : at + count * ck // 2, :] = ((x * rms(x)) * gain).astype(bf16)
    for k in range(sz.chips):
        rows = pl.ds(aligned(j ^ k, ck), ck)
        act[rows, :] = mm(entry[k * ck : (k + 1) * ck, :], w[...]).astype(bf16)


def attend_kernel(sz, place, lengths, act, mixed, den_full, den_rows):
    c, ck, cv = place[1], sz.chunk, sz.cv
    starts = doc_starts(lengths, c)
    lane_q = lax.broadcasted_iota(jnp.int32, (ck, 128), 1) // FEAT
    lane_v = lax.broadcasted_iota(jnp.int32, (ck, sz.vp), 1) // VDIM
    lane = lax.broadcasted_iota(jnp.int32, (ck, 128), 1)
    for b in range(sz.tokens // ck):
        rows = slice(b * ck, (b + 1) * ck)
        width = (b + 1) * ck
        t_at = b * ck + lax.broadcasted_iota(jnp.int32, (ck, 1), 0)
        first = latest_start(t_at, starts)
        u_at = lax.broadcasted_iota(jnp.int32, (ck, width), 1)
        allowed = (u_at <= t_at) & (u_at >= first)
        query = act[rows, 0:128]
        keys = act[0:width, 128:256]
        values = act[0:width, 256:]
        att = jnp.zeros((ck, sz.vp), f32)
        den_wide = jnp.ones((ck, sz.vp), f32)
        den_some = jnp.ones((ck, 128), f32)
        for h in range(sz.heads):
            mine = jnp.where(lane_q == h, query.astype(f32) * 0.25, 0.0).astype(bf16)
            s = mm_nt(mine, keys)
            taylor = jnp.where(allowed, 1.0 + s + 0.5 * s * s, 0.0).astype(bf16)
            den = jnp.sum(taylor.astype(f32), axis=1, keepdims=True)
            num = mm(taylor, values)
            att = jnp.where(lane_v == h, num / den, att)
            den_wide = jnp.where(lane_v == h, den, den_wide)
            den_some = jnp.where(lane == h, den, den_some)
        mixed[rows, :] = att.astype(bf16)[:, 0:cv]
        den_full[rows, :] = den_wide
        den_rows[b] = den_some.T[0:8]


def take_output_kernel(sz, *refs):
    for k in range(sz.planes):
        refs[-2][k] = refs[k][0 : sz.half, sz.qkv : sz.cols]
        refs[-1][k] = refs[k][0 : sz.half, 0 : sz.qkv]


def gather_qkv_kernel(sz, layout, place, *refs):
    n, half, planes = len(layout), sz.half, sz.planes
    out = refs[-1]
    c, plane = place[1], place[2]
    for pieces, side in ((refs[:n], c), (refs[n : 2 * n], 1 - c)):
        for ref, (k, first, count) in zip(pieces, layout):
            for i in range(count * planes // 2):
                z = plane ^ (first * planes // 2 + i)
                at = pl.multiple_of(z * sz.shard + side * half, half)
                out[k, pl.ds(at, half), :] = ref[i]


def output_weight_kernel(sz, layout, place, *refs):
    planes = sz.planes
    *pieces, out, out_c = refs
    j, plane = place[0], place[2]
    for ref, (k, first, count) in zip(pieces, layout):
        out_c[j ^ k, first * planes // 2 : (first + count) * planes // 2] = ref[...]
    for z in range(planes):
        out[plane ^ z] = jnp.concatenate([out_c[q, z] for q in range(sz.chips)], axis=1)


def fetch_weight(sz, large, which, to, stage, sem):
    half, ffc = sz.half, sz.ffc
    rows = pl.ds(which * ffc, ffc)
    if half % 128:
        return [pltpu.make_async_copy(large.at[:, rows], stage, sem)]
    return [
        pltpu.make_async_copy(
            large.at[at, rows], to.at[pl.ds(0, ffc), pl.ds(at * half, half)], sem
        )
        for at in range(2 * sz.planes)
    ]


def settle_weight(sz, to, stage):
    ffc, half = sz.ffc, sz.half
    if half % 128:
        for at in range(2 * sz.planes):
            to[0:ffc, at * half : (at + 1) * half] = stage[at]
    if sz.ffp > ffc:
        to[ffc:, :] = jnp.zeros((sz.ffp - ffc, sz.model), bf16)


def stages(sz, count):
    if sz.half % 128:
        return [((2 * sz.planes, sz.ffc, sz.half), bf16)] * count
    return [((8, 128), bf16)] * count


def picked(layout, ks):
    return [i for i, (k, _, _) in enumerate(layout) if k in ks]


def mlp_kernel(sz, ks, group, layouts, place, *refs):
    n, ck, cv, half, shard, ffc = sz.chips, sz.chunk, sz.cv, sz.half, sz.shard, sz.ffc
    lay_x, lay_g, lay_o = layouts
    some_x, some_g = picked(lay_x, ks), picked(lay_g, ks)
    i, total = len(some_x), len(some_x) + len(some_g)
    xs, gs, mixed = refs[:i], refs[i:total], refs[total : total + len(lay_o)]
    total = total + len(lay_o)
    wo_own, wo_oth, large, gains = refs[total : total + 4]
    outs = refs[total + 4 :]
    dn2_out = outs[: len(ks)]
    n2_out, dgate_out, dup_out, hid_out, norm_out, wo_out, mid_out = outs[len(ks) : len(ks) + 7]
    scratch = outs[len(ks) + 7 :]
    x_s, g_s, o_c, wo, wg, wu, wd, n2_s, dgate_s, dup_s, hid_s, dn2_s, mid_s = scratch[:13]
    stage, sem, out_sem = scratch[13:16], scratch[16], scratch[17]
    j, c = place[0], place[1]
    step = pl.program_id(0)
    size = group * ck
    steps = len(ks) // group

    def inputs(at, which):
        here = list(ks)[at * group : (at + 1) * group]
        found = []
        to = g_s if which else x_s
        layout, some = (lay_g, some_g) if which else (lay_x, some_x)
        for source, index in zip(gs if which else xs, some):
            k, low, count = layout[index]
            if k in here:
                rows = pl.ds(here.index(k) * ck + low * ck // 2, count * ck // 2)
                found.append(pltpu.make_async_copy(source, to.at[rows], sem.at[which]))
        if which:
            return found
        for slot, k in enumerate(here):
            rows = pl.ds(slot * ck, ck)
            for ref, (m, low, count) in zip(mixed, lay_o):
                lanes = pl.ds(low * cv // 2, count * cv // 2)
                source = ref.at[pl.ds(aligned(j ^ k, ck), ck)]
                found.append(pltpu.make_async_copy(source, o_c.at[j ^ m, rows, lanes], sem.at[0]))
        return found

    wo_copies = []
    for z in range(sz.planes):
        for piece, side in ((wo_own, c), (wo_oth, 1 - c)):
            rows = pl.ds(pl.multiple_of(z * shard + side * half, half), half)
            wo_copies.append(pltpu.make_async_copy(piece.at[z], wo.at[rows], sem.at[2]))
    weight_copies = [
        fetch_weight(sz, large, i, to, stage[i], sem.at[3 + i])
        for i, to in enumerate((wg, wu, wd))
    ]

    def fresh(act):
        if steps == 1:
            act()
        else:
            pl.when(step == 0)(act)

    for at in range(steps):

        @pl.when(step == at)
        def _():
            for copy in inputs(at, 0):
                copy.start()

    @fresh
    def _():
        norm_out[...] = jnp.zeros_like(norm_out)
        for copy in wo_copies + weight_copies[0] + weight_copies[1]:
            copy.start()

    for at in range(steps):

        @pl.when(step == at)
        def _():
            for copy in inputs(at, 1):
                copy.start()

    @fresh
    def _():
        for copy in weight_copies[2]:
            copy.start()

    for at in range(steps):

        @pl.when(step == at)
        def _():
            for copy in inputs(at, 0):
                copy.wait()

    @fresh
    def _():
        for copy in wo_copies:
            copy.wait()

    mix = jnp.concatenate([o_c[q] for q in range(n)], axis=1)
    middle = x_s[...].astype(f32) + mm(mix, wo[...])
    normed = middle * rms(middle)
    entry = (normed * gains[1:2]).astype(bf16)
    n2_s[...] = entry
    mid_s[...] = middle[size - ck :]

    @fresh
    def _():
        for which in range(2):
            for copy in weight_copies[which]:
                copy.wait()
            settle_weight(sz, (wg, wu)[which], stage[which])

    gate = mm_nt(entry, wg[...])
    upward = mm_nt(entry, wu[...])

    for at in range(steps):

        @pl.when(step == at)
        def _():
            for copy in inputs(at, 1):
                copy.wait()

    @fresh
    def _():
        for copy in weight_copies[2]:
            copy.wait()
        settle_weight(sz, wd, stage[2])

    grad_hidden = mm_nt(g_s[...], wd[...])
    sig = jax.nn.sigmoid(gate)
    silu = gate * sig
    dgate = (grad_hidden * upward * (sig * (1.0 + gate * (1.0 - sig)))).astype(bf16)
    dup = (grad_hidden * silu).astype(bf16)
    dgate_s[...] = dgate
    dup_s[...] = dup
    hid_s[...] = (silu * upward).astype(bf16)
    rows = pl.ds(aligned(step, size), size)
    saves = [
        pltpu.make_async_copy(source, to.at[rows], out_sem.at[index])
        for index, (source, to) in enumerate(
            ((n2_s, n2_out), (dgate_s, dgate_out), (dup_s, dup_out), (hid_s, hid_out))
        )
    ]
    saves.append(pltpu.make_async_copy(mid_s, mid_out, out_sem.at[4]))
    saves.append(pltpu.make_async_copy(wo, wo_out, out_sem.at[5]))
    for copy in saves:
        copy.start()
    dn2 = mm(dgate, wg[...]) + mm(dup, wu[...])
    dn2_s[...] = dn2.astype(bf16)
    for at in range(steps):

        @pl.when(step == at)
        def _():
            parts = [
                pltpu.make_async_copy(
                    dn2_s.at[pl.ds(slot * ck, ck)],
                    dn2_out[at * group + slot],
                    out_sem.at[6 + slot],
                )
                for slot in range(group)
            ]
            for copy in parts:
                copy.start()
            norm_out[...] += jnp.sum(dn2 * normed, axis=0, keepdims=True)
            for copy in parts:
                copy.wait()

    for copy in saves:
        copy.wait()


def down_kernel(sz, *refs):
    hids, large = refs[:2], refs[2]
    n, ck = sz.chips, sz.chunk
    outs = refs[-n - 3 : -3]
    wd, stage, sem = refs[-3:]
    copies = fetch_weight(sz, large, 2, wd, stage, sem)
    for copy in copies:
        copy.start()
    for copy in copies:
        copy.wait()
    settle_weight(sz, wd, stage)
    for hid, ks in zip(hids, (sz.far, sz.near)):
        for slot, k in enumerate(ks):
            outs[k][...] = mm(hid[slot * ck : (slot + 1) * ck, :], wd[...]).astype(bf16)


def mlp_grads_kernel(sz, layout, *refs):
    n, ck, ffc, half = len(layout), sz.chunk, sz.ffc, sz.half
    gs = refs[:n]
    n2, dgate, dup, hid = (refs[n + 2 * i : n + 2 * i + 2] for i in range(4))
    out, g_far, g_near = refs[-3:]
    for to, ks in ((g_far, list(sz.far)), (g_near, list(sz.near))):
        for ref, (k, first, count) in zip(gs, layout):
            if k in ks:
                at = ks.index(k) * ck + first * ck // 2
                to[at : at + count * ck // 2, :] = ref[...]
    for i, (left, right) in enumerate(((dgate, n2), (dup, n2), (hid, (g_far, g_near)))):
        grads = mm_tn(left[0][...], right[0][...]) + mm_tn(left[1][...], right[1][...])
        grads = grads.astype(bf16)
        for at in range(2 * sz.planes):
            out[at, i * ffc : (i + 1) * ffc, :] = grads[0:ffc, at * half : (at + 1) * half]


def middle_kernel(sz, place, *refs):
    n = sz.chips
    dn2_in = refs[:n]
    middle, g, wo, gains = refs[n : n + 4]
    outs, dh1_out, pay = refs[-n - 2 : -2], refs[-2], refs[-1]
    j = place[0]
    dn2 = dn2_in[0][...].astype(f32)
    for k in range(1, n):
        dn2 = dn2 + dn2_in[k][...].astype(f32)
    mid = middle[...]
    scale = rms(mid)
    normed = mid * scale
    weighted = dn2 * gains[1:2]
    dh1 = g[...].astype(f32) + scale * (
        weighted - normed * jnp.mean(weighted * normed, axis=-1, keepdims=True)
    )
    dh1_out[...] = dh1
    branch = dh1.astype(bf16)
    dmix = mm_nt(branch, wo[...]).astype(bf16)
    for q in range(n):
        pay[q, :, 0 : sz.cv] = dmix[:, q * sz.cv : (q + 1) * sz.cv]
        pay[q, :, sz.cv :] = branch[:, q * sz.co : (q + 1) * sz.co]
    for m in range(n):
        outs[m][...] = pay[j ^ m]


def back_kernel(sz, place, lengths, *refs):
    n, ck, cv = sz.chips, sz.chunk, sz.cv
    heads, total = sz.heads, sz.tokens
    pays = refs[:n]
    act, mixed, den_full, den_rows = refs[n : n + 4]
    outs = refs[n + 4 : 2 * n + 4]
    dact, branch_c, dnum_h, q_h, dden, dq_t, dk, dv = refs[2 * n + 4 :]
    j, c = place[0], place[1]
    lane_q = lax.broadcasted_iota(jnp.int32, (ck, 128), 1) // FEAT
    lane_v = lax.broadcasted_iota(jnp.int32, (ck, sz.vp), 1) // VDIM
    picks = (
        lax.broadcasted_iota(jnp.int32, (8, cv), 1) // VDIM
        == lax.broadcasted_iota(jnp.int32, (8, cv), 0)
    ).astype(f32)
    for k in range(n):
        rows = pl.ds(aligned(j ^ k, ck), ck)
        dmix = pays[k][:, 0:cv].astype(f32)
        branch_c[rows, :] = pays[k][:, cv:]
        dnum = dmix / den_full[rows, 0:cv]
        if sz.vp > cv:
            dnum = jnp.concatenate([dnum, jnp.zeros((ck, sz.vp - cv), f32)], axis=1)
        products = dmix * mixed[rows, :].astype(f32)
        sums = lax.dot_general(
            picks,
            products,
            (((1,), (1,)), ((), ())),
            precision=lax.Precision.HIGHEST,
            preferred_element_type=f32,
        )
        dden[j ^ k] = -sums / den_rows[j ^ k]
        query = act[rows, 0:128].astype(f32) * 0.25
        for h in range(heads):
            dnum_h[h, rows, :] = jnp.where(lane_v == h, dnum, 0.0).astype(bf16)
            q_h[h, rows, :] = jnp.where(lane_q == h, query, 0.0).astype(bf16)
    starts = doc_starts(lengths, c)
    dq_t[...] = jnp.zeros_like(dq_t)
    for b in range(total // ck):
        low = b * ck
        width = total - low
        u_rows = slice(low, low + ck)
        u_at = low + lax.broadcasted_iota(jnp.int32, (ck, 1), 0)
        t_row = low + lax.broadcasted_iota(jnp.int32, (1, width), 1)
        first = latest_start(t_row, starts)
        t_at = low + lax.broadcasted_iota(jnp.int32, (ck, width), 1)
        allowed = (u_at <= t_at) & (u_at >= first)
        keys = act[u_rows, 128:256]
        values = act[u_rows, 256:]
        keys_t = keys.astype(f32).T
        dv_here = jnp.zeros((ck, sz.vp), f32)
        dk_here = jnp.zeros((ck, 128), f32)
        for h in range(heads):
            qs = q_h[h, low:, :]
            ds_in = dnum_h[h, low:, :]
            extra = jnp.concatenate(
                [dden[i][h : h + 1] for i in range(b, total // ck)], axis=1
            )
            s = mm_nt(keys, qs)
            dtaylor = mm_nt(values, ds_in) + extra
            slope = 1.0 + s
            taylor = jnp.where(allowed, slope + 0.5 * s * s, 0.0).astype(bf16)
            dscore = jnp.where(allowed, dtaylor * slope, 0.0).astype(bf16)
            dv_here = dv_here + mm(taylor, ds_in)
            dk_here = dk_here + mm(dscore, qs)
            k_t = keys_t[h * FEAT : (h + 1) * FEAT].astype(bf16)
            dq_t[h * FEAT : (h + 1) * FEAT, low:] += mm(k_t, dscore)
        dk[u_rows, :] = dk_here.astype(bf16)
        dv[u_rows, :] = dv_here.astype(bf16)
    dact[:, 0:128] = (dq_t[...] * 0.25).T.astype(bf16)
    dact[:, 128:256] = dk[...]
    dact[:, 256:] = dv[...]
    for k in range(n):
        rows = pl.ds(aligned(j ^ k, ck), ck)
        outs[k][:, 0 : sz.cq] = dact[rows, 0 : sz.cq]
        outs[k][:, sz.cq : 2 * sz.cq] = dact[rows, 128 : 128 + sz.cq]
        outs[k][:, 2 * sz.cq :] = dact[rows, 256 : 256 + cv]


def back_grads_kernel(sz, layout, place, *refs):
    n, ck, cq, cv, co = sz.chips, sz.chunk, sz.cq, sz.cv, sz.co
    half, cols = sz.half, sz.cols
    i = len(layout)
    mixed = refs[:i]
    entry, dact, branch_c, norm2, norm2_more, gains, w = refs[i : i + 7]
    keep, sends = refs[-3 - sz.planes], refs[-2 - sz.planes : -2]
    dact_s, out = refs[-2:]
    j, c = place[0], place[1]
    for k in range(n):
        rows = slice(k * ck, (k + 1) * ck)
        dact_s[rows, :] = dact[pl.ds(aligned(j ^ k, ck), ck), :]
    grads = mm_tn(dact_s[...], entry[...])
    norm1 = jnp.sum(grads * w[...].astype(f32).T, axis=0, keepdims=True)
    grads = grads.astype(bf16)
    norms = jnp.concatenate(
        [norm1 / gains[0:1], norm2[...] + norm2_more[...], jnp.zeros((14, sz.model), f32)], axis=0
    ).astype(bf16)
    for at in range(2 * sz.planes):
        lanes = slice(at * half, (at + 1) * half)
        out[at, 0:cq, :] = grads[0:cq, lanes]
        out[at, cq : 2 * cq, :] = grads[128 : 128 + cq, lanes]
        out[at, 2 * cq : 2 * cq + cv, :] = grads[256 : 256 + cv, lanes]
        out[at, cols:, :] = norms[:, lanes]
    for ref, (m, first, count) in zip(mixed, layout):
        grads = mm_tn(branch_c[...], ref[...]).astype(bf16)
        at = (j ^ m) * (cv // half) + first * cv // (2 * half)
        for i in range(count * cv // (2 * half)):
            out[at + i, 2 * cq + cv : cols, :] = grads[:, i * half : (i + 1) * half]
    for z in range(sz.planes):
        keep[z] = out[2 * z + c]
        sends[z][...] = out[2 * z + 1 - c]


def pair_sum_kernel(sz, place, keep, *refs):
    received, outs, sums = refs[: sz.planes], refs[sz.planes : -1], refs[-1]
    plane = place[2]
    for z in range(sz.planes):
        sums[z] = (keep[z].astype(f32) + received[z][...].astype(f32)).astype(bf16)
    for k in range(sz.planes):
        outs[k][...] = sums[plane ^ k]


def plane_sum_kernel(sz, *refs):
    total = refs[0][...].astype(f32)
    for ref in refs[1 : sz.planes]:
        total = total + ref[...].astype(f32)
    refs[-1][...] = total.astype(bf16)


def split_rows(sz, place, values, keep, send):
    for core in range(2):

        @pl.when(place[1] == core)
        def _():
            for to, side in ((keep, core), (send, 1 - core)):
                to[...] = values[side * sz.block : (side + 1) * sz.block]


def join_kernel(sz, place, *refs):
    for i in range(2):
        keep, received = refs[2 * i : 2 * i + 2]
        out = refs[-2 + i]
        out[place[1]] = keep[...]
        out[1 - place[1]] = received[...]


def finish_block_kernel(sz, place, *refs):
    result = refs[0][...]
    for part in refs[1 : sz.chips + 1]:
        result = result + part[...].astype(f32)
    keep, send = refs[-2], refs[-1]
    split_rows(sz, place, result.astype(bf16), keep, send)


def finish_tokens_kernel(sz, place, *refs):
    n = sz.chips
    dact_in = refs[:n]
    w_qkv, dh1, x, gains, keep, send = refs[n:]
    values = x[...].astype(f32)
    scale = rms(values)
    normed = values * scale
    dn1 = mm_nt(dact_in[0][...], w_qkv[0])
    for k in range(1, n):
        dn1 = dn1 + mm_nt(dact_in[k][...], w_qkv[k])
    weighted = dn1 * gains[0:1]
    result = dh1[...] + scale * (
        weighted - normed * jnp.mean(weighted * normed, axis=-1, keepdims=True)
    )
    split_rows(sz, place, result, keep, send)


def gathered(sz, layout, place, refs, to):
    n = len(layout)
    j, c = place[0], place[1]
    rows = to.shape[2]
    for some, side in ((refs[:n], c), (refs[n : 2 * n], 1 - c)):
        for ref, (k, first, count) in zip(some, layout):
            at, size = first * rows // 2, count * rows // 2
            to[j ^ k, side, at : at + size] = ref[...]


def finish_attention_kernel(sz, layout, place, *refs):
    n, shard, cq, cv, co = sz.chips, sz.shard, sz.cq, sz.cv, sz.co
    query, key, value, output, norms, all_c = refs[2 * len(layout) :]
    gathered(sz, layout, place, refs, all_c)
    total = jnp.zeros((16, shard), f32)
    for q in range(n):
        part = jnp.concatenate([all_c[q, 0], all_c[q, 1]], axis=1).astype(f32)
        query[:, q * cq : (q + 1) * cq] = part[0:cq].T
        key[:, q * cq : (q + 1) * cq] = part[cq : 2 * cq].T
        value[:, q * cv : (q + 1) * cv] = part[2 * cq : 2 * cq + cv].T
        output[:, q * co : (q + 1) * co] = part[2 * cq + cv : sz.cols].T
        total = total + part[sz.cols :]
    norms[...] = total[0:8]


def finish_mlp_kernel(sz, some, place, *refs):
    half, ffc, n = sz.half, sz.ffc, sz.chips
    m = len(some)
    outs, (pay, stage, sem) = refs[2 * m : 2 * m + 3], refs[2 * m + 3 :]
    j, c = place[0], place[1]
    partners = sorted({k for k, _, _ in some})
    for slot, k in enumerate(partners):
        for at, (piece, first, count) in enumerate(some):
            if piece == k:
                rows = slice(first * 3 * ffc // 2, (first + count) * 3 * ffc // 2)
                pay[c, rows] = refs[at][...]
                pay[1 - c, rows] = refs[m + at][...]
        for i in range(3):
            for side in range(2):
                stage[slot, i, :, side * half : (side + 1) * half] = pay[
                    side, i * ffc : (i + 1) * ffc, :
                ].astype(f32)

        def copies(q):
            count = max(0, min(ffc, sz.hidden - q * ffc))
            if not count:
                return []
            return [
                pltpu.make_async_copy(
                    stage.at[slot, i, pl.ds(0, count)],
                    outs[i].at[pl.ds(q * ffc, count)],
                    sem.at[slot, i],
                )
                for i in range(3)
            ]

        for q in range(n):

            @pl.when((j ^ k) == q)
            def _():
                for copy in copies(q):
                    copy.start()

    for slot, k in enumerate(partners):

        def copies(q):
            count = max(0, min(ffc, sz.hidden - q * ffc))
            if not count:
                return []
            return [
                pltpu.make_async_copy(
                    stage.at[slot, i, pl.ds(0, count)],
                    outs[i].at[pl.ds(q * ffc, count)],
                    sem.at[slot, i],
                )
                for i in range(3)
            ]

        for q in range(n):

            @pl.when((j ^ k) == q)
            def _():
                for copy in copies(q):
                    copy.wait()


def kernel(body, name, outs, scratch=(), smem=0, room=60, in_specs=None, out_specs=None, **more):
    shapes = [jax.ShapeDtypeStruct(shape, dtype) for shape, dtype in outs]
    scratch = [VMEM(shape, dtype) for shape, dtype in scratch] + list(more.pop("semaphores", ()))

    def run(*args, after=(), carry=()):
        n_in, n_out = len(args), len(shapes)
        loose = len(after) + len(carry)

        def trimmed(*refs):
            first = n_in + loose
            body(*refs[:n_in], *refs[first : first + n_out], *refs[first + n_out + len(carry) :])

        takes = in_specs or [scalars()] * smem + [whole()] * (n_in - smem)
        gives = out_specs or [whole()] * n_out
        return pl.pallas_call(
            trimmed,
            name=name,
            out_shape=shapes + [jax.ShapeDtypeStruct(a.shape, a.dtype) for a in carry],
            in_specs=takes + [anywhere()] * loose,
            out_specs=gives + [anywhere()] * len(carry),
            scratch_shapes=scratch,
            input_output_aliases={n_in + len(after) + i: n_out + i for i in range(len(carry))},
            compiler_params=pltpu.CompilerParams(vmem_limit_bytes=room * MIB),
            cost_estimate=pl.CostEstimate(
                flops=int(COST[name] * 1.15e9), bytes_accessed=0, transcendentals=0
            ),
            **more,
        )(*args, *after, *carry)

    return run


def shards(
    n_chip,
    n_dp,
    tokens,
    cotangent,
    doc_lengths,
    norm1_gain,
    w_query,
    w_key,
    w_value,
    w_output,
    norm2_gain,
    w_gate,
    w_up,
    w_down,
):
    rows_here, block, model = tokens.shape
    hidden = w_gate.shape[1]
    sz = Sizes(n_dp, n_chip, block, w_query.shape[0], model, hidden)
    n, ck, cq, cv, co, ffc = sz.chips, sz.chunk, sz.cq, sz.cv, sz.co, sz.ffc
    half, shard, total = sz.half, sz.shard, sz.tokens
    tight = lambda mib: mib if n == 4 else 60
    chip, core = lax.axis_index("chip"), lax.axis_index("core")
    place = jnp.stack([chip, core, lax.axis_index("dp")]).astype(jnp.int32)

    def swap(a):
        return lax.ppermute(a, "core", [(0, 1), (1, 0)])

    def to_chip(a, k):
        return lax.ppermute(a, "chip", [(i, i ^ k) for i in range(n)])

    def to_plane(a, k):
        return lax.ppermute(a, "dp", [(i, i ^ k) for i in range(n_dp)])

    def spread(a, name, axis=0):
        if n != 4 or not TWICE[name]:
            return [a] + [to_chip(a, k) for k in range(1, n)], sz.direct
        first, second = to_chip(a, 1), to_chip(a, 2)
        middle = a.shape[axis] // 2
        low = to_chip(lax.slice_in_dim(second, 0, middle, axis=axis), 1)
        high = to_chip(lax.slice_in_dim(first, middle, 2 * middle, axis=axis), 2)
        return [a, first, second, low, high], sz.pieces

    def exchange(parts):
        return [parts[0]] + [to_chip(parts[k], k) for k in range(1, n)]

    def to_rows(a):
        return lax.all_to_all(a, "core", 0, 0).reshape(ck, model)

    def when(name, *arrays):
        return list(arrays) if TIES[name] else []

    with jax.named_scope("gather_tokens"):
        xs, lay_x = spread(to_rows(tokens), "x")

    with jax.named_scope("pack_small"):
        (small,) = kernel(
            partial(pack_small_kernel, sz), "pack_small", [((half + 16, sz.wa), bf16)], smem=1
        )(
            place,
            w_query,
            w_key,
            w_value,
            w_output,
            norm1_gain,
            norm2_gain,
            after=when("small_x", xs[0]),
        )
        small_own = [small] + [to_plane(small, k) for k in range(1, n_dp)]
        small_oth = [swap(a) for a in small_own]

    with jax.named_scope("pack_large"):
        loads = anywhere() if half % 128 == 0 else whole()
        (large,) = kernel(
            partial(pack_large_kernel, sz),
            "pack_large",
            [((3 * ffc, half), bf16)],
            in_specs=[scalars()] + [loads] * 3,
            semaphores=[pltpu.SemaphoreType.DMA((3,))],
        )(place, w_gate.T, w_up.T, w_down)
        g_here = to_rows(cotangent)
        (large,) = kernel(lambda *refs: None, "after_small", [])(
            after=small_own[1:]
            + when("large_x", *xs[1:3])
            + when("large_x3", *xs[3:])
            + when("large_g", g_here),
            carry=[large],
        )
        large_all = lax.all_gather(large, ("dp", "core"))

    with jax.named_scope("gather_cotangent"):
        if TIES["g_take"]:
            (g_here,) = kernel(lambda *refs: None, "g_take", [])(after=small_own[1:] + xs[1:3], carry=[g_here])
        gs, lay_g = spread(g_here, "g")

    with jax.named_scope("project"):
        act, w_act, entry_one, gains = kernel(
            partial(project_kernel, sz, lay_x),
            "project",
            [
                ((total, sz.qw), bf16),
                ((model, sz.qw), bf16),
                ((total, model), bf16),
                ((2, model), f32),
            ],
            [((n_dp, 2, shard), f32)],
            smem=1,
        )(place, *xs, *small_own, *small_oth, after=when("project_g", *gs[1:3]))

    with jax.named_scope("take"):
        wo_half, qkv_half = kernel(
            partial(take_output_kernel, sz),
            "take_output",
            [((n_dp, half, co), bf16), ((n_dp, half, sz.qkv), bf16)],
        )(*small_own, after=when("take_oth", *small_oth) + when("take_x", *xs[1:]))
        wo_parts, lay_wo = spread(wo_half, "wo")

    with jax.named_scope("attention"):
        mixed_own, den_full, den_rows = kernel(
            partial(attend_kernel, sz),
            "attend",
            [
                ((total, cv), bf16),
                ((total, sz.vp), f32),
                ((total // ck, 8, ck), f32),
            ],
            smem=2,
            room=tight(20),
        )(place, doc_lengths, act, after=when("attend_wo", wo_parts[1])
            + when("attend_g", *gs[1:3])
            + when("attend_g1", gs[1]),
        )
        mixed, lay_o = spread(mixed_own, "o", 1)

    with jax.named_scope("output_weight"):
        wo_own, *carried = kernel(
            partial(output_weight_kernel, sz, lay_wo),
            "output_weight",
            [((n_dp, half, model), bf16)],
            [((n, n_dp, half, co), bf16)],
            smem=1,
            room=tight(20),
        )(
            place,
            *wo_parts,
            after=when("ow_mixed", *mixed[1:3])
            + when("ow_own", mixed_own)
            + when("ow_g", *gs[1:3]),
            carry=when("qkv_ow", qkv_half),
        )
        qkv_half = carried[0] if carried else qkv_half
        wo_oth = swap(wo_own)

    with jax.named_scope("before_mlp"):
        if TIES["qkv_tie"]:
            (qkv_half,) = kernel(lambda *refs: None, "before_mlp", [])(
                after=[*mixed[1:], *gs[1:], wo_oth], carry=[qkv_half]
            )

    with jax.named_scope("mlp"):
        group = 2 if n == 4 else 1
        size = group * ck
        part = total // 2

        def mlp(ks, name, after):
            some_x, some_g = picked(lay_x, ks), picked(lay_g, ks)
            count, loads = len(ks), len(some_x) + len(some_g) + len(mixed) + 3
            results = kernel(
                partial(mlp_kernel, sz, ks, group, (lay_x, lay_g, lay_o)),
                name,
                [((ck, model), bf16)] * count
                + [
                    ((part, model), bf16),
                    ((part, sz.ffp), bf16),
                    ((part, sz.ffp), bf16),
                    ((part, sz.ffp), bf16),
                    ((1, model), f32),
                    ((model, model), bf16),
                    ((ck, model), f32),
                ],
                [
                    ((size, model), bf16),
                    ((size, model), bf16),
                    ((n, size, cv), bf16),
                    ((model, model), bf16),
                    ((sz.ffp, model), bf16),
                    ((sz.ffp, model), bf16),
                    ((sz.ffp, model), bf16),
                    ((size, model), bf16),
                    ((size, sz.ffp), bf16),
                    ((size, sz.ffp), bf16),
                    ((size, sz.ffp), bf16),
                    ((size, model), bf16),
                    ((ck, model), f32),
                ]
                + stages(sz, 3),
                semaphores=[
                    pltpu.SemaphoreType.DMA((6,)),
                    pltpu.SemaphoreType.DMA((6 + group,)),
                ],
                in_specs=[scalars()] + [anywhere()] * loads + [whole()],
                out_specs=[anywhere()] * (count + 4) + [whole()] + [anywhere()] * 2,
                grid=(count // group,),
            )(
                place,
                *[xs[i] for i in some_x],
                *[gs[i] for i in some_g],
                *mixed,
                wo_own,
                wo_oth,
                large_all,
                gains,
                after=after,
            )
            return dict(zip(ks, results[:count])), results[count:]

        far_parts, far = mlp(sz.far, "mlp_far", when("qkv_tie", qkv_half))
        far_in = {k: to_chip(a, k) for k, a in far_parts.items()}
        near_parts, near = mlp(sz.near, "mlp_near", when("near_far", far[4]))
        near_in = {k: to_chip(a, k) for k, a in near_parts.items() if k}
        dn2_in = [near_parts[0]] + [{**far_in, **near_in}[k] for k in range(1, n)]
        wo, middle = near[5], near[6]

    with jax.named_scope("gather_qkv"):
        qkv_own, lay_q = spread(qkv_half, "qkv")

    with jax.named_scope("mlp_grads"):
        mlp_grads, *carried = kernel(
            partial(mlp_grads_kernel, sz, lay_g),
            "mlp_grads",
            [((2 * n_dp, 3 * ffc, half), bf16)],
            [((part, model), bf16)] * 2,
        )(
            *gs,
            *[a for pair in zip(far[:4], near[:4]) for a in pair],
            after=when("grads_far", *far_in.values()),
            carry=when("grads_qkv", *qkv_own),
        )
        qkv_own = carried or qkv_own
        qkv_oth = [swap(a) for a in qkv_own]
        mlp_shard = lax.psum_scatter(mlp_grads, ("dp", "core"), scatter_dimension=0)

    with jax.named_scope("middle"):
        results = kernel(
            partial(middle_kernel, sz),
            "middle",
            [((ck, cv + co), bf16)] * n + [((ck, model), f32)],
            [((n, ck, cv + co), bf16)],
            smem=1,
        )(
            place,
            *dn2_in,
            middle,
            gs[0],
            wo,
            gains,
            after=when("middle_grads", mlp_grads) + when("middle_qkv", *qkv_own[1:]),
        )
        dh1 = results[n]
        pays = exchange(results[:n])

    with jax.named_scope("gather_qkv"):
        (w_qkv,) = kernel(
            partial(gather_qkv_kernel, sz, lay_q),
            "gather_qkv",
            [((n, model, sz.qkv), bf16)],
            smem=1,
            room=tight(20),
        )(place, *qkv_own, *qkv_oth, after=when("gq_middle", dh1))

    with jax.named_scope("down"):
        down_parts = kernel(
            partial(down_kernel, sz),
            "down",
            [((ck, model), bf16)] * n,
            [((sz.ffp, model), bf16)] + stages(sz, 1),
            room=tight(20),
            in_specs=[whole()] * 2 + [anywhere()],
            semaphores=[pltpu.SemaphoreType.DMA],
        )(far[3], near[3], large_all, after=when("down_middle", dh1) + when("down_gq", w_qkv))
        down_in = exchange(down_parts)

    with jax.named_scope("attention_back"):
        results = kernel(
            partial(back_kernel, sz),
            "attention_back",
            [((ck, sz.qkv), bf16)] * n + [((total, sz.qw), bf16), ((total, co), bf16)],
            [
                ((sz.heads, total, sz.vp), bf16),
                ((sz.heads, total, 128), bf16),
                ((total // ck, 8, ck), f32),
                ((128, total), f32),
                ((total, 128), bf16),
                ((total, sz.vp), bf16),
            ],
            smem=2,
            room=tight(44),
        )(
            place,
            doc_lengths,
            *pays,
            act,
            mixed_own,
            den_full,
            den_rows,
            after=when("back_down", down_parts[0]) + when("back_gq", w_qkv),
        )
        dact, branch_c = results[n], results[n + 1]
        dact_in = exchange(results[:n])

    with jax.named_scope("attention_grads"):
        width = sz.cols + 16
        keep, *sends = kernel(
            partial(back_grads_kernel, sz, lay_o),
            "attention_grads",
            [((n_dp, width, half), bf16)] + [((width, half), bf16)] * n_dp,
            [((total, sz.qw), bf16), ((2 * n_dp, width, half), bf16)],
            smem=1,
            room=tight(28),
        )(
            place,
            *mixed,
            entry_one,
            dact,
            branch_c,
            far[4],
            near[4],
            gains,
            w_act,
            after=when("ag_down", *down_in[1:3]),
        )

    with jax.named_scope("finish_block"):
        block_keep, block_send = kernel(
            partial(finish_block_kernel, sz), "finish_block", [((block, model), bf16)] * 2, smem=1
        )(place, middle, *down_in)
        block_other = swap(block_send)

    with jax.named_scope("finish_tokens"):
        grad_keep, grad_send = kernel(
            partial(finish_tokens_kernel, sz), "finish_tokens", [((block, model), f32)] * 2, smem=1
        )(place, *dact_in, w_qkv, dh1, xs[0], gains)
        grad_other = swap(grad_send)

    with jax.named_scope("sum_gradients"):
        *parts, mlp_shard = kernel(
            partial(pair_sum_kernel, sz),
            "pair_sum",
            [((width, half), bf16)] * n_dp,
            [((n_dp, width, half), bf16)],
            smem=1,
            room=tight(20),
        )(
            place,
            keep,
            *[swap(a) for a in sends],
            after=when("pair_tokens", grad_keep) + when("pair_block", block_keep),
            carry=[mlp_shard],
        )
        sums = [parts[0]] + [to_plane(parts[k], k) for k in range(1, n_dp)]

    with jax.named_scope("spread_gradients"):
        att_shard, *carried = kernel(
            partial(plane_sum_kernel, sz), "plane_sum", [((width, half), bf16)], room=tight(20)
        )(
            *sums,
            after=when("plane_tokens", grad_keep) + when("plane_block", block_keep),
            carry=when("mlp_plane", mlp_shard),
        )
        mlp_shard = carried[0] if carried else mlp_shard
        mlp_own, lay_m = spread(mlp_shard, "mlp")
        mlp_oth = [swap(a) for a in mlp_own]
        att_own, lay_a = spread(att_shard, "att")
        att_oth = [swap(a) for a in att_own]

    with jax.named_scope("join"):
        block_out, grad_tokens = kernel(
            partial(join_kernel, sz),
            "join",
            [((2, block, model), bf16), ((2, block, model), f32)],
            smem=1,
        )(place, block_keep, block_other, grad_keep, grad_other)

    with jax.named_scope("finish_attention"):
        total_query, total_key, total_value, total_output, norms = kernel(
            partial(finish_attention_kernel, sz, lay_a),
            "finish_attention",
            [
                ((shard, n * cq), f32),
                ((shard, n * cq), f32),
                ((shard, n * cv), f32),
                ((shard, n * co), f32),
                ((8, shard), f32),
            ],
            [((n, 2, width, half), bf16)],
            smem=1,
            room=tight(20),
        )(place, *att_own, *att_oth, after=when("fa_tokens", grad_keep))

    with jax.named_scope("finish_mlp"):
        total_gate, total_up, total_down = kernel(
            partial(finish_mlp_kernel, sz, lay_m),
            "finish_mlp",
            [((hidden, shard), f32)] * 3,
            [((2, 3 * ffc, half), bf16), ((n, 3, ffc, shard), f32)],
            smem=1,
            room=tight(24),
            out_specs=[anywhere()] * 3,
            semaphores=[pltpu.SemaphoreType.DMA((n, 3))],
        )(place, *mlp_own, *mlp_oth, after=when("fm_norms", norms) + when("fm_join", block_out))

    return (
        block_out,
        grad_tokens,
        norms[0],
        total_query,
        total_key,
        total_value,
        total_output,
        norms[1],
        total_gate.T,
        total_up.T,
        total_down,
    )


def solution(mesh):
    n_dp, n_seq = mesh.shape["dp"], mesh.shape["seq"]
    n_chip = n_seq // 2
    grid = Mesh(mesh.devices.reshape(n_dp, n_chip, 2), ("dp", "chip", "core"))
    seq = ("chip", "core")
    placed = (
        P("dp", seq, None),
        P("dp", seq, None),
        P("dp", None),
        P("dp"),
        P("dp", None),
        P("dp", None),
        P("dp", None),
        P("dp", None),
        P("dp"),
        P("dp", None),
        P("dp", None),
        P(None, "dp"),
    )
    return jax.shard_map(
        partial(shards, n_chip, n_dp),
        mesh=grid,
        in_specs=placed,
        out_specs=(
            P("dp", seq, None),
            P("dp", seq, None),
            P("dp"),
            P("dp", None),
            P("dp", None),
            P("dp", None),
            P("dp", None),
            P("dp"),
            P("dp", None),
            P("dp", None),
            P(None, "dp"),
        ),
        check_vma=False,
    )
```
